32 devices in a mesh: pair: 2 (over y), dp: 16 (over z, x, core).
Axes of the slice: x: 2, y: 2, z: 4, core: 2. Of those that a mesh axis runs over, the one named last changes fastest.
Arguments:
- tokens: bfloat16 [2, 16384, 768], P('pair', 'dp'), may hold values from -6 to 6
- attend_weight: bfloat16 [2, 768, 2304], P('pair'), may hold values from -0.21875 to 0.21875
- attend_bias: float32 [2, 1536], P('pair'), may hold values from -1.2 to 1.2
- merge_weight: bfloat16 [2, 768, 768], P('pair'), may hold values from -0.625 to 0.625
- merge_bias: float32 [2, 768], P('pair'), may hold values from -1.2 to 1.2
- first_gain: float32 [2, 768], P('pair'), may hold values from 0.5 to 1.5
- first_shift: float32 [2, 768], P('pair'), may hold values from -1.2 to 1.2
- expand_weight: bfloat16 [2, 768, 3072], P('pair'), may hold values from -0.21875 to 0.21875
- expand_bias: float32 [2, 3072], P('pair'), may hold values from -1.2 to 1.2
- reduce_weight: bfloat16 [2, 3072, 768], P('pair'), may hold values from -0.109375 to 0.109375
- reduce_bias: float32 [2, 768], P('pair'), may hold values from -1.2 to 1.2
- second_gain: float32 [2, 768], P('pair'), may hold values from 0.5 to 1.5
- second_shift: float32 [2, 768], P('pair'), may hold values from -1.2 to 1.2
- cotangent: bfloat16 [2, 16384, 768], P('pair', 'dp'), may hold values from -6 to 6
- positives: int32 [256, 4], replicated, may hold values from 0 to 63, as said below
- counts: int32 [256], replicated, may hold values from 1 to 4, as said below
Outputs:
- activations: bfloat16 [2, 16384, 768], P('pair', 'dp')
- contrastive_loss: float32 [], replicated
- input_grad: bfloat16 [2, 16384, 768], P('pair', 'dp')
- attend_weight_grad: float32 [2, 768, 2304], P('pair', 'dp')
- attend_bias_grad: float32 [2, 1536], P('pair', 'dp')
- merge_weight_grad: float32 [2, 768, 768], P('pair', 'dp')
- merge_bias_grad: float32 [2, 768], P('pair', 'dp')
- first_gain_grad: float32 [2, 768], P('pair', 'dp')
- first_shift_grad: float32 [2, 768], P('pair', 'dp')
- expand_weight_grad: float32 [2, 768, 3072], P('pair', 'dp')
- expand_bias_grad: float32 [2, 3072], P('pair', 'dp')
- reduce_weight_grad: float32 [2, 3072, 768], P('pair', 'dp')
- reduce_bias_grad: float32 [2, 768], P('pair', 'dp')
- second_gain_grad: float32 [2, 768], P('pair', 'dp')
- second_shift_grad: float32 [2, 768], P('pair', 'dp')
The draws below stay inside these ranges and needn't reach their ends.
Inputs may be any that keep to these rules, and one draw needn't show every extreme that they name: `positives`: entries 0 to counts[i] - 1 of row i are the positive passages of question i (passage j is the j-th sequence of tokens[1]); the 4 entries of a row are distinct passages; the other entries are padding. `counts`: some question has 4 positives.
All inputs are finite; a program needn't handle non-finite values.
Results may differ from the reference program's by a relative error of at most 0.012.
Values may be sent and summed in bfloat16 or wider, within the bound.
A program may use at most 192 MiB of HBM per device.

```python
import math
import jax
import jax.numpy as jnp
from jax import lax

D = 768
HEADS = 12
HEAD = 64
FF = 3072
QLEN = 64
PLEN = 256
KPOS = 4
TOK_DEV = 1024
ROWS = 16384
NQ = 256
NP = 64
N_DP = 16


def draw_positives(key, part):
    key = jax.random.fold_in(key, 11)
    base_key, step_key = jax.random.split(key)
    bases = jax.random.randint(base_key, (NQ, 1), 0, NP).astype(jnp.int32)
    steps = jax.random.randint(step_key, (NQ, KPOS), 1, NP // KPOS + 1).astype(jnp.int32)
    steps = steps.at[:, 0].set(0)
    offsets = jnp.cumsum(steps, axis=1).astype(jnp.int32)
    return ((bases + offsets) % NP).astype(jnp.int32)


def draw_counts(key, part):
    key = jax.random.fold_in(key, 23)
    value_key, row_key = jax.random.split(key)
    values = jax.random.randint(value_key, (NQ,), 1, KPOS + 1).astype(jnp.int32)
    full_row = jax.random.randint(row_key, (), 0, NQ).astype(jnp.int32)
    return jnp.where(jnp.arange(NQ, dtype=jnp.int32) == full_row, KPOS, values).astype(jnp.int32)


def strengthened(drawn, stream_key, source, target, shards_of, factor):
    owner, partner = [(jnp.arange(drawn.shape[position]) // (drawn.shape[position] // shards_of)).reshape([-1 if axis == position else 1 for axis in range(drawn.ndim)]) for position in (source, target)]
    chosen = jax.random.permutation(stream_key, shards_of)[partner]
    strong = (owner == chosen) | (owner == (partner + shards_of // 2) % shards_of)
    return jnp.where(strong, factor * drawn, drawn)


def steps_of(key, dims, pieces, low, top_value):
    level, own = 1.0, jax.random.fold_in(key, 6)
    for axis_at, blocks in pieces:
        steps = jnp.exp(jax.random.uniform(jax.random.fold_in(own, axis_at), (blocks,), jnp.float32, low / len(pieces), top_value / len(pieces)))
        level = level * jnp.repeat(steps, dims[axis_at] // blocks).reshape([-1 if axis == axis_at else 1 for axis in range(len(dims))])
    return level


def noise(stream_key, extent, scale, bound, cuts=(), held_as=jnp.bfloat16):
    result = jax.random.normal(stream_key, extent, jnp.float32) * scale
    if len(cuts) > 0:
        result = steps_of(stream_key, extent, cuts, -0.22, 0.18) * result
    return jnp.clip(result, min=-bound, max=bound).astype(held_as)


def bell_draw_with(key, shape, width, limit, cuts, heavy, kind=jnp.bfloat16):
    drawn = width * jax.random.normal(key, shape, jnp.float32)
    if cuts:
        drawn = drawn * steps_of(key, shape, cuts, -0.22, 0.18)
    return jnp.clip(strengthened(drawn, jax.random.fold_in(key, 3), *heavy), -limit, limit).astype(kind)


def setup_inputs(seed: int = 0) -> dict:
    seeds = jax.random.split(jax.random.key(seed), 17)
    tokens = noise(seeds[0], (2, ROWS, D), 1.0, 6.0, ((0, 2), (1, 16)))
    attend_weight = noise(seeds[1], (2, D, 3 * D), D ** -0.5, 0.21875, ((0, 2),))
    attend_bias = noise(seeds[2], (2, 2 * D), 0.2, 1.2, ((0, 2),), jnp.float32)
    merge_weight = noise(seeds[3], (2, D, D), (D // 8) ** -0.5, 0.625, ((0, 2),))
    merge_bias = noise(seeds[4], (2, D), 0.2, 1.2, ((0, 2),), jnp.float32)
    first_gain = jnp.clip(1.0 + 0.1 * jax.random.normal(seeds[5], (2, D), jnp.float32), 0.5, 1.5)
    first_shift = noise(seeds[6], (2, D), 0.2, 1.2, ((0, 2),), jnp.float32)
    expand_weight = noise(seeds[7], (2, D, FF), D ** -0.5, 0.21875, ((0, 2),))
    expand_bias = noise(seeds[8], (2, FF), 0.2, 1.2, ((0, 2),), jnp.float32)
    reduce_weight = noise(seeds[9], (2, FF, D), FF ** -0.5, 0.109375, ((0, 2),))
    reduce_bias = noise(seeds[10], (2, D), 0.2, 1.2, ((0, 2),), jnp.float32)
    second_gain = jnp.clip(1.0 + 0.1 * jax.random.normal(seeds[11], (2, D), jnp.float32), 0.5, 1.5)
    second_shift = noise(seeds[12], (2, D), 0.2, 1.2, ((0, 2),), jnp.float32)
    cotangent = bell_draw_with(seeds[13], (2, ROWS, D), 1.0, 6.0, ((0, 2), (1, 16)), (1, 2, 16, 2.0))
    positives = draw_positives(jax.random.fold_in(seeds[16], 71), 0)
    counts = draw_counts(jax.random.fold_in(seeds[16], 71), 0)
    return {"tokens": tokens, "attend_weight": attend_weight, "attend_bias": attend_bias, "merge_weight": merge_weight, "merge_bias": merge_bias, "first_gain": first_gain, "first_shift": first_shift, "expand_weight": expand_weight, "expand_bias": expand_bias, "reduce_weight": reduce_weight, "reduce_bias": reduce_bias, "second_gain": second_gain, "second_shift": second_shift, "cotangent": cotangent, "positives": positives, "counts": counts}


eps = 1e-06
loss_weight = 32.0
highest = lax.Precision.HIGHEST

@jax.custom_vjp
def low(v):
    return lax.optimization_barrier(v.astype(jnp.bfloat16)).astype(jnp.float32)

@jax.custom_vjp
def low_back(v):
    return v

def low_keep(v):
    return (low(v), None)

def low_pass(kept, grad):
    return (grad,)

def back_keep(v):
    return (v, None)

def back_low(kept, grad):
    return (low(grad),)
low.defvjp(low_keep, low_pass)
low_back.defvjp(back_keep, back_low)

def matmul(left_side, right_side):
    return jnp.dot(left_side, right_side, precision=highest)

def layer_norm(values, scale_gain, shift_row):
    centred = values - lax.optimization_barrier(jnp.mean(values, axis=-1, keepdims=True))
    variance = lax.optimization_barrier(jnp.mean(centred * centred, axis=-1, keepdims=True))
    return centred * lax.rsqrt(variance + eps) * scale_gain + shift_row

def layer_rows(token_rows, span_length, weights):
    attend_weight, attend_bias, merge_weight, merge_bias, first_gain, first_shift, expand_weight, expand_bias, reduce_weight, reduce_bias, second_gain, second_shift = weights
    model_width = token_rows.shape[1]
    full_bias = jnp.concatenate([attend_bias[:model_width], jnp.zeros((model_width,), attend_bias.dtype), attend_bias[model_width:]])
    packed = low(low_back(matmul(token_rows, attend_weight) + full_bias))
    heads_split = packed.reshape(token_rows.shape[0] // span_length, span_length, 3, HEADS, HEAD)
    scores = low_back(jnp.einsum('sqhd,skhd->shqk', heads_split[:, :, 0], heads_split[:, :, 1], precision=highest) / math.sqrt(HEAD))
    attention_probs = jax.nn.softmax(scores, axis=-1)
    attended = jnp.einsum('shqk,skhd->sqhd', low(attention_probs), heads_split[:, :, 2], precision=highest)
    attended = low(low_back(attended.reshape(token_rows.shape)))
    branch = low_back(matmul(attended, merge_weight) + merge_bias)
    normed_first = layer_norm(token_rows + branch, first_gain, first_shift)
    inner_pre = low_back(matmul(low(normed_first), expand_weight) + expand_bias)
    hidden = low(jax.nn.gelu(inner_pre, approximate=False))
    second = low_back(matmul(hidden, reduce_weight) + reduce_bias)
    return layer_norm(normed_first + second, second_gain, second_shift)

def group_rows():
    factor = 1
    while factor * 2 * TOK_DEV <= 4096 and N_DP % (factor * 2) == 0:
        factor = factor * 2
    return factor * TOK_DEV

def encoder(token_rows, span_length, weights):
    groups = token_rows.reshape(-1, group_rows(), token_rows.shape[1])

    def one_group(carry_in, group_block):
        return (carry_in, layer_rows(group_block, span_length, weights))
    _, results = lax.scan(jax.checkpoint(one_group), jnp.zeros((), token_rows.dtype), groups)
    return results.reshape(token_rows.shape)

def forward(tokens_float, weights, positives, counts):
    question_out = encoder(tokens_float[0], QLEN, tuple((member[0] for member in weights)))
    passage_out = encoder(tokens_float[1], PLEN, tuple((member[1] for member in weights)))
    question_cls = low(question_out[::QLEN])
    passage_cls = low(passage_out[::PLEN])
    match_scores = low_back(matmul(question_cls, passage_cls.T) / math.sqrt(D))
    lse_all = jax.nn.logsumexp(match_scores, axis=1)
    picked = jnp.take_along_axis(match_scores, positives, axis=1)
    live_slots = jnp.arange(KPOS, dtype=jnp.int32)[None, :] < counts[:, None]
    lse_live = jax.nn.logsumexp(jnp.where(live_slots, picked, -jnp.inf), axis=1)
    return (jnp.stack([question_out, passage_out]), jnp.mean(lse_all - lse_live))

def reference(tokens, attend_weight, attend_bias, merge_weight, merge_bias, first_gain, first_shift, expand_weight, expand_bias, reduce_weight, reduce_bias, second_gain, second_shift, cotangent, positives, counts):
    weights = tuple((member.astype(jnp.float32) for member in (attend_weight, attend_bias, merge_weight, merge_bias, first_gain, first_shift, expand_weight, expand_bias, reduce_weight, reduce_bias, second_gain, second_shift)))
    tokens_float = tokens.astype(jnp.float32)

    def objective(token_values, weight_values):
        return forward(token_values, weight_values, positives, counts)
    (final, loss_value), pullback = jax.vjp(objective, tokens_float, weights)
    token_grad, weight_grads = pullback((cotangent.astype(jnp.float32), jnp.asarray(loss_weight * NQ, jnp.float32)))
    return (final.astype(jnp.bfloat16), loss_value, token_grad.astype(jnp.bfloat16), weight_grads[0], weight_grads[1], weight_grads[2], weight_grads[3], weight_grads[4], weight_grads[5], weight_grads[6], weight_grads[7], weight_grads[8], weight_grads[9], weight_grads[10], weight_grads[11])
```

```python
from functools import partial
import math

import jax
import jax.numpy as jnp
from jax import lax
from jax.experimental import pallas as pl
from jax.experimental.pallas import tpu as pltpu
from jax.sharding import PartitionSpec as P

D = 768
HEADS = 12
HEAD = 64
QLEN = 64
PLEN = 256
BLOCK = 512
KPOS = 4
SEQ = 256
PAIRS = HEADS // 2
WIDE = 2 * HEAD

eps = 1e-06
loss_weight = 32.0
negative = -1e30
VMEM_BYTES = 64 * 1024 * 1024
TOGETHER = 1
MESH = pl.DeviceIdType.MESH
f32 = jnp.float32
bf16 = jnp.bfloat16


def dot_nn(a, b):
    return lax.dot_general(a, b, (((1,), (0,)), ((), ())), preferred_element_type=f32)


def dot_nt(a, b):
    return lax.dot_general(a, b, (((1,), (1,)), ((), ())), preferred_element_type=f32)


def dot_tn(a, b):
    return lax.dot_general(a, b, (((0,), (0,)), ((), ())), preferred_element_type=f32)


def gelu_both(v):
    density = jnp.exp(v * v * -0.5)
    t = 1.0 / (1.0 + jnp.abs(v) * (0.3275911 / math.sqrt(2.0)))
    poly = 0.5 * 1.061405429
    poly = poly * t + 0.5 * -1.453152027
    poly = poly * t + 0.5 * 1.421413741
    poly = poly * t + 0.5 * -0.284496736
    poly = poly * t + 0.5 * 0.254829592
    tail = poly * t * density
    below = jnp.where(v >= 0.0, 1.0 - tail, tail)
    return v * below, below + v * density * (1.0 / math.sqrt(2.0 * math.pi))


def norm_stats(values):
    centred = values - jnp.mean(values, axis=-1, keepdims=True)
    inverse = lax.rsqrt(jnp.mean(centred * centred, axis=-1, keepdims=True) + eps)
    return centred * inverse, inverse


def norm_back(upstream, normed, inverse, gain):
    scaled = upstream * gain
    return inverse * (
        scaled
        - jnp.mean(scaled, axis=-1, keepdims=True)
        - normed * jnp.mean(scaled * normed, axis=-1, keepdims=True)
    )


def scoped(f):
    def inner(*args):
        with jax.named_scope(f.__name__):
            return f(*args)

    return inner


def colsum(values):
    return jnp.sum(values, axis=0, keepdims=True)


SMALL = ("ab", "mb", "g1", "h1", "eb", "rb", "g2", "h2", "post", "cnt")
INPUTS = ("tok_hbm", "wa_hbm", "wm_hbm", "we_hbm", "wr_hbm", "cot_hbm") + tuple(k + "_hbm" for k in SMALL)
OUTPUTS = ("act_hbm", "loss", "dx_hbm", "dwa_hbm", "dwm_hbm", "dwe_hbm", "dwr_hbm", "dab", "dmb", "dg1", "dh1", "deb", "drb", "dg2", "dh2")


def layer_kernel(n, rows, ff, names, *refs):
    r = dict(zip(names, refs, strict=True))
    wm, we, wr, tok, pk, att_t = (r[k] for k in ("wm", "we", "wr", "tok", "pk", "att_t"))
    low1, n1, fb, hid, gp, cot = (r[k] for k in ("low1", "n1", "fb", "hid", "gp", "cot"))
    lse, s1, s2, mask, red = (r[k] for k in ("lse", "s1", "s2", "mask", "red"))
    stage32, cls, vec, vec_out = (r[k] for k in ("stage32", "cls", "vec", "vec_out"))
    ab, mb, g1, h1, eb, rb, g2, h2 = (r[k] for k in ("ab", "mb", "g1", "h1", "eb", "rb", "g2", "h2"))
    nz = n // 4
    part = D // n
    half = D // 2
    blocks = rows // SEQ
    ffc = ff // D
    thirds = D // SEQ
    shard = ff // n
    extra = rows // QLEN
    y = lax.axis_index("pair")
    me = lax.axis_index("dp")
    z = me // 4
    x = (me // 2) % 2
    c = me % 2

    sibling = {"dp": z * 4 + x * 2 + (1 - c)}
    across = {"dp": z * 4 + (1 - x) * 2 + c}
    other_pair = {"pair": 1 - y}
    along = [{"dp": ((z + k) % nz) * 4 + x * 2 + c} for k in range(1, nz)]
    partners = [sibling, across, other_pair] + along
    barrier = pltpu.get_barrier_semaphore()
    for partner in partners:
        pl.semaphore_signal(barrier, inc=1, device_id=partner, device_id_type=MESH)

    def remote(source, target, send, recv, device):
        return pltpu.make_async_remote_copy(
            src_ref=source,
            dst_ref=target,
            send_sem=send,
            recv_sem=recv,
            device_id=device,
            device_id_type=MESH,
        )

    loads = {}

    def load(key, source, target):
        loads[key] = pltpu.make_async_copy(source, target, r["load_sem"].at[len(loads)])
        loads[key].start()

    load("tok", r["tok_hbm"], tok)
    for j in range(3):
        for k in range(thirds):
            load(
                ("wa", j, k),
                r["wa_hbm"].at[:, pl.ds(j * D + k * SEQ, SEQ)],
                red.at[j, pl.ds(k * D, D), :],
            )
    for key in SMALL:
        load(key, r[key + "_hbm"], r[key])
    load("wm", r["wm_hbm"], wm)
    load("we", r["we_hbm"], we)
    load("wr", r["wr_hbm"], wr)
    load("cot", r["cot_hbm"], cot)

    row_id = lax.broadcasted_iota(jnp.int32, (SEQ, SEQ), 0)
    col_id = lax.broadcasted_iota(jnp.int32, (SEQ, SEQ), 1)
    together = ((row_id // QLEN) == (col_id // QLEN)) | (row_id * 0 + y == 1)
    mask[...] = jnp.where(together, 0.0, negative)
    vec[...] = jnp.zeros_like(vec)
    first_head = lax.broadcasted_iota(jnp.int32, (SEQ, WIDE), 1) < HEAD

    def split_heads(pair):
        zero = jnp.zeros_like(pair)
        return jnp.where(first_head, pair, zero), jnp.where(first_head, zero, pair)

    def block_rows(b, shift=0):
        return pl.ds(pl.multiple_of(b * SEQ + shift, 16), SEQ)

    def block_lanes(b):
        return pl.ds(pl.multiple_of(b * SEQ, SEQ), SEQ)

    def wide(h):
        return pl.ds(pl.multiple_of(h * WIDE, WIDE), WIDE)

    def loop(first, last, body):
        def step(i, carry):
            with jax.named_scope(body.__name__):
                body(i)
            return carry

        lax.fori_loop(first, last, step, 0)

    loads["tok"].wait()
    for key in SMALL:
        loads[key].wait()
    for j in range(3):
        for k in range(thirds):
            loads[("wa", j, k)].wait()

    def project(b):
        at = block_rows(b)
        here = tok[at, :]
        for j in range(3):
            for k in range(thirds):
                lanes = slice(k * SEQ, (k + 1) * SEQ)
                out = dot_nn(here, red[j, k * D : (k + 1) * D, :])
                if j == 0:
                    out = (out + ab[:, lanes]) * (1.0 / math.sqrt(HEAD))
                elif j == 2:
                    out = out + ab[:, D + k * SEQ : D + (k + 1) * SEQ]
                pk[j, at, lanes] = out.astype(bf16)

    loop(0, blocks, project)

    def attend_pair(b, h):
        at = block_rows(b)
        lanes = wide(h)
        key_pair = pk[1, at, lanes]
        value_t = pk[2, at, lanes].T
        mixed = []
        for s, query in enumerate(split_heads(pk[0, at, lanes])):
            scores = dot_nt(key_pair, query) + mask[...]
            peak = jnp.max(scores, axis=0, keepdims=True)
            weight = jnp.exp(scores - peak)
            total = jnp.sum(weight, axis=0, keepdims=True)
            lse[2 * (b * PAIRS + h) + s] = peak + jnp.log(total)
            out = dot_nn(value_t[s * HEAD : (s + 1) * HEAD], weight.astype(bf16))
            mixed.append(out * (1.0 / total))
        att_t[wide(h), block_lanes(b)] = jnp.concatenate(mixed, axis=0).astype(bf16)

    def attend(i):
        per = PAIRS // TOGETHER
        for k in range(TOGETHER):
            attend_pair(i // per, (i % per) * TOGETHER + k)

    loop(0, blocks * (PAIRS // TOGETHER), attend)

    loads["wm"].wait()

    def merge(b):
        at = block_rows(b)
        branch = dot_tn(att_t[:, block_lanes(b)], wm[...]) + mb[...]
        normed, inverse = norm_stats(tok[at, :].astype(f32) + branch)
        first = normed * g1[...] + h1[...]
        n1[at, :] = normed.astype(bf16)
        s1[at, :] = inverse
        fb[at, :] = first
        low1[at, :] = first.astype(bf16)

    loop(0, blocks, merge)

    loads["we"].wait()
    loads["wr"].wait()

    def act_stage(b, k):
        return red.at[k, block_rows(b), :]

    def act_copies(b):
        return [
            pltpu.make_async_copy(
                act_stage(b, k),
                r["act_hbm"].at[block_rows(b), pl.ds(k * SEQ, SEQ)],
                r["act_sem"].at[b, k],
            )
            for k in range(thirds)
        ]

    def feed_chunk(here, j):
        inner = dot_nn(here, we[:, j * D : (j + 1) * D]) + eb[:, j * D : (j + 1) * D]
        hidden, slope = gelu_both(inner)
        hidden = hidden.astype(bf16)
        return hidden, slope, dot_nn(hidden, wr[j * D : (j + 1) * D, :])

    def feed(b, halfway=None):
        at = block_rows(b)
        here = low1[at, :]
        total = rb[...]
        for j in range(ffc):
            if j == ffc // 2 and halfway is not None:
                halfway()
            hidden, slope, out = feed_chunk(here, j)
            hid[j, :, block_lanes(b)] = hidden.T
            gp[j, at, :] = slope.astype(bf16)
            total = total + out
        normed, inverse = norm_stats(fb[at, :] + total)
        final = (normed * g2[...] + h2[...]).astype(bf16)
        fb[at, :] = normed
        s2[at, :] = inverse
        for k in range(thirds):
            act_stage(b, k)[...] = final[:, k * SEQ : (k + 1) * SEQ]
        for copy in act_copies(b):
            copy.start()

    for k in range(extra):
        stage32[k : k + 1, :] = fb[k * QLEN : k * QLEN + 1, :]
    slot = ((c * 2 + y) * 2 + x) * nz + z
    first_rows = stage32[0:extra, :]
    first_low = first_rows.astype(bf16)
    leading = rb[...]
    for j in range(ffc):
        leading = leading + feed_chunk(first_low, j)[2]
    leading = norm_stats(first_rows + leading)[0] * g2[...] + h2[...]
    cls[pl.ds(pl.multiple_of(slot * extra, extra), extra), :] = leading.astype(bf16)

    def gather(stage, first, count, device):
        part_of = cls.at[pl.ds(pl.multiple_of(first * extra, extra), count * extra), :]
        return remote(part_of, part_of, r["ag_send"].at[stage], r["ag_recv"].at[stage], device)

    pl.semaphore_wait(barrier, len(partners))
    gather_z = [gather(k, slot, 1, along[k]) for k in range(nz - 1)]
    gather_x = gather(nz - 1, ((c * 2 + y) * 2 + x) * nz, nz, across)
    gather_y = gather(nz, (c * 2 + y) * 2 * nz, 2 * nz, other_pair)
    gather_c = [gather(nz + 1 + e, (c * 2 + [y, 1 - y][e]) * 2 * nz, 2 * nz, sibling) for e in range(2)]
    for copy in gather_z:
        copy.start()

    def feed_next(b):
        feed(b)

        @pl.when(b == 0)
        def _():
            for copy in gather_z:
                copy.wait()
            gather_x.start()

        @pl.when(b == 1)
        def _():
            gather_x.wait()
            gather_y.start()
            gather_c[0].start()

    def last_gather():
        gather_y.wait()
        gather_c[1].start()

    loop(0, blocks - 1, feed_next)
    feed(blocks - 1, last_gather)
    gather_c[0].wait()
    gather_c[1].wait()

    nq = n * extra
    spare = blocks * SEQ
    for d in range(n):
        there = ((d % 2) * 4 + (d // 2) % 2) * nz + d // 4
        for e in range(2):
            block = there + e * 2 * nz
            for k in range(thirds):
                red[k, spare + e * nq + d * extra : spare + e * nq + (d + 1) * extra, :] = cls[
                    block * extra : (block + 1) * extra, k * SEQ : (k + 1) * SEQ
                ]

    def gathered(e):
        return jnp.concatenate([red[k, spare + e * nq : spare + (e + 1) * nq, :] for k in range(thirds)], axis=1)

    question = gathered(0)
    passage = gathered(1)
    root_width = math.sqrt(D)
    match = dot_nt(passage, question) * (1.0 / root_width)
    place = lax.broadcasted_iota(jnp.int32, (nq, nq), 0)
    number = place // (PLEN // QLEN)
    real = place % (PLEN // QLEN) == 0
    listed = jnp.zeros((nq, nq), jnp.int32)
    for k in range(KPOS):
        wanted = jnp.where(r["cnt"][...] > k, r["post"][k : k + 1, :], -1)
        listed = jnp.where(number == wanted, 1, listed)
    listed = (listed == 1) & real
    all_scores = jnp.where(real, match, negative)
    all_peak = jnp.max(all_scores, axis=0, keepdims=True)
    all_total = jnp.sum(jnp.exp(all_scores - all_peak), axis=0, keepdims=True)
    lse_all = all_peak + jnp.log(all_total)
    live_scores = jnp.where(listed, match, negative)
    live_peak = jnp.max(live_scores, axis=0, keepdims=True)
    live_total = jnp.sum(jnp.where(listed, jnp.exp(live_scores - live_peak), 0.0), axis=0, keepdims=True)
    lse_live = live_peak + jnp.log(live_total)
    r["loss"][...] = jnp.sum(lse_all - lse_live, axis=1, keepdims=True) * (1.0 / nq)
    grad_match = jnp.exp(all_scores - lse_all) - jnp.where(listed, jnp.exp(live_scores - lse_live), 0.0)
    grad_match = (loss_weight * grad_match).astype(bf16)

    @pl.when(y == 0)
    def _():
        stage32[0:nq, :] = dot_tn(grad_match, gathered(1)) * (1.0 / root_width)

    @pl.when(y == 1)
    def _():
        stage32[0:nq, :] = dot_nn(grad_match, gathered(0)) * (1.0 / root_width)

    loads["cot"].wait()

    per_block = SEQ // QLEN
    own_rows = pl.ds(pl.multiple_of(me * extra, extra), extra)
    stage32[nq : nq + extra, :] = stage32[own_rows, :]
    top_row = lax.broadcasted_iota(jnp.int32, (8, D), 0) == 0

    def second_back(b):
        at = block_rows(b)
        given = cot[at, :].astype(f32)
        pieces = []
        for k in range(per_block):
            own = stage32[pl.ds(nq + b * per_block + k, 1), :]
            pieces.append(given[k * QLEN : k * QLEN + 8] + jnp.where(top_row, own, 0.0))
            pieces.append(given[k * QLEN + 8 : (k + 1) * QLEN])
        upstream = jnp.concatenate(pieces, axis=0)
        normed = fb[at, :]
        grad = norm_back(upstream, normed, s2[at, :], g2[...])
        low = grad.astype(bf16)
        fb[at, :] = grad
        cot[at, :] = low
        vec[5 + ffc : 6 + ffc, :] += colsum(low.astype(f32))
        vec[6 + ffc : 7 + ffc, :] += colsum(upstream * normed)
        vec[7 + ffc : 8 + ffc, :] += colsum(upstream)

    loop(0, blocks, second_back)

    units = (
        [(red, k, shard, "r", k) for k in range(thirds)]
        + [(hid, j, part, "w", j) for j in range(ffc)]
        + [(gp, j, part, "w", ffc + j) for j in range(4)]
    )
    unit_out = (
        [r["dwr_hbm"].at[:, pl.ds(k * SEQ, SEQ)] for k in range(thirds)]
        + [r["dwe_hbm"].at[:, pl.ds(j * D, D)] for j in range(ffc)]
        + [r["dwm_hbm"]]
        + [r["dwa_hbm"].at[:, pl.ds(j * D, D)] for j in range(3)]
    )

    def unit_rows(u, first, count):
        ref, j, each, kind, _ = units[u]
        at = pl.ds(pl.multiple_of(first * each, each), count * each)
        return ref.at[j, at, :] if kind == "r" else ref.at[j, at, pl.ds(0, D)]

    def arrived(u, stage):
        return r["recv_" + stage + units[u][3]].at[units[u][4]]

    def add_rows(u, first, source, source_first, count):
        each = units[u][2]

        def step(i):
            here = unit_rows(u, first + i, 1)
            more = source[pl.ds(pl.multiple_of((source_first + i) * each, each), each), :]
            here[...] = (here[...].astype(f32) + more.astype(f32)).astype(bf16)

        loop(0, count, step)

    def core_copy(u):
        return remote(
            unit_rows(u, (1 - c) * (n // 2), n // 2),
            arrived(u, "c"),
            r["c_send"].at[u],
            r["c_recv"].at[u],
            sibling,
        )

    def across_copy(u):
        return remote(
            unit_rows(u, c * (n // 2) + (1 - x) * nz, nz),
            arrived(u, "x"),
            r["x_send"].at[u],
            r["x_recv"].at[u],
            across,
        )

    def along_copy(u, k):
        return remote(
            unit_rows(u, c * (n // 2) + x * nz + (z + k) % nz, 1),
            arrived(u, "z").at[k - 1],
            r["z_send"].at[u, k - 1],
            r["z_recv"].at[u, k - 1],
            along[k - 1],
        )

    def out_stage(u):
        _, _, each, kind, at = units[u]
        return r["stage_r" if kind == "r" else "stage32"].at[pl.ds(at * each, each), :]

    def out_copy(u):
        return pltpu.make_async_copy(out_stage(u), unit_out[u], r["out_sem"].at[u])

    @scoped
    def core_start(u):
        core_copy(u).start()

    @scoped
    def across_start(u):
        core_copy(u).wait_recv()
        add_rows(u, c * (n // 2) + (1 - x) * nz, arrived(u, "c"), (1 - x) * nz, nz)
        across_copy(u).start()
        add_rows(u, c * (n // 2) + x * nz, arrived(u, "c"), x * nz, nz)

    @scoped
    def along_start(u):
        across_copy(u).wait_recv()
        add_rows(u, c * (n // 2) + x * nz, arrived(u, "x"), 0, nz)
        for k in range(1, nz):
            along_copy(u, k).start()

    @scoped
    def finish(u):
        total = unit_rows(u, c * (n // 2) + x * nz + z, 1)[...].astype(f32)
        for k in range(1, nz):
            along_copy(u, k).wait_recv()
            total = total + arrived(u, "z")[k - 1].astype(f32)
        out_stage(u)[...] = total
        out_copy(u).start()

    def spot(d):
        return ((d % 2) * 2 + (d // 2) % 2) * nz + d // 4

    def spread(u, result, first):
        for d in range(first, first + result.shape[0] // part):
            piece = result[(d - first) * part : (d - first + 1) * part]
            unit_rows(u, spot(d), 1)[...] = piece.astype(bf16)

    for b in range(blocks):
        for copy in act_copies(b):
            copy.wait()
    for u in range(thirds):

        def reduce_grad(t, u=u):
            tiles = D // (2 * shard)
            left = hid[t // tiles, pl.ds(pl.multiple_of((t % tiles) * 2 * shard, 16), 2 * shard), :]
            result = dot_nn(left, cot[:, u * SEQ : (u + 1) * SEQ]).astype(bf16)
            for cc in range(2):
                unit_rows(u, (cc * 2 + t % 2) * nz + t // 2, 1)[...] = result[cc * shard : (cc + 1) * shard]

        loop(0, n // 2, reduce_grad)
        core_start(u)
        if u > 0:
            across_start(u - 1)
    expand_at = thirds
    merge_at = thirds + ffc
    attend_at = merge_at + 1

    for j in range(ffc):

        def inner_back(b, j=j):
            at = block_rows(b)
            grad_hidden = dot_nt(cot[at, :], wr[j * D : (j + 1) * D, :])
            low = (grad_hidden * gp[j, at, :].astype(f32)).astype(bf16)
            gp[j, at, :] = low
            vec[5 + j : 6 + j, :] += colsum(low.astype(f32))
            fb[at, :] += dot_nt(low, we[:, j * D : (j + 1) * D])

        loop(0, blocks, inner_back)
        if j == 1:
            along_start(0)
            across_start(2)
        elif j == 2:
            along_start(1)
            across_start(expand_at)
        for t in range(2):
            left = low1[:, t * half : (t + 1) * half]
            spread(expand_at + j, dot_tn(left, gp[j]), (n // 2) * t)
        core_start(expand_at + j)
        if j == 2:
            finish(0)
        elif j == 3:
            along_start(2)
            across_start(expand_at + 1)
    load("wa_again", r["wa_hbm"], we.at[:, pl.ds(0, 3 * D)])

    def first_back(b):
        at = block_rows(b)
        upstream = fb[at, :]
        normed = n1[at, :].astype(f32)
        grad = norm_back(upstream, normed, s1[at, :], g1[...])
        low = grad.astype(bf16)
        fb[at, :] = grad
        cot[at, :] = low
        vec[2:3, :] += colsum(low.astype(f32))
        vec[3:4, :] += colsum(upstream * normed)
        vec[4:5, :] += colsum(upstream)
        n1[at, :] = dot_nt(low, wm[...]).astype(bf16)

    loop(0, blocks, first_back)
    for t in range(2):
        spread(merge_at, dot_nn(att_t[t * half : (t + 1) * half, :], cot[...]), (n // 2) * t)
    core_start(merge_at)
    along_start(expand_at)
    across_start(expand_at + 2)
    finish(1)

    def attend_back(i):
        b = i // PAIRS
        h = i % PAIRS
        at = block_rows(b)
        lanes = wide(h)
        key_pair = pk[1, at, lanes]
        value_pair = pk[2, at, lanes]
        key_t = key_pair.T
        queries = split_heads(pk[0, at, lanes])
        grads = split_heads(n1[at, lanes])
        probs = []
        slopes = []
        query_grads = []
        for s in range(2):
            prob = jnp.exp(dot_nt(key_pair, queries[s]) + mask[...] - lse[2 * i + s])
            grad_prob = dot_nt(value_pair, grads[s])
            mean = jnp.sum(prob * grad_prob, axis=0, keepdims=True)
            slope = (prob * (grad_prob - mean)).astype(bf16)
            probs.append(prob.astype(bf16))
            slopes.append(slope)
            query_grads.append(dot_nn(key_t[s * HEAD : (s + 1) * HEAD], slope))
        grad_value = dot_nn(jnp.concatenate(probs, axis=1), jnp.concatenate(grads, axis=0)).astype(bf16)
        grad_key = dot_nn(jnp.concatenate(slopes, axis=1), jnp.concatenate(queries, axis=0)).astype(bf16)
        grad_query = (jnp.concatenate(query_grads, axis=0) * (1.0 / math.sqrt(HEAD))).T.astype(bf16)
        pk[0, at, lanes] = grad_query
        pk[1, at, lanes] = grad_key
        pk[2, at, lanes] = grad_value
        vec[0:1, lanes] += colsum(grad_query.astype(f32))
        vec[1:2, lanes] += colsum(grad_value.astype(f32))

        @pl.when(i == 7)
        def _():
            along_start(expand_at + 1)
            across_start(expand_at + 3)
            finish(2)

        @pl.when(i == 14)
        def _():
            along_start(expand_at + 2)
            across_start(merge_at)
            finish(expand_at)

        @pl.when(i == 21)
        def _():
            along_start(expand_at + 3)
            finish(expand_at + 1)

    loop(0, blocks * PAIRS, attend_back)

    for d in range(n):
        def chunk(row, first, d=d):
            at = first * part
            return vec[row + at // D : row + at // D + 1, at % D : at % D + part]

        at = spot(d)
        for e in range(2):
            vec_out[at, e : e + 1, 0:part] = chunk(0, 2 * d + e)
        for e in range(3):
            vec_out[at, 2 + e : 3 + e, 0:part] = chunk(2 + e, d)
            vec_out[at, 5 + ffc + e : 6 + ffc + e, 0:part] = chunk(5 + ffc + e, d)
        for e in range(ffc):
            vec_out[at, 5 + e : 6 + e, 0:part] = chunk(5, ffc * d + e)

    def vec_part(first, count):
        return vec_out.at[pl.ds(first, count)]

    mine = c * (n // 2) + x * nz
    vec_c = remote(
        vec_part((1 - c) * (n // 2), n // 2), r["vec_c"], r["v_send"].at[0], r["v_recv"].at[0], sibling
    )
    vec_x = remote(
        vec_part(c * (n // 2) + (1 - x) * nz, nz), r["vec_x"], r["v_send"].at[1], r["v_recv"].at[1], across
    )
    vec_z = [
        remote(
            vec_part(mine + (z + k) % nz, 1),
            r["vec_z"].at[pl.ds(k - 1, 1)],
            r["v_send"].at[1 + k],
            r["v_recv"].at[1 + k],
            along[k - 1],
        )
        for k in range(1, nz)
    ]
    vec_c.start()

    for j in range(3):
        unit = attend_at + j
        for t in range(2):
            spread(unit, dot_tn(tok[:, t * half : (t + 1) * half], pk[j]), (n // 2) * t)
        core_start(unit)
        if j == 0:
            vec_c.wait()
            vec_out[pl.ds(c * (n // 2), n // 2)] += r["vec_c"][...]
            vec_x.start()
        elif j == 1:
            across_start(attend_at)
            along_start(merge_at)
            finish(expand_at + 2)
            vec_x.wait()
            vec_out[pl.ds(mine, nz)] += r["vec_x"][...]
            for copy in vec_z:
                copy.start()

    loads["wa_again"].wait()

    def dx_copy(b):
        return pltpu.make_async_copy(tok.at[block_rows(b), :], r["dx_hbm"].at[block_rows(b), :], r["dx_sem"].at[b])

    def token_grad(b):
        at = block_rows(b)
        total = fb[at, :]
        for j in range(3):
            total = total + dot_nt(pk[j, at, :], we[:, j * D : (j + 1) * D])
        tok[at, :] = total.astype(bf16)
        dx_copy(b).start()

        @pl.when(b == 0)
        def _():
            across_start(attend_at + 1)
            finish(expand_at + 3)

        @pl.when(b == 3)
        def _():
            along_start(attend_at)
            across_start(attend_at + 2)
            finish(merge_at)

    loop(0, blocks, token_grad)
    for copy in vec_z:
        copy.wait()
    total = vec_out[mine + z]
    for k in range(1, nz):
        total = total + r["vec_z"][k - 1]
    for e in range(2):
        r["dab"][:, e * part : (e + 1) * part] = total[e : e + 1, 0:part]
    for e in range(ffc):
        r["deb"][:, e * part : (e + 1) * part] = total[5 + e : 6 + e, 0:part]
    for key, row in (("dmb", 2), ("dg1", 3), ("dh1", 4), ("drb", 5 + ffc), ("dg2", 6 + ffc), ("dh2", 7 + ffc)):
        r[key][...] = total[row : row + 1, 0:part]
    along_start(attend_at + 1)
    finish(attend_at)
    along_start(attend_at + 2)
    finish(attend_at + 1)
    finish(attend_at + 2)
    for u in range(len(units)):
        core_copy(u).wait_send()
        across_copy(u).wait_send()
        for k in range(1, nz):
            along_copy(u, k).wait_send()
        out_copy(u).wait()
    for b in range(blocks):
        dx_copy(b).wait()


def hand_over_kernel(count, *refs):
    given, wanted, held = (refs[k * count : (k + 1) * count] for k in range(3))
    sems = refs[-1]
    arriving = [pltpu.make_async_copy(given[k], held[k], sems.at[0, k]) for k in range(count)]
    leaving = [pltpu.make_async_copy(held[k], wanted[k], sems.at[1, k]) for k in range(count)]
    for copy in arriving:
        copy.start()
    for k in range(count):
        arriving[k].wait()
        leaving[k].start()
    for copy in leaving:
        copy.wait()


def fused_shards(n, *args):
    tokens, cotangent = args[0][0], args[13][0]
    rows = tokens.shape[0]
    ff = args[7].shape[2]
    ffc = ff // D
    nz = n // 4
    part = D // n
    shard = ff // n
    thirds = D // SEQ
    extra = rows // QLEN
    blocks = rows // SEQ
    wide_units = ffc + 4
    units = thirds + wide_units
    wa, wm, we, wr = (args[k][0] for k in (1, 3, 7, 9))
    small = [args[k] for k in (2, 4, 5, 6, 8, 10, 11, 12)] + [args[14].T, args[15][None, :]]
    dma = pltpu.SemaphoreType.DMA
    scratch = dict(
        zip(SMALL, [pltpu.VMEM(value.shape, value.dtype) for value in small], strict=True),
        wm=pltpu.VMEM((D, D), bf16),
        we=pltpu.VMEM((D, ff), bf16),
        wr=pltpu.VMEM((ff, D), bf16),
        tok=pltpu.VMEM((rows, D), bf16),
        pk=pltpu.VMEM((3, rows, D), bf16),
        att_t=pltpu.VMEM((D, rows), bf16),
        low1=pltpu.VMEM((rows, D), bf16),
        n1=pltpu.VMEM((rows, D), bf16),
        fb=pltpu.VMEM((rows, D), f32),
        hid=pltpu.VMEM((ffc, D, rows), bf16),
        gp=pltpu.VMEM((ffc, rows, D), bf16),
        cot=pltpu.VMEM((rows, D), bf16),
        lse=pltpu.VMEM((blocks * HEADS, 1, SEQ), f32),
        s1=pltpu.VMEM((rows, 1), f32),
        s2=pltpu.VMEM((rows, 1), f32),
        mask=pltpu.VMEM((SEQ, SEQ), f32),
        red=pltpu.VMEM((thirds, ff, SEQ), bf16),
        stage_r=pltpu.VMEM((thirds * shard, SEQ), f32),
        stage32=pltpu.VMEM((wide_units * part, D), f32),
        cls=pltpu.VMEM((8 * nz * extra, D), bf16),
        vec=pltpu.VMEM((16, D), f32),
        vec_out=pltpu.VMEM((n, 16, 128), f32),
        vec_c=pltpu.VMEM((n // 2, 16, 128), f32),
        vec_x=pltpu.VMEM((nz, 16, 128), f32),
        vec_z=pltpu.VMEM((nz - 1, 16, 128), f32),
        recv_cr=pltpu.VMEM((thirds, ff // 2, SEQ), bf16),
        recv_xr=pltpu.VMEM((thirds, ff // 4, SEQ), bf16),
        recv_zr=pltpu.VMEM((thirds, nz - 1, shard, SEQ), bf16),
        recv_cw=pltpu.VMEM((wide_units, D // 2, D), bf16),
        recv_xw=pltpu.VMEM((wide_units, D // 4, D), bf16),
        recv_zw=pltpu.VMEM((wide_units, nz - 1, part, D), bf16),
        load_sem=dma((32,)),
        act_sem=dma((blocks, thirds)),
        dx_sem=dma((blocks,)),
        out_sem=dma((units,)),
        c_send=dma((units,)),
        c_recv=dma((units,)),
        x_send=dma((units,)),
        x_recv=dma((units,)),
        z_send=dma((units, nz - 1)),
        z_recv=dma((units, nz - 1)),
        ag_send=dma((nz + 3,)),
        ag_recv=dma((nz + 3,)),
        v_send=dma((nz + 1,)),
        v_recv=dma((nz + 1,)),
    )
    names = list(INPUTS) + list(OUTPUTS) + list(scratch)
    hbm = pl.BlockSpec(memory_space=pl.ANY)
    near = pl.BlockSpec(memory_space=pltpu.VMEM)
    shape = jax.ShapeDtypeStruct
    shapes = [
        shape((rows, D), bf16),
        shape((1, 1), f32),
        shape((rows, D), bf16),
        shape((part, 3 * D), f32),
        shape((part, D), f32),
        shape((part, ff), f32),
        shape((ff // n, D), f32),
        shape((1, 2 * part), f32),
        shape((1, part), f32),
        shape((1, part), f32),
        shape((1, part), f32),
        shape((1, ff // n), f32),
        shape((1, part), f32),
        shape((1, part), f32),
        shape((1, part), f32),
    ]
    outs = pl.pallas_call(
        partial(layer_kernel, n, rows, ff, names),
        out_shape=shapes,
        in_specs=[hbm] * (6 + len(small)),
        out_specs=[hbm, near] + [hbm] * 5 + [near] * 8,
        scratch_shapes=list(scratch.values()),
        compiler_params=pltpu.CompilerParams(
            collective_id=0, has_side_effects=True, vmem_limit_bytes=VMEM_BYTES
        ),
    )(tokens, wa, wm, we, wr, cotangent, *small)
    act, loss, dx, dwa, dwm, dwe, dwr, dab, dmb, dg1, dh1, deb, drb, dg2, dh2 = pl.pallas_call(
        partial(hand_over_kernel, len(shapes)),
        out_shape=shapes,
        in_specs=[hbm] * len(shapes),
        out_specs=[hbm] * len(shapes),
        scratch_shapes=[pltpu.VMEM(out.shape, out.dtype) for out in shapes] + [dma((2, len(shapes)))],
    )(*outs)
    return (
        act[None],
        loss[0, 0],
        dx[None],
        dwa[None],
        dab,
        dwm[None],
        dmb,
        dg1,
        dh1,
        dwe[None],
        deb,
        dwr[None],
        drb,
        dg2,
        dh2,
    )


def layer_norm(values, scale_gain, shift_row):
    centred = values - jnp.mean(values, axis=-1, keepdims=True)
    inverse = lax.rsqrt(jnp.mean(centred * centred, axis=-1, keepdims=True) + eps)
    normed = centred * inverse
    return (normed * scale_gain + shift_row, normed, inverse)


def norm_backward(upstream, normed, inverse, scale_gain):
    scaled = upstream * scale_gain
    centred = (
        scaled
        - jnp.mean(scaled, axis=-1, keepdims=True)
        - normed * jnp.mean(scaled * normed, axis=-1, keepdims=True)
    )
    return (centred * inverse, jnp.sum(upstream * normed, axis=0), jnp.sum(upstream, axis=0))


def masked_scores(query_block, key_block, same_sequence):
    raw_scores = jnp.einsum(
        "qhd,khd->hqk", query_block, key_block, preferred_element_type=jnp.float32
    ) * (1.0 / math.sqrt(HEAD))
    return jnp.where(same_sequence[None], raw_scores, negative)


def shards(
    tokens,
    attend_weight,
    attend_bias,
    merge_weight,
    merge_bias,
    first_gain,
    first_shift,
    expand_weight,
    expand_bias,
    reduce_weight,
    reduce_bias,
    second_gain,
    second_shift,
    cotangent,
    positives,
    counts,
):
    half_index = lax.axis_index("pair")
    group_index = lax.axis_index("dp")
    span_length = jnp.where(half_index == 0, QLEN, PLEN).astype(jnp.int32)
    token_rows = tokens[0]
    row_count, model_width = token_rows.shape
    block_count = row_count // BLOCK
    places = jnp.arange(BLOCK, dtype=jnp.int32) // span_length
    same_sequence = places[:, None] == places[None, :]
    zero_keys = jnp.zeros((model_width,), jnp.float32)
    full_bias = jnp.concatenate(
        [attend_bias[0, :model_width], zero_keys, attend_bias[0, model_width:]]
    )
    packed = (
        jnp.dot(token_rows, attend_weight[0], preferred_element_type=jnp.float32) + full_bias
    ).astype(jnp.bfloat16)
    heads_split = packed.reshape(block_count, BLOCK, 3, HEADS, HEAD)
    queries = heads_split[:, :, 0]
    keys_all = heads_split[:, :, 1]
    values_all = heads_split[:, :, 2]

    def attend_block(members):
        query_block, key_block, value_block = members
        scores = masked_scores(query_block, key_block, same_sequence)
        peak = jnp.max(scores, axis=-1, keepdims=True)
        totals = jnp.sum(jnp.exp(scores - peak), axis=-1, keepdims=True)
        log_total = peak + jnp.log(totals)
        probs16 = jnp.exp(scores - log_total).astype(jnp.bfloat16)
        mixed = jnp.einsum("hqk,khd->qhd", probs16, value_block, preferred_element_type=jnp.float32)
        return (mixed, log_total[..., 0])

    attended, log_totals = lax.map(attend_block, (queries, keys_all, values_all))
    attended16 = attended.reshape(row_count, model_width).astype(jnp.bfloat16)
    branch = (
        jnp.dot(attended16, merge_weight[0], preferred_element_type=jnp.float32) + merge_bias[0]
    )
    rows_float = token_rows.astype(jnp.float32)
    normed_first, first_normed, first_inverse = layer_norm(
        rows_float + branch, first_gain[0], first_shift[0]
    )
    first16 = normed_first.astype(jnp.bfloat16)
    inner_pre = (
        jnp.dot(first16, expand_weight[0], preferred_element_type=jnp.float32) + expand_bias[0]
    )
    hidden16 = jax.nn.gelu(inner_pre, approximate=False).astype(jnp.bfloat16)
    second = (
        jnp.dot(hidden16, reduce_weight[0], preferred_element_type=jnp.float32) + reduce_bias[0]
    )
    final, final_normed, final_inverse = layer_norm(
        normed_first + second, second_gain[0], second_shift[0]
    )
    question_count = row_count // QLEN
    passage_count = row_count // PLEN
    leading = final.reshape(question_count, QLEN, model_width)[:, 0].astype(jnp.bfloat16)
    every_leading = lax.all_gather(leading, ("pair", "dp"), axis=0, tiled=True)
    half_rows = every_leading.shape[0] // 2
    question_cls = every_leading[:half_rows]
    passage_cls = every_leading[half_rows:].reshape(-1, PLEN // QLEN, model_width)[:, 0]
    root_width = math.sqrt(D)
    match_scores = (
        jnp.einsum("qd,pd->qp", question_cls, passage_cls, preferred_element_type=jnp.float32)
        / root_width
    )
    row_peak = jnp.max(match_scores, axis=1, keepdims=True)
    lse_all = row_peak + jnp.log(jnp.sum(jnp.exp(match_scores - row_peak), axis=1, keepdims=True))
    picked = jnp.take_along_axis(match_scores, positives, axis=1)
    live_slots = jnp.arange(KPOS, dtype=jnp.int32)[None, :] < counts[:, None]
    live_peak = jnp.max(jnp.where(live_slots, picked, negative), axis=1, keepdims=True)
    live_total = jnp.sum(
        jnp.where(live_slots, jnp.exp(picked - live_peak), 0.0), axis=1, keepdims=True
    )
    lse_live = live_peak + jnp.log(live_total)
    loss_value = jnp.mean(lse_all[:, 0] - lse_live[:, 0])
    live_weights = jnp.where(live_slots, jnp.exp(picked - lse_live), 0.0)
    columns = jnp.arange(match_scores.shape[1], dtype=jnp.int32)[None, :]
    grad_match = jnp.exp(match_scores - lse_all)
    for slot in range(KPOS):
        grad_match = grad_match - jnp.where(
            columns == positives[:, slot : slot + 1], live_weights[:, slot : slot + 1], 0.0
        )
    grad_match16 = (loss_weight * grad_match).astype(jnp.bfloat16)
    own_questions = lax.dynamic_slice_in_dim(
        grad_match16, group_index * question_count, question_count, 0
    )
    grad_question = (
        jnp.dot(own_questions, passage_cls, preferred_element_type=jnp.float32) / root_width
    )
    own_passages = lax.dynamic_slice_in_dim(
        grad_match16, group_index * passage_count, passage_count, 1
    )
    grad_passage = (
        jnp.einsum("qp,qd->pd", own_passages, question_cls, preferred_element_type=jnp.float32)
        / root_width
    )
    spread_question = (
        jnp.zeros((question_count, QLEN, model_width), jnp.float32)
        .at[:, 0]
        .set(grad_question)
        .reshape(row_count, model_width)
    )
    spread_passage = (
        jnp.zeros((passage_count, PLEN, model_width), jnp.float32)
        .at[:, 0]
        .set(grad_passage)
        .reshape(row_count, model_width)
    )
    grad_final = cotangent[0].astype(jnp.float32) + jnp.where(
        half_index == 0, spread_question, spread_passage
    )
    grad_pair_two, second_gain_grad, second_shift_grad = norm_backward(
        grad_final, final_normed, final_inverse, second_gain[0]
    )
    grad_second16 = grad_pair_two.astype(jnp.bfloat16)
    reduce_weight_grad = jnp.einsum(
        "tf,td->fd", hidden16, grad_second16, preferred_element_type=jnp.float32
    )
    reduce_bias_grad = jnp.sum(grad_second16.astype(jnp.float32), axis=0)
    grad_hidden = jnp.einsum(
        "td,fd->tf", grad_second16, reduce_weight[0], preferred_element_type=jnp.float32
    )
    _, gelu_pullback = jax.vjp(partial(jax.nn.gelu, approximate=False), inner_pre)
    grad_inner16 = gelu_pullback(grad_hidden)[0].astype(jnp.bfloat16)
    expand_weight_grad = jnp.einsum(
        "td,tf->df", first16, grad_inner16, preferred_element_type=jnp.float32
    )
    expand_bias_grad = jnp.sum(grad_inner16.astype(jnp.float32), axis=0)
    grad_first = (
        jnp.einsum("tf,df->td", grad_inner16, expand_weight[0], preferred_element_type=jnp.float32)
        + grad_pair_two
    )
    feed_shares = (
        expand_weight_grad,
        expand_bias_grad,
        reduce_weight_grad,
        reduce_bias_grad,
        second_gain_grad,
        second_shift_grad,
    )
    grad_pair_one, first_gain_grad, first_shift_grad = norm_backward(
        grad_first, first_normed, first_inverse, first_gain[0]
    )
    grad_branch16 = grad_pair_one.astype(jnp.bfloat16)
    merge_weight_grad = jnp.einsum(
        "td,te->de", attended16, grad_branch16, preferred_element_type=jnp.float32
    )
    merge_bias_grad = jnp.sum(grad_branch16.astype(jnp.float32), axis=0)
    grad_attended16 = jnp.einsum(
        "te,de->td", grad_branch16, merge_weight[0], preferred_element_type=jnp.float32
    ).astype(jnp.bfloat16)
    grad_attended_blocks = grad_attended16.reshape(block_count, BLOCK, HEADS, HEAD)

    def attend_backward(members):
        query_block, key_block, value_block, grad_out, log_total = members
        scores = masked_scores(query_block, key_block, same_sequence)
        probs = jnp.exp(scores - log_total[..., None])
        probs16 = probs.astype(jnp.bfloat16)
        grad_value = jnp.einsum(
            "hqk,qhd->khd", probs16, grad_out, preferred_element_type=jnp.float32
        )
        grad_probs = jnp.einsum(
            "qhd,khd->hqk", grad_out, value_block, preferred_element_type=jnp.float32
        )
        grad_scores16 = (
            probs * (grad_probs - jnp.sum(probs * grad_probs, axis=-1, keepdims=True))
        ).astype(jnp.bfloat16)
        grad_query = jnp.einsum(
            "hqk,khd->qhd", grad_scores16, key_block, preferred_element_type=jnp.float32
        ) * (1.0 / math.sqrt(HEAD))
        grad_key = jnp.einsum(
            "hqk,qhd->khd", grad_scores16, query_block, preferred_element_type=jnp.float32
        ) * (1.0 / math.sqrt(HEAD))
        return (grad_query, grad_key, grad_value)

    grad_queries, grad_keys, grad_values = lax.map(
        attend_backward, (queries, keys_all, values_all, grad_attended_blocks, log_totals)
    )
    grad_packed16 = (
        jnp.stack([grad_queries, grad_keys, grad_values], axis=2)
        .reshape(row_count, 3 * model_width)
        .astype(jnp.bfloat16)
    )
    attend_weight_grad = jnp.einsum(
        "td,te->de", token_rows, grad_packed16, preferred_element_type=jnp.float32
    )
    packed_sums = jnp.sum(grad_packed16.astype(jnp.float32), axis=0)
    attend_bias_grad = jnp.concatenate([packed_sums[:model_width], packed_sums[2 * model_width :]])
    grad_rows = (
        jnp.einsum("te,de->td", grad_packed16, attend_weight[0], preferred_element_type=jnp.float32)
        + grad_pair_one
    )
    every_share = (
        lax.psum_scatter(attend_weight_grad, "dp", scatter_dimension=0, tiled=True),
        lax.psum_scatter(attend_bias_grad, "dp", scatter_dimension=0, tiled=True),
        lax.psum_scatter(merge_weight_grad, "dp", scatter_dimension=0, tiled=True),
        lax.psum_scatter(merge_bias_grad, "dp", scatter_dimension=0, tiled=True),
        lax.psum_scatter(first_gain_grad, "dp", scatter_dimension=0, tiled=True),
        lax.psum_scatter(first_shift_grad, "dp", scatter_dimension=0, tiled=True),
        lax.psum_scatter(expand_weight_grad, "dp", scatter_dimension=0, tiled=True),
        lax.psum_scatter(expand_bias_grad, "dp", scatter_dimension=0, tiled=True),
        lax.psum_scatter(reduce_weight_grad, "dp", scatter_dimension=0, tiled=True),
        lax.psum_scatter(reduce_bias_grad, "dp", scatter_dimension=0, tiled=True),
        lax.psum_scatter(second_gain_grad, "dp", scatter_dimension=0, tiled=True),
        lax.psum_scatter(second_shift_grad, "dp", scatter_dimension=0, tiled=True),
    )
    attend_shares = every_share[:6]
    feed_shares = every_share[6:]
    return (
        final.astype(jnp.bfloat16)[None],
        loss_value,
        grad_rows.astype(jnp.bfloat16)[None],
        attend_shares[0][None],
        attend_shares[1][None],
        attend_shares[2][None],
        attend_shares[3][None],
        attend_shares[4][None],
        attend_shares[5][None],
        feed_shares[0][None],
        feed_shares[1][None],
        feed_shares[2][None],
        feed_shares[3][None],
        feed_shares[4][None],
        feed_shares[5][None],
    )


def solution(mesh):
    in_specs = (
        P("pair", "dp", None),
        P("pair", None, None),
        P("pair", None),
        P("pair", None, None),
        P("pair", None),
        P("pair", None),
        P("pair", None),
        P("pair", None, None),
        P("pair", None),
        P("pair", None, None),
        P("pair", None),
        P("pair", None),
        P("pair", None),
        P("pair", "dp", None),
        P(),
        P(),
    )
    out_specs = (
        P("pair", "dp", None),
        P(),
        P("pair", "dp", None),
        P("pair", "dp", None),
        P("pair", "dp"),
        P("pair", "dp", None),
        P("pair", "dp"),
        P("pair", "dp"),
        P("pair", "dp"),
        P("pair", "dp", None),
        P("pair", "dp"),
        P("pair", "dp", None),
        P("pair", "dp"),
        P("pair", "dp"),
        P("pair", "dp"),
    )
    n = mesh.shape["dp"]
    fits = mesh.shape["pair"] == 2 and n % 4 == 0 and D % n == 0 and (D // n) % 16 == 0
    body = partial(fused_shards, n) if fits else shards
    return jax.shard_map(body, mesh=mesh, in_specs=in_specs, out_specs=out_specs, check_vma=False)
```

```python
from functools import partial
import math
from types import SimpleNamespace

import jax
import jax.numpy as jnp
from jax import lax
from jax.experimental import pallas as pl
from jax.experimental.pallas import tpu as pltpu
from jax.sharding import PartitionSpec as P

D = 768
HEADS = 12
HEAD = 64
QLEN = 64
PLEN = 256
BLOCK = 512
KPOS = 4
SEQ = 256
PAIRS = HEADS // 2
WIDE = 2 * HEAD

eps = 1e-06
loss_weight = 32.0
negative = -1e30
VMEM_BYTES = 64 * 1024 * 1024
TOGETHER = 6
BACK_TOGETHER = 2
LINE = 4
PIECES = (1, 1, 1, 1, 1, 1, 1, 1, 1, 2, 2)
MODES = "babbaaaaaaaab"
SCHEDULE = {
    "r0": ((0, 0),),
    "r1": ((0, 1),),
    "r2_0": ((1, 0),),
    "r2": ((0, 2), (1, 1),),
    "i0_0": ((2, 0),),
    "i0_1": ((1, 2),),
    "e0": ((0, 3),),
    "i1_1": ((2, 2), (1, 3),),
    "e1": ((0, 4),),
    "i2_0": ((2, 1), (2, 3),),
    "i2_1": ((3, 0), (1, 4),),
    "e2": ((0, 5),),
    "i3_1": ((1, 5), (3, 2), (3, 1),),
    "e3": ((0, 6),),
    "f1": ((3, 3),),
    "f2": ((1, 6),),
    "f3": ((4, 0),),
    "m": ((0, 7),),
    "t1": ((2, 4),),
    "t2": ((1, 7), (4, 2),),
    "t5": ((2, 5),),
    "t6": ((4, 1),),
    "t10": ((2, 6), (3, 4), (4, 3),),
    "v": ((0, 13),),
    "a0": ((0, 8), (3, 5), (1, 13),),
    "a1": ((0, 9), (0, 10), (2, 7), (1, 8), (2, 13), (4, 4),),
    "a2": ((0, 11), (0, 12), (3, 6), (1, 9), (1, 10), (4, 5),),
    "x0": ((1, 11),),
    "x2": ((1, 12), (3, 7), (4, 6), (3, 13), (2, 8),),
    "x3": ((2, 12),),
    "end": ((2, 9), (4, 7), (2, 10), (3, 8), (3, 9), (2, 11), (3, 10), (4, 8), (3, 12), (4, 9), (3, 11), (4, 10), (4, 12), (4, 11),),
}
MESH = pl.DeviceIdType.MESH
f32 = jnp.float32
bf16 = jnp.bfloat16


def dot_nn(a, b):
    return lax.dot_general(a, b, (((1,), (0,)), ((), ())), preferred_element_type=f32)


def dot_nt(a, b):
    return lax.dot_general(a, b, (((1,), (1,)), ((), ())), preferred_element_type=f32)


def dot_tn(a, b):
    return lax.dot_general(a, b, (((0,), (0,)), ((), ())), preferred_element_type=f32)


def gelu_both(v):
    below = 0.5 + 0.5 * lax.erf(v * (1.0 / math.sqrt(2.0)))
    density = jnp.exp(v * v * -0.5) * (1.0 / math.sqrt(2.0 * math.pi))
    return v * below, below + v * density


def norm_stats(values):
    centred = values - jnp.mean(values, axis=-1, keepdims=True)
    inverse = lax.rsqrt(jnp.mean(centred * centred, axis=-1, keepdims=True) + eps)
    return centred * inverse, inverse


def norm_back(upstream, normed, inverse, gain):
    scaled = upstream * gain
    return inverse * (
        scaled
        - jnp.mean(scaled, axis=-1, keepdims=True)
        - normed * jnp.mean(scaled * normed, axis=-1, keepdims=True)
    )


def scoped(f):
    def inner(*args):
        with jax.named_scope(f.__name__):
            return f(*args)

    return inner


def colsum(values):
    return jnp.sum(values, axis=0, keepdims=True)


def colsum_low(values):
    return dot_nn(jnp.ones((8, values.shape[0]), values.dtype), values)[0:1]


def layer_kernel(n, rows, ff, names, small_count, *refs):
    r = SimpleNamespace(**dict(zip(names, refs, strict=True)))
    wm, we, wr, tok, pk, att_t = r.wm, r.we, r.wr, r.tok, r.pk, r.att_t
    low1, n1, fb, hid, gp, cot = r.low1, r.n1, r.fb, r.hid, r.gp, r.cot
    lse, s1, s2, mask, red = r.lse, r.s1, r.s2, r.mask, r.red
    stage32, cls, vec, vec_out = r.stage32, r.cls, r.vec, r.vec_out
    ab, mb, g1, h1, eb, rb, g2, h2 = r.ab, r.mb, r.g1, r.h1, r.eb, r.rb, r.g2, r.h2
    small = list(zip(refs[6 : 6 + small_count], (ab, mb, g1, h1, eb, rb, g2, h2, r.post, r.cnt), strict=True))
    nz = n // 4
    part = D // n
    half = D // 2
    blocks = rows // SEQ
    ffc = ff // D
    thirds = D // SEQ
    shard = ff // n
    extra = rows // QLEN
    y = lax.axis_index("pair")
    me = lax.axis_index("dp")
    z = me // 4
    x = (me // 2) % 2
    c = me % 2

    sibling = {"dp": z * 4 + x * 2 + (1 - c)}
    across = {"dp": z * 4 + (1 - x) * 2 + c}
    other_pair = {"pair": 1 - y}
    slanted = {"pair": 1 - y, "dp": z * 4 + (1 - x) * 2 + c}
    along = [{"dp": ((z + k) % nz) * 4 + x * 2 + c} for k in range(1, nz)]
    partners = [sibling, across, other_pair, slanted] + along
    barrier = pltpu.get_barrier_semaphore()
    for partner in partners:
        pl.semaphore_signal(barrier, inc=1, device_id=partner, device_id_type=MESH)

    def remote(source, target, send, recv, device):
        return pltpu.make_async_remote_copy(
            src_ref=source,
            dst_ref=target,
            send_sem=send,
            recv_sem=recv,
            device_id=device,
            device_id_type=MESH,
        )

    loads = {}

    def load(key, source, target):
        loads[key] = pltpu.make_async_copy(source, target, r.load_sem.at[len(loads)])
        loads[key].start()

    load("tok", r.tok_hbm, tok)
    for j in range(3):
        for k in range(thirds):
            load(
                ("wa", j, k),
                r.wa_hbm.at[:, pl.ds(j * D + k * SEQ, SEQ)],
                red.at[j, pl.ds(k * D, D), :],
            )
    for k, (source, target) in enumerate(small):
        load(k, source, target)
    load("wm", r.wm_hbm, wm)
    load("we", r.we_hbm, we)
    load("wr", r.wr_hbm, wr)
    load("cot", r.cot_hbm, cot)

    row_id = lax.broadcasted_iota(jnp.int32, (SEQ, SEQ), 0)
    col_id = lax.broadcasted_iota(jnp.int32, (SEQ, SEQ), 1)
    together = ((row_id // QLEN) == (col_id // QLEN)) | (row_id * 0 + y == 1)
    mask[...] = jnp.where(together, 0.0, negative)
    vec[...] = jnp.zeros_like(vec)
    first_head = lax.broadcasted_iota(jnp.int32, (SEQ, WIDE), 1) < HEAD

    def split_heads(pair):
        zero = jnp.zeros_like(pair)
        return jnp.where(first_head, pair, zero), jnp.where(first_head, zero, pair)

    def block_rows(b, shift=0):
        return pl.ds(pl.multiple_of(b * SEQ + shift, 16), SEQ)

    def block_lanes(b):
        return pl.ds(pl.multiple_of(b * SEQ, SEQ), SEQ)

    def wide(h):
        return pl.ds(pl.multiple_of(h * WIDE, WIDE), WIDE)

    def loop(first, last, body):
        def step(i, carry):
            with jax.named_scope(body.__name__):
                body(i)
            return carry

        lax.fori_loop(first, last, step, 0)

    loads["tok"].wait()
    for k in range(small_count):
        loads[k].wait()
    for j in range(3):
        for k in range(thirds):
            loads[("wa", j, k)].wait()

    def project(b):
        at = block_rows(b)
        here = tok[at, :]
        for j in range(3):
            for k in range(thirds):
                lanes = slice(k * SEQ, (k + 1) * SEQ)
                out = dot_nn(here, red[j, k * D : (k + 1) * D, :])
                if j == 0:
                    out = (out + ab[:, lanes]) * (1.0 / math.sqrt(HEAD))
                elif j == 2:
                    out = out + ab[:, D + k * SEQ : D + (k + 1) * SEQ]
                pk[j, at, lanes] = out.astype(bf16)

    loop(0, blocks, project)

    def attend(i):
        per = PAIRS // TOGETHER
        b = i // per
        at = block_rows(b)
        pairs = [(i % per) * TOGETHER + k for k in range(TOGETHER)]
        scores = []
        for h in pairs:
            key_pair = pk[1, at, wide(h)]
            scores += [dot_nt(key_pair, query) for query in split_heads(pk[0, at, wide(h)])]
        weights = []
        scales = []
        for k, score in enumerate(scores):
            score = score + mask[...]
            peak = jnp.max(score, axis=0, keepdims=True)
            weight = jnp.exp(score - peak)
            total = jnp.sum(weight, axis=0, keepdims=True)
            lse[2 * (b * PAIRS + pairs[k // 2]) + k % 2] = peak + jnp.log(total)
            weights.append(weight.astype(bf16))
            scales.append(1.0 / total)
        for k, h in enumerate(pairs):
            value_t = pk[2, at, wide(h)].T
            mixed = [
                dot_nn(value_t[s * HEAD : (s + 1) * HEAD], weights[2 * k + s]) * scales[2 * k + s] for s in range(2)
            ]
            att_t[wide(h), block_lanes(b)] = jnp.concatenate(mixed, axis=0).astype(bf16)

    loop(0, blocks * (PAIRS // TOGETHER), attend)

    def feed_chunk(here, j):
        inner = dot_nn(here, we[:, j * D : (j + 1) * D]) + eb[:, j * D : (j + 1) * D]
        hidden, slope = gelu_both(inner)
        hidden = hidden.astype(bf16)
        return hidden, slope, dot_nn(hidden, wr[j * D : (j + 1) * D, :])

    for key in ("wm", "we", "wr"):
        loads[key].wait()
    picks = lax.broadcasted_iota(jnp.int32, (extra, rows), 1) == QLEN * lax.broadcasted_iota(
        jnp.int32, (extra, rows), 0
    )
    first_attended = dot_nt(jnp.where(picks, 1.0, 0.0).astype(bf16), att_t[...]).astype(bf16)
    for k in range(extra):
        stage32[k : k + 1, :] = tok[k * QLEN : k * QLEN + 16, :].astype(f32)[0:1, :]
    first_rows = norm_stats(stage32[0:extra, :] + (dot_nn(first_attended, wm[...]) + mb[...]))[0] * g1[...] + h1[...]
    first_low = first_rows.astype(bf16)
    leading = rb[...]
    for j in range(ffc):
        leading = leading + feed_chunk(first_low, j)[2]
    leading = norm_stats(first_rows + leading)[0] * g2[...] + h2[...]
    slot = ((c * 2 + y) * 2 + x) * nz + z
    cls[pl.ds(pl.multiple_of(slot * extra, extra), extra), :] = leading.astype(bf16)

    def gather(stage, first, count, device):
        part_of = cls.at[pl.ds(pl.multiple_of(first * extra, extra), count * extra), :]
        return remote(part_of, part_of, r.ag_send.at[stage], r.ag_recv.at[stage], device)

    pl.semaphore_wait(barrier, len(partners))
    gather_z = [gather(k, slot, 1, along[k]) for k in range(nz - 1)]
    line = ((c * 2 + y) * 2 + x) * nz
    gather_plane = [gather(nz - 1 + k, line, nz, to) for k, to in enumerate((across, other_pair, slanted))]
    gather_core = gather(nz + 2, c * 4 * nz, 4 * nz, sibling)
    for copy in gather_z:
        copy.start()

    def merge(b):
        at = block_rows(b)
        branch = dot_tn(att_t[:, block_lanes(b)], wm[...]) + mb[...]
        normed, inverse = norm_stats(tok[at, :].astype(f32) + branch)
        first = normed * g1[...] + h1[...]
        n1[at, :] = normed.astype(bf16)
        s1[at, :] = inverse
        fb[at, :] = first
        low1[at, :] = first.astype(bf16)

    loop(0, blocks, merge)


    def act_stage(b, k):
        return red.at[k, block_rows(b), :]

    def act_copies(b):
        return [
            pltpu.make_async_copy(
                act_stage(b, k),
                r.act_hbm.at[block_rows(b), pl.ds(k * SEQ, SEQ)],
                r.act_sem.at[b, k],
            )
            for k in range(thirds)
        ]

    def feed(b):
        at = block_rows(b)
        here = low1[at, :]
        total = rb[...]
        for j in range(ffc):
            hidden, slope, out = feed_chunk(here, j)
            hid[j, :, block_lanes(b)] = hidden.T
            gp[j, at, :] = slope.astype(bf16)
            total = total + out
        normed, inverse = norm_stats(fb[at, :] + total)
        final = (normed * g2[...] + h2[...]).astype(bf16)
        fb[at, :] = normed
        s2[at, :] = inverse
        for k in range(thirds):
            act_stage(b, k)[...] = final[:, k * SEQ : (k + 1) * SEQ]
        for copy in act_copies(b):
            copy.start()

    def feed_next(b):
        feed(b)

        @pl.when(b == 0)
        def _():
            for copy in gather_z:
                copy.wait()
            for copy in gather_plane:
                copy.start()

        @pl.when(b == 2)
        def _():
            for copy in gather_plane:
                copy.wait()
            gather_core.start()

    loop(0, blocks, feed_next)
    gather_core.wait()

    nq = n * extra
    spare = blocks * SEQ
    for d in range(n):
        there = ((d % 2) * 4 + (d // 2) % 2) * nz + d // 4
        for e in range(2):
            block = there + e * 2 * nz
            for k in range(thirds):
                red[k, spare + e * nq + d * extra : spare + e * nq + (d + 1) * extra, :] = cls[
                    block * extra : (block + 1) * extra, k * SEQ : (k + 1) * SEQ
                ]

    def gathered(e):
        return jnp.concatenate([red[k, spare + e * nq : spare + (e + 1) * nq, :] for k in range(thirds)], axis=1)

    question = gathered(0)
    passage = gathered(1)
    root_width = math.sqrt(D)
    match = dot_nt(passage, question) * (1.0 / root_width)
    place = lax.broadcasted_iota(jnp.int32, (nq, nq), 0)
    number = place // (PLEN // QLEN)
    real = place % (PLEN // QLEN) == 0
    listed = jnp.zeros((nq, nq), jnp.int32)
    for k in range(KPOS):
        wanted = jnp.where(r.cnt[...] > k, r.post[k : k + 1, :], -1)
        listed = jnp.where(number == wanted, 1, listed)
    listed = (listed == 1) & real
    all_scores = jnp.where(real, match, negative)
    all_peak = jnp.max(all_scores, axis=0, keepdims=True)
    all_total = jnp.sum(jnp.exp(all_scores - all_peak), axis=0, keepdims=True)
    lse_all = all_peak + jnp.log(all_total)
    live_scores = jnp.where(listed, match, negative)
    live_peak = jnp.max(live_scores, axis=0, keepdims=True)
    live_total = jnp.sum(jnp.where(listed, jnp.exp(live_scores - live_peak), 0.0), axis=0, keepdims=True)
    lse_live = live_peak + jnp.log(live_total)
    r.loss[...] = jnp.sum(lse_all - lse_live, axis=1, keepdims=True) * (1.0 / nq)
    grad_match = jnp.exp(all_scores - lse_all) - jnp.where(listed, jnp.exp(live_scores - lse_live), 0.0)
    grad_match = (loss_weight * grad_match).astype(bf16)

    @pl.when(y == 0)
    def _():
        stage32[0:nq, :] = dot_tn(grad_match, gathered(1)) * (1.0 / root_width)

    @pl.when(y == 1)
    def _():
        stage32[0:nq, :] = dot_nn(grad_match, gathered(0)) * (1.0 / root_width)

    loads["cot"].wait()

    per_block = SEQ // QLEN
    own_rows = pl.ds(pl.multiple_of(me * extra, extra), extra)
    stage32[nq : nq + extra, :] = stage32[own_rows, :]
    top_row = lax.broadcasted_iota(jnp.int32, (8, D), 0) == 0

    def second_back(b):
        at = block_rows(b)
        given = cot[at, :].astype(f32)
        pieces = []
        for k in range(per_block):
            own = stage32[pl.ds(nq + b * per_block + k, 1), :]
            pieces.append(given[k * QLEN : k * QLEN + 8] + jnp.where(top_row, own, 0.0))
            pieces.append(given[k * QLEN + 8 : (k + 1) * QLEN])
        upstream = jnp.concatenate(pieces, axis=0)
        normed = fb[at, :]
        grad = norm_back(upstream, normed, s2[at, :], g2[...])
        low = grad.astype(bf16)
        fb[at, :] = grad
        cot[at, :] = low
        vec[5 + ffc : 6 + ffc, :] += colsum_low(low)
        vec[6 + ffc : 7 + ffc, :] += colsum(upstream * normed)
        vec[7 + ffc : 8 + ffc, :] += colsum(upstream)

    loop(0, blocks, second_back)

    units = []
    unit_out = []

    def leave(ref, j, kind, at, width, out, first, pieces):
        for k in range(pieces):
            piece = width // pieces
            units.append((ref, j, part if kind else shard, kind, at, k * piece, piece))
            unit_out.append(out.at[:, pl.ds(first + k * piece, piece)])

    for k in range(thirds):
        leave(red, k, 0, k, SEQ, r.dwr_hbm, k * SEQ, PIECES[k])
    for j in range(ffc):
        leave(hid, j, 1, j, D, r.dwe_hbm, j * D, PIECES[thirds + j])
    leave(gp, 0, 1, ffc, D, r.dwm_hbm, 0, PIECES[thirds + ffc])
    for j in range(3):
        leave(gp, 1 + j, 1, ffc + 1 + j, D, r.dwa_hbm, j * D, PIECES[thirds + ffc + 1 + j])
    landing = ((r.recv_cr, r.recv_xr, r.recv_zr), (r.recv_cw, r.recv_xw, r.recv_zw))

    def unit_rows(u, first, count):
        ref, j, each, _, _, column, width = units[u]
        return ref.at[j, pl.ds(pl.multiple_of(first * each, each), count * each), pl.ds(column, width)]

    def arrived(u, stage):
        _, _, _, kind, at, column, width = units[u]
        return landing[kind][stage].at[at, :, pl.ds(column, width)]

    def add_rows(u, first, source, source_first, count):
        each = units[u][2]

        def step(i):
            here = unit_rows(u, first + i, 1)
            more = source[pl.ds(pl.multiple_of((source_first + i) * each, each), each), :]
            here[...] = (here[...].astype(f32) + more.astype(f32)).astype(bf16)

        loop(0, count, step)

    def core_copy(u):
        return remote(
            unit_rows(u, (1 - c) * (n // 2), n // 2),
            arrived(u, 0),
            r.c_send.at[u],
            r.c_recv.at[u],
            sibling,
        )

    here = c * (n // 2) + x * nz
    there = c * (n // 2) + (1 - x) * nz
    mate = z + 1 - 2 * (z % 2)
    far = 2 - 2 * (z // 2)
    outer = (z == 0) | (z == 3)
    skip = 1 - z // 2
    mate_at = {"dp": mate * 4 + x * 2 + c}
    far_at = [{"dp": (far + k) * 4 + x * 2 + c} for k in range(2)]

    def across_copy(u, k, first, count):
        return remote(
            unit_rows(u, there + first, count),
            arrived(u, 1).at[shards_of(u, first, count), :],
            r.x_send.at[u, k],
            r.x_recv.at[u, k],
            across,
        )

    def across_copies(u):
        if MODES[u] == "a":
            return [across_copy(u, 0, 0, nz)]
        return [across_copy(u, 0, far, 2), across_copy(u, 1, z, 1)]

    def shards_of(u, first, count):
        each = units[u][2]
        return pl.ds(pl.multiple_of(first * each, each), count * each)

    def line_copy(u, k, source, count, slot, device, arrival=None):
        return remote(
            unit_rows(u, source, count),
            arrived(u, 2).at[shards_of(u, slot, count), :],
            r.z_send.at[u, k],
            r.z_recv.at[u, k if arrival is None else arrival],
            device,
        )

    def end_copy(u):
        return line_copy(u, 0, here + skip, 3, 0, mate_at)

    def inner_copy(u):
        return line_copy(u, 0, here + mate, 1, 0, mate_at)

    def middle_copies(u):
        return [line_copy(u, 1 + k, here + far + k, 1, 3, far_at[k], 1) for k in range(2)]

    def early_copy(u):
        return line_copy(u, 3, there + mate, 1, 3, mate_at)

    def along_copy(u, k):
        return line_copy(u, k - 1, here + (z + k) % nz, 1, k - 1, along[k - 1])

    def out_stage(u):
        _, _, each, kind, at, column, width = units[u]
        return (stage32 if kind else r.stage_r).at[pl.ds(at * each, each), pl.ds(column, width)]

    def out_copy(u):
        return pltpu.make_async_copy(out_stage(u), unit_out[u], r.out_sem.at[u])

    @scoped
    def core_start(u):
        core_copy(u).start()

    @scoped
    def leave_core(u):
        core_copy(u).wait_recv()
        if MODES[u] == "a":
            add_rows(u, there, arrived(u, 0), (1 - x) * nz, nz)
            across_copies(u)[0].start()
        else:
            add_rows(u, there + mate, arrived(u, 0), (1 - x) * nz + mate, 1)
            early_copy(u).start()
            add_rows(u, there + far, arrived(u, 0), (1 - x) * nz + far, 2)
            across_copies(u)[0].start()
            add_rows(u, there + z, arrived(u, 0), (1 - x) * nz + z, 1)
        add_rows(u, here, arrived(u, 0), x * nz, nz)

    @scoped
    def second_step(u):
        if MODES[u] == "a":
            across_copies(u)[0].wait_recv()
            add_rows(u, here, arrived(u, 1), 0, nz)

            @pl.when(outer)
            def _():
                end_copy(u).start()

            @pl.when(jnp.logical_not(outer))
            def _():
                inner_copy(u).start()
        else:
            early_copy(u).wait_recv()
            add_rows(u, there + z, arrived(u, 2), 3, 1)
            across_copies(u)[1].start()

    @scoped
    def third_step(u):
        if MODES[u] == "a":

            @pl.when(jnp.logical_not(outer))
            def _():
                end_copy(u).wait_recv()
                add_rows(u, here + skip, arrived(u, 2), 0, 3)
                for copy in middle_copies(u):
                    copy.start()
        else:
            for copy in across_copies(u):
                copy.wait_recv()
            add_rows(u, here + far, arrived(u, 1), far, 2)
            add_rows(u, here + z, arrived(u, 1), z, 1)
            for k in range(1, nz):
                along_copy(u, k).start()

    @scoped
    def finish(u):
        def landed(slot):
            return arrived(u, 2)[shards_of(u, slot, 1), :].astype(f32)

        own = unit_rows(u, here + z, 1)
        if MODES[u] == "a":
            middle_copies(u)[0].wait_recv()
            out_stage(u)[...] = own[...].astype(f32) + landed(3)

            @pl.when(outer)
            def _():
                inner_copy(u).wait_recv()
                out_stage(u)[...] += landed(0)
        else:
            total = own[...].astype(f32)
            for k in range(1, nz):
                along_copy(u, k).wait_recv()
                total = total + landed(k - 1)
            out_stage(u)[...] = total
        out_copy(u).start()

    def vec_part(first, count):
        return vec_out.at[pl.ds(first, count)]

    mine = c * (n // 2) + x * nz
    vec_c = remote(
        vec_part((1 - c) * (n // 2), n // 2), r.vec_c, r.v_send.at[0], r.v_recv.at[0], sibling
    )
    vec_x = remote(
        vec_part(c * (n // 2) + (1 - x) * nz, nz), r.vec_x, r.v_send.at[1], r.v_recv.at[1], across
    )
    vec_z = [
        remote(
            vec_part(mine + (z + k) % nz, 1),
            r.vec_z.at[pl.ds(k - 1, 1)],
            r.v_send.at[1 + k],
            r.v_recv.at[1 + k],
            along[k - 1],
        )
        for k in range(1, nz)
    ]
    def vec_start():
        vec_c.start()

    def vec_leave_core():
        vec_c.wait()
        vec_out[pl.ds(c * (n // 2), n // 2)] += r.vec_c[...]
        vec_x.start()

    def vec_leave_plane():
        vec_x.wait()
        vec_out[pl.ds(mine, nz)] += r.vec_x[...]
        for copy in vec_z:
            copy.start()

    def vec_finish():
        for copy in vec_z:
            copy.wait()
        total = vec_out[mine + z]
        for k in range(1, nz):
            total = total + r.vec_z[k - 1]
        for e in range(2):
            r.dab[:, e * part : (e + 1) * part] = total[e : e + 1, 0:part]
        for e in range(ffc):
            r.deb[:, e * part : (e + 1) * part] = total[5 + e : 6 + e, 0:part]
        for out, row in ((r.dmb, 2), (r.dg1, 3), (r.dh1, 4), (r.drb, 5 + ffc), (r.dg2, 6 + ffc), (r.dh2, 7 + ffc)):
            out[...] = total[row : row + 1, 0:part]

    steps = (core_start, leave_core, second_step, third_step, finish)
    vec_steps = (vec_start, vec_leave_core, vec_leave_plane, vec_finish)

    def tick(name):
        for step, u in SCHEDULE.get(name, ()):
            if u == len(units):
                vec_steps[step]()
            else:
                steps[step](u)

    def ticks_at(name, count, i):
        for k in range(count):
            if name + str(k) in SCHEDULE:
                pl.when(i == k)(partial(tick, name + str(k)))

    def spot(d):
        return ((d % 2) * 2 + (d // 2) % 2) * nz + d // 4

    def spread(ref, j, result, first):
        for d in range(first, first + result.shape[0] // part):
            piece = result[(d - first) * part : (d - first + 1) * part]
            ref[j, spot(d) * part : (spot(d) + 1) * part, 0:D] = piece.astype(bf16)

    for b in range(blocks):
        for copy in act_copies(b):
            copy.wait()
    for u in range(thirds):

        def reduce_grad(i, u=u):
            left = hid[pl.ds(i * 1, 1)].reshape(1 * D, rows)
            result = dot_nn(left, cot[:, u * SEQ : (u + 1) * SEQ]).astype(bf16)
            for k in range(1 * D // shard):
                d = i * (1 * D // shard) + k
                to = pl.ds(pl.multiple_of((((k % 2) * 2 + (k // 2) % 2) * nz + d // 4) * shard, 16), shard)
                red[u, to, :] = result[k * shard : (k + 1) * shard]
            if u > 0:
                ticks_at("r%d_" % u, ffc // 1, i)

        loop(0, ffc // 1, reduce_grad)
        tick("r%d" % u)
    for j in range(ffc):

        def inner_back(b, j=j):
            at = pl.ds(pl.multiple_of(b * 2 * SEQ, 2 * SEQ), 2 * SEQ)
            grad_hidden = dot_nt(cot[at, :], wr[j * D : (j + 1) * D, :])
            low = (grad_hidden * gp[j, at, :].astype(f32)).astype(bf16)
            gp[j, at, :] = low
            vec[5 + j : 6 + j, :] += colsum(low.astype(f32))
            fb[at, :] += dot_nt(low, we[:, j * D : (j + 1) * D])

            ticks_at("i%d_" % j, blocks // 2, b)

        loop(0, blocks // 2, inner_back)
        for t in range(2):
            left = low1[:, t * half : (t + 1) * half]
            spread(hid, j, dot_tn(left, gp[j]), (n // 2) * t)
        tick("e%d" % j)
    load("wa_again", r.wa_hbm, we.at[:, pl.ds(0, 3 * D)])

    def first_back(b):
        at = block_rows(b)
        upstream = fb[at, :]
        normed = n1[at, :].astype(f32)
        grad = norm_back(upstream, normed, s1[at, :], g1[...])
        low = grad.astype(bf16)
        fb[at, :] = grad
        cot[at, :] = low
        vec[2:3, :] += colsum_low(low)
        vec[3:4, :] += colsum(upstream * normed)
        vec[4:5, :] += colsum(upstream)
        n1[at, :] = dot_nt(low, wm[...]).astype(bf16)
        ticks_at("f", blocks, b)

    loop(0, blocks, first_back)
    for t in range(2):
        spread(gp, 0, dot_nn(att_t[t * half : (t + 1) * half, :], cot[...]), (n // 2) * t)
    tick("m")

    def attend_back(i):
        per = PAIRS // BACK_TOGETHER
        b = i // per
        at = block_rows(b)
        pairs = [(i % per) * BACK_TOGETHER + k for k in range(BACK_TOGETHER)]
        queries = []
        grads = []
        scores = []
        grad_probs = []
        for h in pairs:
            queries.append(split_heads(pk[0, at, wide(h)]))
            grads.append(split_heads(n1[at, wide(h)]))
            scores += [dot_nt(pk[1, at, wide(h)], query) for query in queries[-1]]
            grad_probs += [dot_nt(pk[2, at, wide(h)], grad) for grad in grads[-1]]
        probs = []
        slopes = []
        for k in range(2 * BACK_TOGETHER):
            prob = jnp.exp(scores[k] + mask[...] - lse[2 * (b * PAIRS + pairs[k // 2]) + k % 2])
            mean = jnp.sum(prob * grad_probs[k], axis=0, keepdims=True)
            slopes.append((prob * (grad_probs[k] - mean)).astype(bf16))
            probs.append(prob.astype(bf16))
        for k, h in enumerate(pairs):
            lanes = wide(h)
            both = slice(2 * k, 2 * k + 2)
            key_t = pk[1, at, lanes].T
            grad_value = dot_nn(jnp.concatenate(probs[both], axis=1), jnp.concatenate(grads[k], axis=0)).astype(bf16)
            grad_key = dot_nn(jnp.concatenate(slopes[both], axis=1), jnp.concatenate(queries[k], axis=0)).astype(bf16)
            grad_query = [dot_nn(key_t[s * HEAD : (s + 1) * HEAD], slopes[2 * k + s]) for s in range(2)]
            grad_query = (jnp.concatenate(grad_query, axis=0) * (1.0 / math.sqrt(HEAD))).T.astype(bf16)
            pk[0, at, lanes] = grad_query
            pk[1, at, lanes] = grad_key
            pk[2, at, lanes] = grad_value
            vec[0:1, lanes] += colsum(grad_query.astype(f32))
            vec[1:2, lanes] += colsum(grad_value.astype(f32))

        ticks_at("t", blocks * per, i)

    loop(0, blocks * (PAIRS // BACK_TOGETHER), attend_back)

    for d in range(n):
        def chunk(row, first, d=d):
            at = first * part
            return vec[row + at // D : row + at // D + 1, at % D : at % D + part]

        at = spot(d)
        for e in range(2):
            vec_out[at, e : e + 1, 0:part] = chunk(0, 2 * d + e)
        for e in range(3):
            vec_out[at, 2 + e : 3 + e, 0:part] = chunk(2 + e, d)
            vec_out[at, 5 + ffc + e : 6 + ffc + e, 0:part] = chunk(5 + ffc + e, d)
        for e in range(ffc):
            vec_out[at, 5 + e : 6 + e, 0:part] = chunk(5, ffc * d + e)

    tick("v")

    for j in range(3):
        for t in range(2):
            spread(gp, 1 + j, dot_tn(tok[:, t * half : (t + 1) * half], pk[j]), (n // 2) * t)
        tick("a%d" % j)

    loads["wa_again"].wait()

    def dx_copy(b):
        return pltpu.make_async_copy(tok.at[block_rows(b), :], r.dx_hbm.at[block_rows(b), :], r.dx_sem.at[b])

    def token_grad(b):
        at = block_rows(b)
        total = fb[at, :]
        for j in range(3):
            total = total + dot_nt(pk[j, at, :], we[:, j * D : (j + 1) * D])
        tok[at, :] = total.astype(bf16)
        dx_copy(b).start()

        ticks_at("x", blocks, b)

    loop(0, blocks, token_grad)
    tick("end")
    for u in range(len(units)):
        core_copy(u).wait_send()
        for copy in across_copies(u):
            copy.wait_send()
        if MODES[u] == "a":

            @pl.when(outer)
            def _(u=u):
                end_copy(u).wait_send()

            @pl.when(jnp.logical_not(outer))
            def _(u=u):
                inner_copy(u).wait_send()
                for copy in middle_copies(u):
                    copy.wait_send()
        else:
            early_copy(u).wait_send()
            for k in range(1, nz):
                along_copy(u, k).wait_send()
        out_copy(u).wait()
    for b in range(blocks):
        dx_copy(b).wait()


def hand_over_kernel(count, *refs):
    given, wanted, held = (refs[k * count : (k + 1) * count] for k in range(3))
    sems = refs[-1]
    arriving = [pltpu.make_async_copy(given[k], held[k], sems.at[0, k]) for k in range(count)]
    leaving = [pltpu.make_async_copy(held[k], wanted[k], sems.at[1, k]) for k in range(count)]
    for copy in arriving:
        copy.start()
    for k in range(count):
        arriving[k].wait()
        leaving[k].start()
    for copy in leaving:
        copy.wait()


def fused_shards(n, *args):
    tokens, cotangent = args[0][0], args[13][0]
    rows = tokens.shape[0]
    ff = args[7].shape[2]
    ffc = ff // D
    nz = n // 4
    part = D // n
    shard = ff // n
    thirds = D // SEQ
    extra = rows // QLEN
    blocks = rows // SEQ
    wide_units = ffc + 4
    units = sum(PIECES)
    wa, wm, we, wr = (args[k][0] for k in (1, 3, 7, 9))
    small = dict(
        ab=args[2],
        mb=args[4],
        g1=args[5],
        h1=args[6],
        eb=args[8],
        rb=args[10],
        g2=args[11],
        h2=args[12],
        post=args[14].T,
        cnt=args[15][None, :],
    )
    given = dict(tok_hbm=tokens, wa_hbm=wa, wm_hbm=wm, we_hbm=we, wr_hbm=wr, cot_hbm=cotangent)
    given.update({k + "_hbm": v for k, v in small.items()})
    dma = pltpu.SemaphoreType.DMA
    scratch = dict(
        {k: pltpu.VMEM(v.shape, v.dtype) for k, v in small.items()},
        wm=pltpu.VMEM((D, D), bf16),
        we=pltpu.VMEM((D, ff), bf16),
        wr=pltpu.VMEM((ff, D), bf16),
        tok=pltpu.VMEM((rows, D), bf16),
        pk=pltpu.VMEM((3, rows, D), bf16),
        att_t=pltpu.VMEM((D, rows), bf16),
        low1=pltpu.VMEM((rows, D), bf16),
        n1=pltpu.VMEM((rows, D), bf16),
        fb=pltpu.VMEM((rows, D), f32),
        hid=pltpu.VMEM((ffc, D, rows), bf16),
        gp=pltpu.VMEM((ffc, rows, D), bf16),
        cot=pltpu.VMEM((rows, D), bf16),
        lse=pltpu.VMEM((blocks * HEADS, 1, SEQ), f32),
        s1=pltpu.VMEM((rows, 1), f32),
        s2=pltpu.VMEM((rows, 1), f32),
        mask=pltpu.VMEM((SEQ, SEQ), f32),
        red=pltpu.VMEM((thirds, ff, SEQ), bf16),
        stage_r=pltpu.VMEM((thirds * shard, SEQ), f32),
        stage32=pltpu.VMEM((wide_units * part, D), f32),
        cls=pltpu.VMEM((8 * nz * extra, D), bf16),
        vec=pltpu.VMEM((16, D), f32),
        vec_out=pltpu.VMEM((n, 16, 128), f32),
        vec_c=pltpu.VMEM((n // 2, 16, 128), f32),
        vec_x=pltpu.VMEM((nz, 16, 128), f32),
        vec_z=pltpu.VMEM((nz - 1, 16, 128), f32),
        recv_cr=pltpu.VMEM((thirds, ff // 2, SEQ), bf16),
        recv_xr=pltpu.VMEM((thirds, ff // 4, SEQ), bf16),
        recv_zr=pltpu.VMEM((thirds, nz * shard, SEQ), bf16),
        recv_cw=pltpu.VMEM((wide_units, D // 2, D), bf16),
        recv_xw=pltpu.VMEM((wide_units, D // 4, D), bf16),
        recv_zw=pltpu.VMEM((wide_units, nz * part, D), bf16),
        load_sem=dma((32,)),
        act_sem=dma((blocks, thirds)),
        dx_sem=dma((blocks,)),
        out_sem=dma((units,)),
        c_send=dma((units,)),
        c_recv=dma((units,)),
        x_send=dma((units, 2)),
        x_recv=dma((units, 2)),
        z_send=dma((units, nz)),
        z_recv=dma((units, nz)),
        ag_send=dma((nz + 3,)),
        ag_recv=dma((nz + 3,)),
        v_send=dma((nz + 1,)),
        v_recv=dma((nz + 1,)),
    )
    hbm = pl.BlockSpec(memory_space=pl.ANY)
    near = pl.BlockSpec(memory_space=pltpu.VMEM)
    shape = jax.ShapeDtypeStruct
    row_out = shape((1, part), f32)
    wanted = dict(
        act_hbm=shape((rows, D), bf16),
        loss=shape((1, 1), f32),
        dx_hbm=shape((rows, D), bf16),
        dwa_hbm=shape((part, 3 * D), f32),
        dwm_hbm=shape((part, D), f32),
        dwe_hbm=shape((part, ff), f32),
        dwr_hbm=shape((ff // n, D), f32),
        dab=shape((1, 2 * part), f32),
        dmb=row_out,
        dg1=row_out,
        dh1=row_out,
        deb=shape((1, ff // n), f32),
        drb=row_out,
        dg2=row_out,
        dh2=row_out,
    )
    shapes = list(wanted.values())
    names = list(given) + list(wanted) + list(scratch)
    outs = pl.pallas_call(
        partial(layer_kernel, n, rows, ff, names, len(small)),
        out_shape=shapes,
        in_specs=[hbm] * len(given),
        out_specs=[hbm, near] + [hbm] * 5 + [near] * 8,
        scratch_shapes=list(scratch.values()),
        compiler_params=pltpu.CompilerParams(
            collective_id=0, has_side_effects=True, vmem_limit_bytes=VMEM_BYTES
        ),
    )(*given.values())
    act, loss, dx, dwa, dwm, dwe, dwr, dab, dmb, dg1, dh1, deb, drb, dg2, dh2 = pl.pallas_call(
        partial(hand_over_kernel, len(shapes)),
        out_shape=shapes,
        in_specs=[hbm] * len(shapes),
        out_specs=[hbm] * len(shapes),
        scratch_shapes=[pltpu.VMEM(out.shape, out.dtype) for out in shapes] + [dma((2, len(shapes)))],
    )(*outs)
    return (
        act[None],
        loss[0, 0],
        dx[None],
        dwa[None],
        dab,
        dwm[None],
        dmb,
        dg1,
        dh1,
        dwe[None],
        deb,
        dwr[None],
        drb,
        dg2,
        dh2,
    )


def layer_norm(values, scale_gain, shift_row):
    centred = values - jnp.mean(values, axis=-1, keepdims=True)
    inverse = lax.rsqrt(jnp.mean(centred * centred, axis=-1, keepdims=True) + eps)
    normed = centred * inverse
    return (normed * scale_gain + shift_row, normed, inverse)


def norm_backward(upstream, normed, inverse, scale_gain):
    scaled = upstream * scale_gain
    centred = (
        scaled
        - jnp.mean(scaled, axis=-1, keepdims=True)
        - normed * jnp.mean(scaled * normed, axis=-1, keepdims=True)
    )
    return (centred * inverse, jnp.sum(upstream * normed, axis=0), jnp.sum(upstream, axis=0))


def masked_scores(query_block, key_block, same_sequence):
    raw_scores = jnp.einsum(
        "qhd,khd->hqk", query_block, key_block, preferred_element_type=jnp.float32
    ) * (1.0 / math.sqrt(HEAD))
    return jnp.where(same_sequence[None], raw_scores, negative)


def shards(
    tokens,
    attend_weight,
    attend_bias,
    merge_weight,
    merge_bias,
    first_gain,
    first_shift,
    expand_weight,
    expand_bias,
    reduce_weight,
    reduce_bias,
    second_gain,
    second_shift,
    cotangent,
    positives,
    counts,
):
    half_index = lax.axis_index("pair")
    group_index = lax.axis_index("dp")
    span_length = jnp.where(half_index == 0, QLEN, PLEN).astype(jnp.int32)
    token_rows = tokens[0]
    row_count, model_width = token_rows.shape
    block_count = row_count // BLOCK
    places = jnp.arange(BLOCK, dtype=jnp.int32) // span_length
    same_sequence = places[:, None] == places[None, :]
    zero_keys = jnp.zeros((model_width,), jnp.float32)
    full_bias = jnp.concatenate(
        [attend_bias[0, :model_width], zero_keys, attend_bias[0, model_width:]]
    )
    packed = (
        jnp.dot(token_rows, attend_weight[0], preferred_element_type=jnp.float32) + full_bias
    ).astype(jnp.bfloat16)
    heads_split = packed.reshape(block_count, BLOCK, 3, HEADS, HEAD)
    queries = heads_split[:, :, 0]
    keys_all = heads_split[:, :, 1]
    values_all = heads_split[:, :, 2]

    def attend_block(members):
        query_block, key_block, value_block = members
        scores = masked_scores(query_block, key_block, same_sequence)
        peak = jnp.max(scores, axis=-1, keepdims=True)
        totals = jnp.sum(jnp.exp(scores - peak), axis=-1, keepdims=True)
        log_total = peak + jnp.log(totals)
        probs16 = jnp.exp(scores - log_total).astype(jnp.bfloat16)
        mixed = jnp.einsum("hqk,khd->qhd", probs16, value_block, preferred_element_type=jnp.float32)
        return (mixed, log_total[..., 0])

    attended, log_totals = lax.map(attend_block, (queries, keys_all, values_all))
    attended16 = attended.reshape(row_count, model_width).astype(jnp.bfloat16)
    branch = (
        jnp.dot(attended16, merge_weight[0], preferred_element_type=jnp.float32) + merge_bias[0]
    )
    rows_float = token_rows.astype(jnp.float32)
    normed_first, first_normed, first_inverse = layer_norm(
        rows_float + branch, first_gain[0], first_shift[0]
    )
    first16 = normed_first.astype(jnp.bfloat16)
    inner_pre = (
        jnp.dot(first16, expand_weight[0], preferred_element_type=jnp.float32) + expand_bias[0]
    )
    hidden16 = jax.nn.gelu(inner_pre, approximate=False).astype(jnp.bfloat16)
    second = (
        jnp.dot(hidden16, reduce_weight[0], preferred_element_type=jnp.float32) + reduce_bias[0]
    )
    final, final_normed, final_inverse = layer_norm(
        normed_first + second, second_gain[0], second_shift[0]
    )
    question_count = row_count // QLEN
    passage_count = row_count // PLEN
    leading = final.reshape(question_count, QLEN, model_width)[:, 0].astype(jnp.bfloat16)
    every_leading = lax.all_gather(leading, ("pair", "dp"), axis=0, tiled=True)
    half_rows = every_leading.shape[0] // 2
    question_cls = every_leading[:half_rows]
    passage_cls = every_leading[half_rows:].reshape(-1, PLEN // QLEN, model_width)[:, 0]
    root_width = math.sqrt(D)
    match_scores = (
        jnp.einsum("qd,pd->qp", question_cls, passage_cls, preferred_element_type=jnp.float32)
        / root_width
    )
    row_peak = jnp.max(match_scores, axis=1, keepdims=True)
    lse_all = row_peak + jnp.log(jnp.sum(jnp.exp(match_scores - row_peak), axis=1, keepdims=True))
    picked = jnp.take_along_axis(match_scores, positives, axis=1)
    live_slots = jnp.arange(KPOS, dtype=jnp.int32)[None, :] < counts[:, None]
    live_peak = jnp.max(jnp.where(live_slots, picked, negative), axis=1, keepdims=True)
    live_total = jnp.sum(
        jnp.where(live_slots, jnp.exp(picked - live_peak), 0.0), axis=1, keepdims=True
    )
    lse_live = live_peak + jnp.log(live_total)
    loss_value = jnp.mean(lse_all[:, 0] - lse_live[:, 0])
    live_weights = jnp.where(live_slots, jnp.exp(picked - lse_live), 0.0)
    columns = jnp.arange(match_scores.shape[1], dtype=jnp.int32)[None, :]
    grad_match = jnp.exp(match_scores - lse_all)
    for slot in range(KPOS):
        grad_match = grad_match - jnp.where(
            columns == positives[:, slot : slot + 1], live_weights[:, slot : slot + 1], 0.0
        )
    grad_match16 = (loss_weight * grad_match).astype(jnp.bfloat16)
    own_questions = lax.dynamic_slice_in_dim(
        grad_match16, group_index * question_count, question_count, 0
    )
    grad_question = (
        jnp.dot(own_questions, passage_cls, preferred_element_type=jnp.float32) / root_width
    )
    own_passages = lax.dynamic_slice_in_dim(
        grad_match16, group_index * passage_count, passage_count, 1
    )
    grad_passage = (
        jnp.einsum("qp,qd->pd", own_passages, question_cls, preferred_element_type=jnp.float32)
        / root_width
    )
    spread_question = (
        jnp.zeros((question_count, QLEN, model_width), jnp.float32)
        .at[:, 0]
        .set(grad_question)
        .reshape(row_count, model_width)
    )
    spread_passage = (
        jnp.zeros((passage_count, PLEN, model_width), jnp.float32)
        .at[:, 0]
        .set(grad_passage)
        .reshape(row_count, model_width)
    )
    grad_final = cotangent[0].astype(jnp.float32) + jnp.where(
        half_index == 0, spread_question, spread_passage
    )
    grad_pair_two, second_gain_grad, second_shift_grad = norm_backward(
        grad_final, final_normed, final_inverse, second_gain[0]
    )
    grad_second16 = grad_pair_two.astype(jnp.bfloat16)
    reduce_weight_grad = jnp.einsum(
        "tf,td->fd", hidden16, grad_second16, preferred_element_type=jnp.float32
    )
    reduce_bias_grad = jnp.sum(grad_second16.astype(jnp.float32), axis=0)
    grad_hidden = jnp.einsum(
        "td,fd->tf", grad_second16, reduce_weight[0], preferred_element_type=jnp.float32
    )
    _, gelu_pullback = jax.vjp(partial(jax.nn.gelu, approximate=False), inner_pre)
    grad_inner16 = gelu_pullback(grad_hidden)[0].astype(jnp.bfloat16)
    expand_weight_grad = jnp.einsum(
        "td,tf->df", first16, grad_inner16, preferred_element_type=jnp.float32
    )
    expand_bias_grad = jnp.sum(grad_inner16.astype(jnp.float32), axis=0)
    grad_first = (
        jnp.einsum("tf,df->td", grad_inner16, expand_weight[0], preferred_element_type=jnp.float32)
        + grad_pair_two
    )
    feed_shares = (
        expand_weight_grad,
        expand_bias_grad,
        reduce_weight_grad,
        reduce_bias_grad,
        second_gain_grad,
        second_shift_grad,
    )
    grad_pair_one, first_gain_grad, first_shift_grad = norm_backward(
        grad_first, first_normed, first_inverse, first_gain[0]
    )
    grad_branch16 = grad_pair_one.astype(jnp.bfloat16)
    merge_weight_grad = jnp.einsum(
        "td,te->de", attended16, grad_branch16, preferred_element_type=jnp.float32
    )
    merge_bias_grad = jnp.sum(grad_branch16.astype(jnp.float32), axis=0)
    grad_attended16 = jnp.einsum(
        "te,de->td", grad_branch16, merge_weight[0], preferred_element_type=jnp.float32
    ).astype(jnp.bfloat16)
    grad_attended_blocks = grad_attended16.reshape(block_count, BLOCK, HEADS, HEAD)

    def attend_backward(members):
        query_block, key_block, value_block, grad_out, log_total = members
        scores = masked_scores(query_block, key_block, same_sequence)
        probs = jnp.exp(scores - log_total[..., None])
        probs16 = probs.astype(jnp.bfloat16)
        grad_value = jnp.einsum(
            "hqk,qhd->khd", probs16, grad_out, preferred_element_type=jnp.float32
        )
        grad_probs = jnp.einsum(
            "qhd,khd->hqk", grad_out, value_block, preferred_element_type=jnp.float32
        )
        grad_scores16 = (
            probs * (grad_probs - jnp.sum(probs * grad_probs, axis=-1, keepdims=True))
        ).astype(jnp.bfloat16)
        grad_query = jnp.einsum(
            "hqk,khd->qhd", grad_scores16, key_block, preferred_element_type=jnp.float32
        ) * (1.0 / math.sqrt(HEAD))
        grad_key = jnp.einsum(
            "hqk,qhd->khd", grad_scores16, query_block, preferred_element_type=jnp.float32
        ) * (1.0 / math.sqrt(HEAD))
        return (grad_query, grad_key, grad_value)

    grad_queries, grad_keys, grad_values = lax.map(
        attend_backward, (queries, keys_all, values_all, grad_attended_blocks, log_totals)
    )
    grad_packed16 = (
        jnp.stack([grad_queries, grad_keys, grad_values], axis=2)
        .reshape(row_count, 3 * model_width)
        .astype(jnp.bfloat16)
    )
    attend_weight_grad = jnp.einsum(
        "td,te->de", token_rows, grad_packed16, preferred_element_type=jnp.float32
    )
    packed_sums = jnp.sum(grad_packed16.astype(jnp.float32), axis=0)
    attend_bias_grad = jnp.concatenate([packed_sums[:model_width], packed_sums[2 * model_width :]])
    grad_rows = (
        jnp.einsum("te,de->td", grad_packed16, attend_weight[0], preferred_element_type=jnp.float32)
        + grad_pair_one
    )
    every_share = (
        lax.psum_scatter(attend_weight_grad, "dp", scatter_dimension=0, tiled=True),
        lax.psum_scatter(attend_bias_grad, "dp", scatter_dimension=0, tiled=True),
        lax.psum_scatter(merge_weight_grad, "dp", scatter_dimension=0, tiled=True),
        lax.psum_scatter(merge_bias_grad, "dp", scatter_dimension=0, tiled=True),
        lax.psum_scatter(first_gain_grad, "dp", scatter_dimension=0, tiled=True),
        lax.psum_scatter(first_shift_grad, "dp", scatter_dimension=0, tiled=True),
        lax.psum_scatter(expand_weight_grad, "dp", scatter_dimension=0, tiled=True),
        lax.psum_scatter(expand_bias_grad, "dp", scatter_dimension=0, tiled=True),
        lax.psum_scatter(reduce_weight_grad, "dp", scatter_dimension=0, tiled=True),
        lax.psum_scatter(reduce_bias_grad, "dp", scatter_dimension=0, tiled=True),
        lax.psum_scatter(second_gain_grad, "dp", scatter_dimension=0, tiled=True),
        lax.psum_scatter(second_shift_grad, "dp", scatter_dimension=0, tiled=True),
    )
    attend_shares = every_share[:6]
    feed_shares = every_share[6:]
    return (
        final.astype(jnp.bfloat16)[None],
        loss_value,
        grad_rows.astype(jnp.bfloat16)[None],
        attend_shares[0][None],
        attend_shares[1][None],
        attend_shares[2][None],
        attend_shares[3][None],
        attend_shares[4][None],
        attend_shares[5][None],
        feed_shares[0][None],
        feed_shares[1][None],
        feed_shares[2][None],
        feed_shares[3][None],
        feed_shares[4][None],
        feed_shares[5][None],
    )


def solution(mesh):
    in_specs = (
        P("pair", "dp", None),
        P("pair", None, None),
        P("pair", None),
        P("pair", None, None),
        P("pair", None),
        P("pair", None),
        P("pair", None),
        P("pair", None, None),
        P("pair", None),
        P("pair", None, None),
        P("pair", None),
        P("pair", None),
        P("pair", None),
        P("pair", "dp", None),
        P(),
        P(),
    )
    out_specs = (
        P("pair", "dp", None),
        P(),
        P("pair", "dp", None),
        P("pair", "dp", None),
        P("pair", "dp"),
        P("pair", "dp", None),
        P("pair", "dp"),
        P("pair", "dp"),
        P("pair", "dp"),
        P("pair", "dp", None),
        P("pair", "dp"),
        P("pair", "dp", None),
        P("pair", "dp"),
        P("pair", "dp"),
        P("pair", "dp"),
    )
    n = mesh.shape["dp"]
    fits = mesh.shape["pair"] == 2 and n == 4 * LINE
    body = partial(fused_shards, n) if fits else shards
    return jax.shard_map(body, mesh=mesh, in_specs=in_specs, out_specs=out_specs, check_vma=False)
```

```python
from functools import partial
import math
from types import SimpleNamespace

import jax
import jax.numpy as jnp
from jax import lax
from jax.experimental import pallas as pl
from jax.experimental.pallas import tpu as pltpu
from jax.sharding import PartitionSpec as P

D = 768
HEADS = 12
HEAD = 64
QLEN = 64
PLEN = 256
BLOCK = 512
KPOS = 4
SEQ = 256
PAIRS = HEADS // 2
WIDE = 2 * HEAD

eps = 1e-06
loss_weight = 32.0
negative = -1e30
VMEM_BYTES = 64 * 1024 * 1024
TOGETHER = 6
BACK_TOGETHER = 2
LINE = 4
PIECES = (1, 1, 1, 1, 1, 1, 1, 2, 2, 2, 2)
MODES = "cdacacacadaacac"
SCHEDULE = {
    "r0": ((0, 0),),
    "r1": ((0, 1),),
    "r2_0": ((1, 0),),
    "r2": ((0, 2), (1, 1),),
    "i0_1": ((1, 2),),
    "e0": ((0, 3),),
    "i1_1": ((2, 0), (1, 3),),
    "e1": ((0, 4),),
    "i2_1": ((1, 4),),
    "e2": ((0, 5),),
    "i3_0": ((2, 2),),
    "i3_1": ((2, 1), (1, 5),),
    "e3": ((0, 6),),
    "f0": ((2, 3),),
    "f3": ((1, 6),),
    "m": ((0, 7), (0, 8), (3, 2), (4, 0), (2, 4),),
    "t1": ((4, 1),),
    "t2": ((1, 7),),
    "t3": ((4, 3),),
    "t4": ((1, 8),),
    "t5": ((2, 5), (3, 4),),
    "t6": ((4, 2),),
    "t10": ((2, 6),),
    "v": ((0, 15), (4, 5), (2, 7),),
    "a0": ((0, 9), (0, 10), (1, 15),),
    "a1": ((0, 11), (0, 12), (2, 8), (1, 9), (2, 15), (3, 6), (1, 10), (4, 4),),
    "a2": ((0, 13), (0, 14), (1, 11), (1, 12), (4, 7),),
    "x0": ((1, 13), (3, 8), (1, 14),),
    "x1": ((2, 10),),
    "x3": ((2, 11),),
    "end": ((2, 9), (3, 15), (4, 6), (2, 12), (3, 10), (4, 8), (2, 13), (3, 11), (4, 12), (2, 14), (4, 10), (4, 9), (3, 13), (4, 11), (4, 14), (4, 13),),
}
MESH = pl.DeviceIdType.MESH
f32 = jnp.float32
bf16 = jnp.bfloat16


def dot_nn(a, b):
    return lax.dot_general(a, b, (((1,), (0,)), ((), ())), preferred_element_type=f32)


def dot_nt(a, b):
    return lax.dot_general(a, b, (((1,), (1,)), ((), ())), preferred_element_type=f32)


def dot_tn(a, b):
    return lax.dot_general(a, b, (((0,), (0,)), ((), ())), preferred_element_type=f32)


def gelu_both(v):
    below = 0.5 + 0.5 * lax.erf(v * (1.0 / math.sqrt(2.0)))
    density = jnp.exp(v * v * -0.5) * (1.0 / math.sqrt(2.0 * math.pi))
    return v * below, below + v * density


def norm_stats(values):
    centred = values - jnp.mean(values, axis=-1, keepdims=True)
    inverse = lax.rsqrt(jnp.mean(centred * centred, axis=-1, keepdims=True) + eps)
    return centred * inverse, inverse


def norm_back(upstream, normed, inverse, gain):
    scaled = upstream * gain
    return inverse * (
        scaled
        - jnp.mean(scaled, axis=-1, keepdims=True)
        - normed * jnp.mean(scaled * normed, axis=-1, keepdims=True)
    )


def scoped(f):
    def inner(*args):
        with jax.named_scope(f.__name__):
            return f(*args)

    return inner


def colsum(values):
    return jnp.sum(values, axis=0, keepdims=True)


def colsum_low(values):
    return dot_nn(jnp.ones((8, values.shape[0]), values.dtype), values)[0:1]


def layer_kernel(n, rows, ff, names, small_count, *refs):
    r = SimpleNamespace(**dict(zip(names, refs, strict=True)))
    wm, we, wr, tok, pk, att_t = r.wm, r.we, r.wr, r.tok, r.pk, r.att_t
    low1, n1, fb, hid, gp, cot = r.low1, r.n1, r.fb, r.hid, r.gp, r.cot
    lse, s1, s2, mask, red = r.lse, r.s1, r.s2, r.mask, r.red
    stage32, cls, vec, vec_out = r.stage32, r.cls, r.vec, r.vec_out
    ab, mb, g1, h1, eb, rb, g2, h2 = r.ab, r.mb, r.g1, r.h1, r.eb, r.rb, r.g2, r.h2
    small = list(zip(refs[6 : 6 + small_count], (ab, mb, g1, h1, eb, rb, g2, h2, r.post, r.cnt), strict=True))
    nz = n // 4
    part = D // n
    half = D // 2
    blocks = rows // SEQ
    ffc = ff // D
    thirds = D // SEQ
    shard = ff // n
    extra = rows // QLEN
    y = lax.axis_index("pair")
    me = lax.axis_index("dp")
    z = me // 4
    x = (me // 2) % 2
    c = me % 2

    sibling = {"dp": z * 4 + x * 2 + (1 - c)}
    across = {"dp": z * 4 + (1 - x) * 2 + c}
    other_pair = {"pair": 1 - y}
    slanted = {"pair": 1 - y, "dp": z * 4 + (1 - x) * 2 + c}
    along = [{"dp": ((z + k) % nz) * 4 + x * 2 + c} for k in range(1, nz)]
    partners = [sibling, across, other_pair, slanted] + along
    barrier = pltpu.get_barrier_semaphore()
    for partner in partners:
        pl.semaphore_signal(barrier, inc=1, device_id=partner, device_id_type=MESH)

    def remote(source, target, send, recv, device):
        return pltpu.make_async_remote_copy(
            src_ref=source,
            dst_ref=target,
            send_sem=send,
            recv_sem=recv,
            device_id=device,
            device_id_type=MESH,
        )

    loads = {}

    def load(key, source, target):
        loads[key] = pltpu.make_async_copy(source, target, r.load_sem.at[len(loads)])
        loads[key].start()

    load("tok", r.tok_hbm, tok)
    for j in range(3):
        for k in range(thirds):
            load(
                ("wa", j, k),
                r.wa_hbm.at[:, pl.ds(j * D + k * SEQ, SEQ)],
                red.at[j, pl.ds(k * D, D), :],
            )
    for k, (source, target) in enumerate(small):
        load(k, source, target)
    load("wm", r.wm_hbm, wm)
    load("we", r.we_hbm, we)
    load("wr", r.wr_hbm, wr)
    load("cot", r.cot_hbm, cot)

    row_id = lax.broadcasted_iota(jnp.int32, (SEQ, SEQ), 0)
    col_id = lax.broadcasted_iota(jnp.int32, (SEQ, SEQ), 1)
    together = ((row_id // QLEN) == (col_id // QLEN)) | (row_id * 0 + y == 1)
    mask[...] = jnp.where(together, 0.0, negative)
    vec[...] = jnp.zeros_like(vec)
    first_head = lax.broadcasted_iota(jnp.int32, (SEQ, WIDE), 1) < HEAD

    def split_heads(pair):
        zero = jnp.zeros_like(pair)
        return jnp.where(first_head, pair, zero), jnp.where(first_head, zero, pair)

    def block_rows(b, shift=0):
        return pl.ds(pl.multiple_of(b * SEQ + shift, 16), SEQ)

    def block_lanes(b):
        return pl.ds(pl.multiple_of(b * SEQ, SEQ), SEQ)

    def wide(h):
        return pl.ds(pl.multiple_of(h * WIDE, WIDE), WIDE)

    def loop(first, last, body):
        def step(i, carry):
            with jax.named_scope(body.__name__):
                body(i)
            return carry

        lax.fori_loop(first, last, step, 0)

    loads["tok"].wait()
    for k in range(small_count):
        loads[k].wait()
    for j in range(3):
        for k in range(thirds):
            loads[("wa", j, k)].wait()

    def project(b):
        at = block_rows(b)
        here = tok[at, :]
        for j in range(3):
            for k in range(thirds):
                lanes = slice(k * SEQ, (k + 1) * SEQ)
                out = dot_nn(here, red[j, k * D : (k + 1) * D, :])
                if j == 0:
                    out = (out + ab[:, lanes]) * (1.0 / math.sqrt(HEAD))
                elif j == 2:
                    out = out + ab[:, D + k * SEQ : D + (k + 1) * SEQ]
                pk[j, at, lanes] = out.astype(bf16)

    loop(0, blocks, project)

    def attend(i):
        per = PAIRS // TOGETHER
        b = i // per
        at = block_rows(b)
        pairs = [(i % per) * TOGETHER + k for k in range(TOGETHER)]
        scores = []
        for h in pairs:
            key_pair = pk[1, at, wide(h)]
            scores += [dot_nt(key_pair, query) for query in split_heads(pk[0, at, wide(h)])]
        weights = []
        scales = []
        for k, score in enumerate(scores):
            score = score + mask[...]
            peak = jnp.max(score, axis=0, keepdims=True)
            weight = jnp.exp(score - peak)
            total = jnp.sum(weight, axis=0, keepdims=True)
            lse[2 * (b * PAIRS + pairs[k // 2]) + k % 2] = peak + jnp.log(total)
            weights.append(weight.astype(bf16))
            scales.append(1.0 / total)
        for k, h in enumerate(pairs):
            value_t = pk[2, at, wide(h)].T
            mixed = [
                dot_nn(value_t[s * HEAD : (s + 1) * HEAD], weights[2 * k + s]) * scales[2 * k + s] for s in range(2)
            ]
            att_t[wide(h), block_lanes(b)] = jnp.concatenate(mixed, axis=0).astype(bf16)

    loop(0, blocks * (PAIRS // TOGETHER), attend)

    def feed_chunk(here, j):
        inner = dot_nn(here, we[:, j * D : (j + 1) * D]) + eb[:, j * D : (j + 1) * D]
        hidden, slope = gelu_both(inner)
        hidden = hidden.astype(bf16)
        return hidden, slope, dot_nn(hidden, wr[j * D : (j + 1) * D, :])

    for key in ("wm", "we", "wr"):
        loads[key].wait()
    picks = lax.broadcasted_iota(jnp.int32, (extra, rows), 1) == QLEN * lax.broadcasted_iota(
        jnp.int32, (extra, rows), 0
    )
    first_attended = dot_nt(jnp.where(picks, 1.0, 0.0).astype(bf16), att_t[...]).astype(bf16)
    for k in range(extra):
        stage32[k : k + 1, :] = tok[k * QLEN : k * QLEN + 16, :].astype(f32)[0:1, :]
    first_rows = norm_stats(stage32[0:extra, :] + (dot_nn(first_attended, wm[...]) + mb[...]))[0] * g1[...] + h1[...]
    first_low = first_rows.astype(bf16)
    leading = rb[...]
    for j in range(ffc):
        leading = leading + feed_chunk(first_low, j)[2]
    leading = norm_stats(first_rows + leading)[0] * g2[...] + h2[...]
    slot = ((c * 2 + y) * 2 + x) * nz + z
    cls[pl.ds(pl.multiple_of(slot * extra, extra), extra), :] = leading.astype(bf16)

    def gather(stage, first, count, device):
        part_of = cls.at[pl.ds(pl.multiple_of(first * extra, extra), count * extra), :]
        return remote(part_of, part_of, r.ag_send.at[stage], r.ag_recv.at[stage], device)

    pl.semaphore_wait(barrier, len(partners))
    gather_z = [gather(k, slot, 1, along[k]) for k in range(nz - 1)]
    line = ((c * 2 + y) * 2 + x) * nz
    gather_plane = [gather(nz - 1 + k, line, nz, to) for k, to in enumerate((across, other_pair, slanted))]
    gather_core = gather(nz + 2, c * 4 * nz, 4 * nz, sibling)
    for copy in gather_z:
        copy.start()

    def merge(b):
        at = block_rows(b)
        branch = dot_tn(att_t[:, block_lanes(b)], wm[...]) + mb[...]
        normed, inverse = norm_stats(tok[at, :].astype(f32) + branch)
        first = normed * g1[...] + h1[...]
        n1[at, :] = normed.astype(bf16)
        s1[at, :] = inverse
        fb[at, :] = first
        low1[at, :] = first.astype(bf16)

    loop(0, blocks, merge)


    def act_stage(b, k):
        return red.at[k, block_rows(b), :]

    def act_copies(b):
        return [
            pltpu.make_async_copy(
                act_stage(b, k),
                r.act_hbm.at[block_rows(b), pl.ds(k * SEQ, SEQ)],
                r.act_sem.at[b, k],
            )
            for k in range(thirds)
        ]

    def feed(b):
        at = block_rows(b)
        here = low1[at, :]
        total = rb[...]
        for j in range(ffc):
            hidden, slope, out = feed_chunk(here, j)
            hid[j, :, block_lanes(b)] = hidden.T
            gp[j, at, :] = slope.astype(bf16)
            total = total + out
        normed, inverse = norm_stats(fb[at, :] + total)
        final = (normed * g2[...] + h2[...]).astype(bf16)
        fb[at, :] = normed
        s2[at, :] = inverse
        for k in range(thirds):
            act_stage(b, k)[...] = final[:, k * SEQ : (k + 1) * SEQ]
        for copy in act_copies(b):
            copy.start()

    def feed_next(b):
        feed(b)

        @pl.when(b == 0)
        def _():
            for copy in gather_z:
                copy.wait()
            for copy in gather_plane:
                copy.start()

        @pl.when(b == 2)
        def _():
            for copy in gather_plane:
                copy.wait()
            gather_core.start()

    loop(0, blocks, feed_next)
    gather_core.wait()

    nq = n * extra
    spare = blocks * SEQ
    for d in range(n):
        there = ((d % 2) * 4 + (d // 2) % 2) * nz + d // 4
        for e in range(2):
            block = there + e * 2 * nz
            for k in range(thirds):
                red[k, spare + e * nq + d * extra : spare + e * nq + (d + 1) * extra, :] = cls[
                    block * extra : (block + 1) * extra, k * SEQ : (k + 1) * SEQ
                ]

    def gathered(e):
        return jnp.concatenate([red[k, spare + e * nq : spare + (e + 1) * nq, :] for k in range(thirds)], axis=1)

    question = gathered(0)
    passage = gathered(1)
    root_width = math.sqrt(D)
    match = dot_nt(passage, question) * (1.0 / root_width)
    place = lax.broadcasted_iota(jnp.int32, (nq, nq), 0)
    number = place // (PLEN // QLEN)
    real = place % (PLEN // QLEN) == 0
    listed = jnp.zeros((nq, nq), jnp.int32)
    for k in range(KPOS):
        wanted = jnp.where(r.cnt[...] > k, r.post[k : k + 1, :], -1)
        listed = jnp.where(number == wanted, 1, listed)
    listed = (listed == 1) & real
    all_scores = jnp.where(real, match, negative)
    all_peak = jnp.max(all_scores, axis=0, keepdims=True)
    all_total = jnp.sum(jnp.exp(all_scores - all_peak), axis=0, keepdims=True)
    lse_all = all_peak + jnp.log(all_total)
    live_scores = jnp.where(listed, match, negative)
    live_peak = jnp.max(live_scores, axis=0, keepdims=True)
    live_total = jnp.sum(jnp.where(listed, jnp.exp(live_scores - live_peak), 0.0), axis=0, keepdims=True)
    lse_live = live_peak + jnp.log(live_total)
    r.loss[...] = jnp.sum(lse_all - lse_live, axis=1, keepdims=True) * (1.0 / nq)
    grad_match = jnp.exp(all_scores - lse_all) - jnp.where(listed, jnp.exp(live_scores - lse_live), 0.0)
    grad_match = (loss_weight * grad_match).astype(bf16)

    @pl.when(y == 0)
    def _():
        stage32[0:nq, :] = dot_tn(grad_match, gathered(1)) * (1.0 / root_width)

    @pl.when(y == 1)
    def _():
        stage32[0:nq, :] = dot_nn(grad_match, gathered(0)) * (1.0 / root_width)

    loads["cot"].wait()

    per_block = SEQ // QLEN
    own_rows = pl.ds(pl.multiple_of(me * extra, extra), extra)
    stage32[nq : nq + extra, :] = stage32[own_rows, :]
    top_row = lax.broadcasted_iota(jnp.int32, (8, D), 0) == 0

    def second_back(b):
        at = block_rows(b)
        given = cot[at, :].astype(f32)
        pieces = []
        for k in range(per_block):
            own = stage32[pl.ds(nq + b * per_block + k, 1), :]
            pieces.append(given[k * QLEN : k * QLEN + 8] + jnp.where(top_row, own, 0.0))
            pieces.append(given[k * QLEN + 8 : (k + 1) * QLEN])
        upstream = jnp.concatenate(pieces, axis=0)
        normed = fb[at, :]
        grad = norm_back(upstream, normed, s2[at, :], g2[...])
        low = grad.astype(bf16)
        fb[at, :] = grad
        cot[at, :] = low
        vec[5 + ffc : 6 + ffc, :] += colsum_low(low)
        vec[6 + ffc : 7 + ffc, :] += colsum(upstream * normed)
        vec[7 + ffc : 8 + ffc, :] += colsum(upstream)

    loop(0, blocks, second_back)

    units = []
    unit_out = []

    def leave(ref, j, kind, at, width, out, first, pieces):
        for k in range(pieces):
            piece = width // pieces
            units.append((ref, j, part if kind else shard, kind, at, k * piece, piece))
            unit_out.append(out.at[:, pl.ds(first + k * piece, piece)])

    for k in range(thirds):
        leave(red, k, 0, k, SEQ, r.dwr_hbm, k * SEQ, PIECES[k])
    for j in range(ffc):
        leave(hid, j, 1, j, D, r.dwe_hbm, j * D, PIECES[thirds + j])
    leave(gp, 0, 1, ffc, D, r.dwm_hbm, 0, PIECES[thirds + ffc])
    for j in range(3):
        leave(gp, 1 + j, 1, ffc + 1 + j, D, r.dwa_hbm, j * D, PIECES[thirds + ffc + 1 + j])
    landing = ((r.recv_cr, r.recv_xr, r.recv_zr), (r.recv_cw, r.recv_xw, r.recv_zw))

    def unit_rows(u, first, count):
        ref, j, each, _, _, column, width = units[u]
        return ref.at[j, pl.ds(pl.multiple_of(first * each, each), count * each), pl.ds(column, width)]

    def arrived(u, stage):
        _, _, _, kind, at, column, width = units[u]
        return landing[kind][stage].at[at, :, pl.ds(column, width)]

    def add_rows(u, first, source, source_first, count):
        each = units[u][2]

        def step(i):
            here = unit_rows(u, first + i, 1)
            more = source[pl.ds(pl.multiple_of((source_first + i) * each, each), each), :]
            here[...] = (here[...].astype(f32) + more.astype(f32)).astype(bf16)

        loop(0, count, step)

    def core_copy(u):
        return remote(
            unit_rows(u, (1 - c) * (n // 2), n // 2),
            arrived(u, 0),
            r.c_send.at[u],
            r.c_recv.at[u],
            sibling,
        )

    here = c * (n // 2) + x * nz
    there = c * (n // 2) + (1 - x) * nz
    mate = z + 1 - 2 * (z % 2)
    far = 2 - 2 * (z // 2)
    outer = (z == 0) | (z == 3)
    skip = 1 - z // 2
    mate_at = {"dp": mate * 4 + x * 2 + c}
    far_at = [{"dp": (far + k) * 4 + x * 2 + c} for k in range(2)]

    def across_copy(u, k, first, count):
        return remote(
            unit_rows(u, there + first, count),
            arrived(u, 1).at[shards_of(u, first, count), :],
            r.x_send.at[u, k],
            r.x_recv.at[u, k],
            across,
        )

    def across_copies(u):
        if MODES[u] == "d":
            return [line_x_copy(u)]
        if MODES[u] != "b":
            return [across_copy(u, 0, 0, nz)]
        return [across_copy(u, 0, far, 2), across_copy(u, 1, z, 1)]

    def line_x_copy(u):
        return remote(
            unit_rows(u, there + z, 1),
            arrived(u, 2).at[shards_of(u, 3, 1), :],
            r.x_send.at[u, 3],
            r.x_recv.at[u, 3],
            across,
        )

    def line_copies(u):
        copies = []
        for k in range(1, nz):
            to = (z + k) % nz
            copies.append(along_copy(u, k))
            copies.append(
                remote(
                    unit_rows(u, there + to, 1),
                    arrived(u, 1).at[shards_of(u, k - 1, 1), :],
                    r.x_send.at[u, k - 1],
                    r.x_recv.at[u, k - 1],
                    along[k - 1],
                )
            )
        return copies

    def shards_of(u, first, count):
        each = units[u][2]
        return pl.ds(pl.multiple_of(first * each, each), count * each)

    def line_copy(u, k, source, count, slot, device, arrival=None):
        return remote(
            unit_rows(u, source, count),
            arrived(u, 2).at[shards_of(u, slot, count), :],
            r.z_send.at[u, k],
            r.z_recv.at[u, k if arrival is None else arrival],
            device,
        )

    def end_copy(u):
        return line_copy(u, 0, here + skip, 3, 0, mate_at)

    def inner_copy(u):
        return line_copy(u, 0, here + mate, 1, 0, mate_at)

    def middle_copies(u):
        return [line_copy(u, 1 + k, here + far + k, 1, 3, far_at[k], 1) for k in range(2)]


    def early_copy(u):
        return line_copy(u, 3, there + mate, 1, 3, mate_at)

    def along_copy(u, k):
        return line_copy(u, k - 1, here + (z + k) % nz, 1, k - 1, along[k - 1])

    def out_stage(u):
        _, _, each, kind, at, column, width = units[u]
        return (stage32 if kind else r.stage_r).at[pl.ds(at * each, each), pl.ds(column, width)]

    def out_copy(u):
        return pltpu.make_async_copy(out_stage(u), unit_out[u], r.out_sem.at[u])

    @scoped
    def core_start(u):
        core_copy(u).start()

    @scoped
    def leave_core(u):
        core_copy(u).wait_recv()
        if MODES[u] == "d":
            add_rows(u, c * (n // 2), arrived(u, 0), 0, n // 2)
            for copy in line_copies(u):
                copy.start()
            return
        if MODES[u] != "b":
            add_rows(u, there, arrived(u, 0), (1 - x) * nz, nz)
            across_copies(u)[0].start()
        else:
            add_rows(u, there + mate, arrived(u, 0), (1 - x) * nz + mate, 1)
            early_copy(u).start()
            add_rows(u, there + far, arrived(u, 0), (1 - x) * nz + far, 2)
            across_copies(u)[0].start()
            add_rows(u, there + z, arrived(u, 0), (1 - x) * nz + z, 1)
        add_rows(u, here, arrived(u, 0), x * nz, nz)

    @scoped
    def second_step(u):
        if MODES[u] == "a":
            across_copies(u)[0].wait_recv()
            add_rows(u, here, arrived(u, 1), 0, nz)

            @pl.when(outer)
            def _():
                end_copy(u).start()

            @pl.when(jnp.logical_not(outer))
            def _():
                inner_copy(u).start()
        elif MODES[u] == "d":
            for copy in line_copies(u):
                copy.wait_recv()
            for k in range(nz - 1):
                add_rows(u, there + z, arrived(u, 1), k, 1)
                add_rows(u, here + z, arrived(u, 2), k, 1)
            line_x_copy(u).start()
        elif MODES[u] == "c":
            across_copies(u)[0].wait_recv()
            add_rows(u, here, arrived(u, 1), 0, nz)
            for k in range(1, nz):
                along_copy(u, k).start()
        else:
            early_copy(u).wait_recv()
            add_rows(u, there + z, arrived(u, 2), 3, 1)
            across_copies(u)[1].start()

    @scoped
    def third_step(u):
        if MODES[u] == "a":

            @pl.when(jnp.logical_not(outer))
            def _():
                end_copy(u).wait_recv()
                add_rows(u, here + skip, arrived(u, 2), 0, 3)
                for copy in middle_copies(u):
                    copy.start()
        else:
            for copy in across_copies(u):
                copy.wait_recv()
            add_rows(u, here + far, arrived(u, 1), far, 2)
            add_rows(u, here + z, arrived(u, 1), z, 1)
            for k in range(1, nz):
                along_copy(u, k).start()

    @scoped
    def finish(u):
        def landed(slot):
            return arrived(u, 2)[shards_of(u, slot, 1), :].astype(f32)

        own = unit_rows(u, here + z, 1)
        if MODES[u] == "d":
            line_x_copy(u).wait_recv()
            out_stage(u)[...] = own[...].astype(f32) + landed(3)
        elif MODES[u] == "a":
            middle_copies(u)[0].wait_recv()
            out_stage(u)[...] = own[...].astype(f32) + landed(3)

            @pl.when(outer)
            def _():
                inner_copy(u).wait_recv()
                out_stage(u)[...] += landed(0)
        else:
            total = own[...].astype(f32)
            for k in range(1, nz):
                along_copy(u, k).wait_recv()
                total = total + landed(k - 1)
            out_stage(u)[...] = total
        out_copy(u).start()

    def vec_part(first, count):
        return vec_out.at[pl.ds(first, count)]

    mine = c * (n // 2) + x * nz
    vec_c = remote(
        vec_part((1 - c) * (n // 2), n // 2), r.vec_c, r.v_send.at[0], r.v_recv.at[0], sibling
    )
    vec_x = remote(
        vec_part(c * (n // 2) + (1 - x) * nz, nz), r.vec_x, r.v_send.at[1], r.v_recv.at[1], across
    )
    vec_z = [
        remote(
            vec_part(mine + (z + k) % nz, 1),
            r.vec_z.at[pl.ds(k - 1, 1)],
            r.v_send.at[1 + k],
            r.v_recv.at[1 + k],
            along[k - 1],
        )
        for k in range(1, nz)
    ]
    def vec_start():
        vec_c.start()

    def vec_leave_core():
        vec_c.wait()
        vec_out[pl.ds(c * (n // 2), n // 2)] += r.vec_c[...]
        vec_x.start()

    def vec_leave_plane():
        vec_x.wait()
        vec_out[pl.ds(mine, nz)] += r.vec_x[...]
        for copy in vec_z:
            copy.start()

    def vec_finish():
        for copy in vec_z:
            copy.wait()
        total = vec_out[mine + z]
        for k in range(1, nz):
            total = total + r.vec_z[k - 1]
        for e in range(2):
            r.dab[:, e * part : (e + 1) * part] = total[e : e + 1, 0:part]
        for e in range(ffc):
            r.deb[:, e * part : (e + 1) * part] = total[5 + e : 6 + e, 0:part]
        for out, row in ((r.dmb, 2), (r.dg1, 3), (r.dh1, 4), (r.drb, 5 + ffc), (r.dg2, 6 + ffc), (r.dh2, 7 + ffc)):
            out[...] = total[row : row + 1, 0:part]

    steps = (core_start, leave_core, second_step, third_step, finish)
    vec_steps = (vec_start, vec_leave_core, vec_leave_plane, vec_finish)

    def tick(name):
        for step, u in SCHEDULE.get(name, ()):
            if u == len(units):
                vec_steps[step]()
            else:
                steps[step](u)

    def ticks_at(name, count, i):
        for k in range(count):
            if name + str(k) in SCHEDULE:
                pl.when(i == k)(partial(tick, name + str(k)))

    def spot(d):
        return ((d % 2) * 2 + (d // 2) % 2) * nz + d // 4

    def spread(ref, j, result, first):
        for d in range(first, first + result.shape[0] // part):
            piece = result[(d - first) * part : (d - first + 1) * part]
            ref[j, spot(d) * part : (spot(d) + 1) * part, 0:D] = piece.astype(bf16)

    for b in range(blocks):
        for copy in act_copies(b):
            copy.wait()
    for u in range(thirds):

        def reduce_grad(i, u=u):
            left = hid[pl.ds(i * 1, 1)].reshape(1 * D, rows)
            result = dot_nn(left, cot[:, u * SEQ : (u + 1) * SEQ]).astype(bf16)
            for k in range(1 * D // shard):
                d = i * (1 * D // shard) + k
                to = pl.ds(pl.multiple_of((((k % 2) * 2 + (k // 2) % 2) * nz + d // 4) * shard, 16), shard)
                red[u, to, :] = result[k * shard : (k + 1) * shard]
            if u > 0:
                ticks_at("r%d_" % u, ffc // 1, i)

        loop(0, ffc // 1, reduce_grad)
        tick("r%d" % u)
    for j in range(ffc):

        def inner_back(b, j=j):
            at = pl.ds(pl.multiple_of(b * 2 * SEQ, 2 * SEQ), 2 * SEQ)
            grad_hidden = dot_nt(cot[at, :], wr[j * D : (j + 1) * D, :])
            low = (grad_hidden * gp[j, at, :].astype(f32)).astype(bf16)
            gp[j, at, :] = low
            vec[5 + j : 6 + j, :] += colsum(low.astype(f32))
            fb[at, :] += dot_nt(low, we[:, j * D : (j + 1) * D])

            ticks_at("i%d_" % j, blocks // 2, b)

        loop(0, blocks // 2, inner_back)
        for t in range(2):
            left = low1[:, t * half : (t + 1) * half]
            spread(hid, j, dot_tn(left, gp[j]), (n // 2) * t)
        tick("e%d" % j)
    load("wa_again", r.wa_hbm, we.at[:, pl.ds(0, 3 * D)])

    def first_back(b):
        at = block_rows(b)
        upstream = fb[at, :]
        normed = n1[at, :].astype(f32)
        grad = norm_back(upstream, normed, s1[at, :], g1[...])
        low = grad.astype(bf16)
        fb[at, :] = grad
        cot[at, :] = low
        vec[2:3, :] += colsum_low(low)
        vec[3:4, :] += colsum(upstream * normed)
        vec[4:5, :] += colsum(upstream)
        n1[at, :] = dot_nt(low, wm[...]).astype(bf16)
        ticks_at("f", blocks, b)

    loop(0, blocks, first_back)
    for t in range(2):
        spread(gp, 0, dot_nn(att_t[t * half : (t + 1) * half, :], cot[...]), (n // 2) * t)
    tick("m")

    def attend_back(i):
        per = PAIRS // BACK_TOGETHER
        b = i // per
        at = block_rows(b)
        pairs = [(i % per) * BACK_TOGETHER + k for k in range(BACK_TOGETHER)]
        queries = []
        grads = []
        scores = []
        grad_probs = []
        for h in pairs:
            queries.append(split_heads(pk[0, at, wide(h)]))
            grads.append(split_heads(n1[at, wide(h)]))
            scores += [dot_nt(pk[1, at, wide(h)], query) for query in queries[-1]]
            grad_probs += [dot_nt(pk[2, at, wide(h)], grad) for grad in grads[-1]]
        probs = []
        slopes = []
        for k in range(2 * BACK_TOGETHER):
            prob = jnp.exp(scores[k] + mask[...] - lse[2 * (b * PAIRS + pairs[k // 2]) + k % 2])
            mean = jnp.sum(prob * grad_probs[k], axis=0, keepdims=True)
            slopes.append((prob * (grad_probs[k] - mean)).astype(bf16))
            probs.append(prob.astype(bf16))
        for k, h in enumerate(pairs):
            lanes = wide(h)
            both = slice(2 * k, 2 * k + 2)
            key_t = pk[1, at, lanes].T
            grad_value = dot_nn(jnp.concatenate(probs[both], axis=1), jnp.concatenate(grads[k], axis=0)).astype(bf16)
            grad_key = dot_nn(jnp.concatenate(slopes[both], axis=1), jnp.concatenate(queries[k], axis=0)).astype(bf16)
            grad_query = [dot_nn(key_t[s * HEAD : (s + 1) * HEAD], slopes[2 * k + s]) for s in range(2)]
            grad_query = (jnp.concatenate(grad_query, axis=0) * (1.0 / math.sqrt(HEAD))).T.astype(bf16)
            pk[0, at, lanes] = grad_query
            pk[1, at, lanes] = grad_key
            pk[2, at, lanes] = grad_value
            vec[0:1, lanes] += colsum(grad_query.astype(f32))
            vec[1:2, lanes] += colsum(grad_value.astype(f32))

        ticks_at("t", blocks * per, i)

    loop(0, blocks * (PAIRS // BACK_TOGETHER), attend_back)

    for d in range(n):
        def chunk(row, first, d=d):
            at = first * part
            return vec[row + at // D : row + at // D + 1, at % D : at % D + part]

        at = spot(d)
        for e in range(2):
            vec_out[at, e : e + 1, 0:part] = chunk(0, 2 * d + e)
        for e in range(3):
            vec_out[at, 2 + e : 3 + e, 0:part] = chunk(2 + e, d)
            vec_out[at, 5 + ffc + e : 6 + ffc + e, 0:part] = chunk(5 + ffc + e, d)
        for e in range(ffc):
            vec_out[at, 5 + e : 6 + e, 0:part] = chunk(5, ffc * d + e)

    tick("v")

    for j in range(3):
        for t in range(2):
            spread(gp, 1 + j, dot_tn(tok[:, t * half : (t + 1) * half], pk[j]), (n // 2) * t)
        tick("a%d" % j)

    loads["wa_again"].wait()

    def dx_copy(b):
        return pltpu.make_async_copy(tok.at[block_rows(b), :], r.dx_hbm.at[block_rows(b), :], r.dx_sem.at[b])

    def token_grad(b):
        at = block_rows(b)
        total = fb[at, :]
        for j in range(3):
            total = total + dot_nt(pk[j, at, :], we[:, j * D : (j + 1) * D])
        tok[at, :] = total.astype(bf16)
        dx_copy(b).start()

        ticks_at("x", blocks, b)

    loop(0, blocks, token_grad)
    tick("end")
    for u in range(len(units)):
        core_copy(u).wait_send()
        for copy in across_copies(u):
            copy.wait_send()
        if MODES[u] == "d":
            for copy in line_copies(u):
                copy.wait_send()
        elif MODES[u] == "a":

            @pl.when(outer)
            def _(u=u):
                end_copy(u).wait_send()

            @pl.when(jnp.logical_not(outer))
            def _(u=u):
                inner_copy(u).wait_send()
                for copy in middle_copies(u):
                    copy.wait_send()
        else:
            if MODES[u] == "b":
                early_copy(u).wait_send()
            for k in range(1, nz):
                along_copy(u, k).wait_send()
        out_copy(u).wait()
    for b in range(blocks):
        dx_copy(b).wait()


def hand_over_kernel(count, *refs):
    given, wanted, held = (refs[k * count : (k + 1) * count] for k in range(3))
    sems = refs[-1]
    arriving = [pltpu.make_async_copy(given[k], held[k], sems.at[0, k]) for k in range(count)]
    leaving = [pltpu.make_async_copy(held[k], wanted[k], sems.at[1, k]) for k in range(count)]
    for copy in arriving:
        copy.start()
    for k in range(count):
        arriving[k].wait()
        leaving[k].start()
    for copy in leaving:
        copy.wait()


def fused_shards(n, *args):
    tokens, cotangent = args[0][0], args[13][0]
    rows = tokens.shape[0]
    ff = args[7].shape[2]
    ffc = ff // D
    nz = n // 4
    part = D // n
    shard = ff // n
    thirds = D // SEQ
    extra = rows // QLEN
    blocks = rows // SEQ
    wide_units = ffc + 4
    units = sum(PIECES)
    wa, wm, we, wr = (args[k][0] for k in (1, 3, 7, 9))
    small = dict(
        ab=args[2],
        mb=args[4],
        g1=args[5],
        h1=args[6],
        eb=args[8],
        rb=args[10],
        g2=args[11],
        h2=args[12],
        post=args[14].T,
        cnt=args[15][None, :],
    )
    given = dict(tok_hbm=tokens, wa_hbm=wa, wm_hbm=wm, we_hbm=we, wr_hbm=wr, cot_hbm=cotangent)
    given.update({k + "_hbm": v for k, v in small.items()})
    dma = pltpu.SemaphoreType.DMA
    scratch = dict(
        {k: pltpu.VMEM(v.shape, v.dtype) for k, v in small.items()},
        wm=pltpu.VMEM((D, D), bf16),
        we=pltpu.VMEM((D, ff), bf16),
        wr=pltpu.VMEM((ff, D), bf16),
        tok=pltpu.VMEM((rows, D), bf16),
        pk=pltpu.VMEM((3, rows, D), bf16),
        att_t=pltpu.VMEM((D, rows), bf16),
        low1=pltpu.VMEM((rows, D), bf16),
        n1=pltpu.VMEM((rows, D), bf16),
        fb=pltpu.VMEM((rows, D), f32),
        hid=pltpu.VMEM((ffc, D, rows), bf16),
        gp=pltpu.VMEM((ffc, rows, D), bf16),
        cot=pltpu.VMEM((rows, D), bf16),
        lse=pltpu.VMEM((blocks * HEADS, 1, SEQ), f32),
        s1=pltpu.VMEM((rows, 1), f32),
        s2=pltpu.VMEM((rows, 1), f32),
        mask=pltpu.VMEM((SEQ, SEQ), f32),
        red=pltpu.VMEM((thirds, ff, SEQ), bf16),
        stage_r=pltpu.VMEM((thirds * shard, SEQ), f32),
        stage32=pltpu.VMEM((wide_units * part, D), f32),
        cls=pltpu.VMEM((8 * nz * extra, D), bf16),
        vec=pltpu.VMEM((16, D), f32),
        vec_out=pltpu.VMEM((n, 16, 128), f32),
        vec_c=pltpu.VMEM((n // 2, 16, 128), f32),
        vec_x=pltpu.VMEM((nz, 16, 128), f32),
        vec_z=pltpu.VMEM((nz - 1, 16, 128), f32),
        recv_cr=pltpu.VMEM((thirds, ff // 2, SEQ), bf16),
        recv_xr=pltpu.VMEM((thirds, ff // 4, SEQ), bf16),
        recv_zr=pltpu.VMEM((thirds, nz * shard, SEQ), bf16),
        recv_cw=pltpu.VMEM((wide_units, D // 2, D), bf16),
        recv_xw=pltpu.VMEM((wide_units, D // 4, D), bf16),
        recv_zw=pltpu.VMEM((wide_units, nz * part, D), bf16),
        load_sem=dma((32,)),
        act_sem=dma((blocks, thirds)),
        dx_sem=dma((blocks,)),
        out_sem=dma((units,)),
        c_send=dma((units,)),
        c_recv=dma((units,)),
        x_send=dma((units, nz)),
        x_recv=dma((units, nz)),
        z_send=dma((units, nz)),
        z_recv=dma((units, nz)),
        ag_send=dma((nz + 3,)),
        ag_recv=dma((nz + 3,)),
        v_send=dma((nz + 1,)),
        v_recv=dma((nz + 1,)),
    )
    hbm = pl.BlockSpec(memory_space=pl.ANY)
    near = pl.BlockSpec(memory_space=pltpu.VMEM)
    shape = jax.ShapeDtypeStruct
    row_out = shape((1, part), f32)
    wanted = dict(
        act_hbm=shape((rows, D), bf16),
        loss=shape((1, 1), f32),
        dx_hbm=shape((rows, D), bf16),
        dwa_hbm=shape((part, 3 * D), f32),
        dwm_hbm=shape((part, D), f32),
        dwe_hbm=shape((part, ff), f32),
        dwr_hbm=shape((ff // n, D), f32),
        dab=shape((1, 2 * part), f32),
        dmb=row_out,
        dg1=row_out,
        dh1=row_out,
        deb=shape((1, ff // n), f32),
        drb=row_out,
        dg2=row_out,
        dh2=row_out,
    )
    shapes = list(wanted.values())
    names = list(given) + list(wanted) + list(scratch)
    outs = pl.pallas_call(
        partial(layer_kernel, n, rows, ff, names, len(small)),
        out_shape=shapes,
        in_specs=[hbm] * len(given),
        out_specs=[hbm, near] + [hbm] * 5 + [near] * 8,
        scratch_shapes=list(scratch.values()),
        compiler_params=pltpu.CompilerParams(
            collective_id=0, has_side_effects=True, vmem_limit_bytes=VMEM_BYTES
        ),
    )(*given.values())
    act, loss, dx, dwa, dwm, dwe, dwr, dab, dmb, dg1, dh1, deb, drb, dg2, dh2 = pl.pallas_call(
        partial(hand_over_kernel, len(shapes)),
        out_shape=shapes,
        in_specs=[hbm] * len(shapes),
        out_specs=[hbm] * len(shapes),
        scratch_shapes=[pltpu.VMEM(out.shape, out.dtype) for out in shapes] + [dma((2, len(shapes)))],
    )(*outs)
    return (
        act[None],
        loss[0, 0],
        dx[None],
        dwa[None],
        dab,
        dwm[None],
        dmb,
        dg1,
        dh1,
        dwe[None],
        deb,
        dwr[None],
        drb,
        dg2,
        dh2,
    )


def layer_norm(values, scale_gain, shift_row):
    centred = values - jnp.mean(values, axis=-1, keepdims=True)
    inverse = lax.rsqrt(jnp.mean(centred * centred, axis=-1, keepdims=True) + eps)
    normed = centred * inverse
    return (normed * scale_gain + shift_row, normed, inverse)


def norm_backward(upstream, normed, inverse, scale_gain):
    scaled = upstream * scale_gain
    centred = (
        scaled
        - jnp.mean(scaled, axis=-1, keepdims=True)
        - normed * jnp.mean(scaled * normed, axis=-1, keepdims=True)
    )
    return (centred * inverse, jnp.sum(upstream * normed, axis=0), jnp.sum(upstream, axis=0))


def masked_scores(query_block, key_block, same_sequence):
    raw_scores = jnp.einsum(
        "qhd,khd->hqk", query_block, key_block, preferred_element_type=jnp.float32
    ) * (1.0 / math.sqrt(HEAD))
    return jnp.where(same_sequence[None], raw_scores, negative)


def shards(
    tokens,
    attend_weight,
    attend_bias,
    merge_weight,
    merge_bias,
    first_gain,
    first_shift,
    expand_weight,
    expand_bias,
    reduce_weight,
    reduce_bias,
    second_gain,
    second_shift,
    cotangent,
    positives,
    counts,
):
    half_index = lax.axis_index("pair")
    group_index = lax.axis_index("dp")
    span_length = jnp.where(half_index == 0, QLEN, PLEN).astype(jnp.int32)
    token_rows = tokens[0]
    row_count, model_width = token_rows.shape
    block_count = row_count // BLOCK
    places = jnp.arange(BLOCK, dtype=jnp.int32) // span_length
    same_sequence = places[:, None] == places[None, :]
    zero_keys = jnp.zeros((model_width,), jnp.float32)
    full_bias = jnp.concatenate(
        [attend_bias[0, :model_width], zero_keys, attend_bias[0, model_width:]]
    )
    packed = (
        jnp.dot(token_rows, attend_weight[0], preferred_element_type=jnp.float32) + full_bias
    ).astype(jnp.bfloat16)
    heads_split = packed.reshape(block_count, BLOCK, 3, HEADS, HEAD)
    queries = heads_split[:, :, 0]
    keys_all = heads_split[:, :, 1]
    values_all = heads_split[:, :, 2]

    def attend_block(members):
        query_block, key_block, value_block = members
        scores = masked_scores(query_block, key_block, same_sequence)
        peak = jnp.max(scores, axis=-1, keepdims=True)
        totals = jnp.sum(jnp.exp(scores - peak), axis=-1, keepdims=True)
        log_total = peak + jnp.log(totals)
        probs16 = jnp.exp(scores - log_total).astype(jnp.bfloat16)
        mixed = jnp.einsum("hqk,khd->qhd", probs16, value_block, preferred_element_type=jnp.float32)
        return (mixed, log_total[..., 0])

    attended, log_totals = lax.map(attend_block, (queries, keys_all, values_all))
    attended16 = attended.reshape(row_count, model_width).astype(jnp.bfloat16)
    branch = (
        jnp.dot(attended16, merge_weight[0], preferred_element_type=jnp.float32) + merge_bias[0]
    )
    rows_float = token_rows.astype(jnp.float32)
    normed_first, first_normed, first_inverse = layer_norm(
        rows_float + branch, first_gain[0], first_shift[0]
    )
    first16 = normed_first.astype(jnp.bfloat16)
    inner_pre = (
        jnp.dot(first16, expand_weight[0], preferred_element_type=jnp.float32) + expand_bias[0]
    )
    hidden16 = jax.nn.gelu(inner_pre, approximate=False).astype(jnp.bfloat16)
    second = (
        jnp.dot(hidden16, reduce_weight[0], preferred_element_type=jnp.float32) + reduce_bias[0]
    )
    final, final_normed, final_inverse = layer_norm(
        normed_first + second, second_gain[0], second_shift[0]
    )
    question_count = row_count // QLEN
    passage_count = row_count // PLEN
    leading = final.reshape(question_count, QLEN, model_width)[:, 0].astype(jnp.bfloat16)
    every_leading = lax.all_gather(leading, ("pair", "dp"), axis=0, tiled=True)
    half_rows = every_leading.shape[0] // 2
    question_cls = every_leading[:half_rows]
    passage_cls = every_leading[half_rows:].reshape(-1, PLEN // QLEN, model_width)[:, 0]
    root_width = math.sqrt(D)
    match_scores = (
        jnp.einsum("qd,pd->qp", question_cls, passage_cls, preferred_element_type=jnp.float32)
        / root_width
    )
    row_peak = jnp.max(match_scores, axis=1, keepdims=True)
    lse_all = row_peak + jnp.log(jnp.sum(jnp.exp(match_scores - row_peak), axis=1, keepdims=True))
    picked = jnp.take_along_axis(match_scores, positives, axis=1)
    live_slots = jnp.arange(KPOS, dtype=jnp.int32)[None, :] < counts[:, None]
    live_peak = jnp.max(jnp.where(live_slots, picked, negative), axis=1, keepdims=True)
    live_total = jnp.sum(
        jnp.where(live_slots, jnp.exp(picked - live_peak), 0.0), axis=1, keepdims=True
    )
    lse_live = live_peak + jnp.log(live_total)
    loss_value = jnp.mean(lse_all[:, 0] - lse_live[:, 0])
    live_weights = jnp.where(live_slots, jnp.exp(picked - lse_live), 0.0)
    columns = jnp.arange(match_scores.shape[1], dtype=jnp.int32)[None, :]
    grad_match = jnp.exp(match_scores - lse_all)
    for slot in range(KPOS):
        grad_match = grad_match - jnp.where(
            columns == positives[:, slot : slot + 1], live_weights[:, slot : slot + 1], 0.0
        )
    grad_match16 = (loss_weight * grad_match).astype(jnp.bfloat16)
    own_questions = lax.dynamic_slice_in_dim(
        grad_match16, group_index * question_count, question_count, 0
    )
    grad_question = (
        jnp.dot(own_questions, passage_cls, preferred_element_type=jnp.float32) / root_width
    )
    own_passages = lax.dynamic_slice_in_dim(
        grad_match16, group_index * passage_count, passage_count, 1
    )
    grad_passage = (
        jnp.einsum("qp,qd->pd", own_passages, question_cls, preferred_element_type=jnp.float32)
        / root_width
    )
    spread_question = (
        jnp.zeros((question_count, QLEN, model_width), jnp.float32)
        .at[:, 0]
        .set(grad_question)
        .reshape(row_count, model_width)
    )
    spread_passage = (
        jnp.zeros((passage_count, PLEN, model_width), jnp.float32)
        .at[:, 0]
        .set(grad_passage)
        .reshape(row_count, model_width)
    )
    grad_final = cotangent[0].astype(jnp.float32) + jnp.where(
        half_index == 0, spread_question, spread_passage
    )
    grad_pair_two, second_gain_grad, second_shift_grad = norm_backward(
        grad_final, final_normed, final_inverse, second_gain[0]
    )
    grad_second16 = grad_pair_two.astype(jnp.bfloat16)
    reduce_weight_grad = jnp.einsum(
        "tf,td->fd", hidden16, grad_second16, preferred_element_type=jnp.float32
    )
    reduce_bias_grad = jnp.sum(grad_second16.astype(jnp.float32), axis=0)
    grad_hidden = jnp.einsum(
        "td,fd->tf", grad_second16, reduce_weight[0], preferred_element_type=jnp.float32
    )
    _, gelu_pullback = jax.vjp(partial(jax.nn.gelu, approximate=False), inner_pre)
    grad_inner16 = gelu_pullback(grad_hidden)[0].astype(jnp.bfloat16)
    expand_weight_grad = jnp.einsum(
        "td,tf->df", first16, grad_inner16, preferred_element_type=jnp.float32
    )
    expand_bias_grad = jnp.sum(grad_inner16.astype(jnp.float32), axis=0)
    grad_first = (
        jnp.einsum("tf,df->td", grad_inner16, expand_weight[0], preferred_element_type=jnp.float32)
        + grad_pair_two
    )
    feed_shares = (
        expand_weight_grad,
        expand_bias_grad,
        reduce_weight_grad,
        reduce_bias_grad,
        second_gain_grad,
        second_shift_grad,
    )
    grad_pair_one, first_gain_grad, first_shift_grad = norm_backward(
        grad_first, first_normed, first_inverse, first_gain[0]
    )
    grad_branch16 = grad_pair_one.astype(jnp.bfloat16)
    merge_weight_grad = jnp.einsum(
        "td,te->de", attended16, grad_branch16, preferred_element_type=jnp.float32
    )
    merge_bias_grad = jnp.sum(grad_branch16.astype(jnp.float32), axis=0)
    grad_attended16 = jnp.einsum(
        "te,de->td", grad_branch16, merge_weight[0], preferred_element_type=jnp.float32
    ).astype(jnp.bfloat16)
    grad_attended_blocks = grad_attended16.reshape(block_count, BLOCK, HEADS, HEAD)

    def attend_backward(members):
        query_block, key_block, value_block, grad_out, log_total = members
        scores = masked_scores(query_block, key_block, same_sequence)
        probs = jnp.exp(scores - log_total[..., None])
        probs16 = probs.astype(jnp.bfloat16)
        grad_value = jnp.einsum(
            "hqk,qhd->khd", probs16, grad_out, preferred_element_type=jnp.float32
        )
        grad_probs = jnp.einsum(
            "qhd,khd->hqk", grad_out, value_block, preferred_element_type=jnp.float32
        )
        grad_scores16 = (
            probs * (grad_probs - jnp.sum(probs * grad_probs, axis=-1, keepdims=True))
        ).astype(jnp.bfloat16)
        grad_query = jnp.einsum(
            "hqk,khd->qhd", grad_scores16, key_block, preferred_element_type=jnp.float32
        ) * (1.0 / math.sqrt(HEAD))
        grad_key = jnp.einsum(
            "hqk,qhd->khd", grad_scores16, query_block, preferred_element_type=jnp.float32
        ) * (1.0 / math.sqrt(HEAD))
        return (grad_query, grad_key, grad_value)

    grad_queries, grad_keys, grad_values = lax.map(
        attend_backward, (queries, keys_all, values_all, grad_attended_blocks, log_totals)
    )
    grad_packed16 = (
        jnp.stack([grad_queries, grad_keys, grad_values], axis=2)
        .reshape(row_count, 3 * model_width)
        .astype(jnp.bfloat16)
    )
    attend_weight_grad = jnp.einsum(
        "td,te->de", token_rows, grad_packed16, preferred_element_type=jnp.float32
    )
    packed_sums = jnp.sum(grad_packed16.astype(jnp.float32), axis=0)
    attend_bias_grad = jnp.concatenate([packed_sums[:model_width], packed_sums[2 * model_width :]])
    grad_rows = (
        jnp.einsum("te,de->td", grad_packed16, attend_weight[0], preferred_element_type=jnp.float32)
        + grad_pair_one
    )
    every_share = (
        lax.psum_scatter(attend_weight_grad, "dp", scatter_dimension=0, tiled=True),
        lax.psum_scatter(attend_bias_grad, "dp", scatter_dimension=0, tiled=True),
        lax.psum_scatter(merge_weight_grad, "dp", scatter_dimension=0, tiled=True),
        lax.psum_scatter(merge_bias_grad, "dp", scatter_dimension=0, tiled=True),
        lax.psum_scatter(first_gain_grad, "dp", scatter_dimension=0, tiled=True),
        lax.psum_scatter(first_shift_grad, "dp", scatter_dimension=0, tiled=True),
        lax.psum_scatter(expand_weight_grad, "dp", scatter_dimension=0, tiled=True),
        lax.psum_scatter(expand_bias_grad, "dp", scatter_dimension=0, tiled=True),
        lax.psum_scatter(reduce_weight_grad, "dp", scatter_dimension=0, tiled=True),
        lax.psum_scatter(reduce_bias_grad, "dp", scatter_dimension=0, tiled=True),
        lax.psum_scatter(second_gain_grad, "dp", scatter_dimension=0, tiled=True),
        lax.psum_scatter(second_shift_grad, "dp", scatter_dimension=0, tiled=True),
    )
    attend_shares = every_share[:6]
    feed_shares = every_share[6:]
    return (
        final.astype(jnp.bfloat16)[None],
        loss_value,
        grad_rows.astype(jnp.bfloat16)[None],
        attend_shares[0][None],
        attend_shares[1][None],
        attend_shares[2][None],
        attend_shares[3][None],
        attend_shares[4][None],
        attend_shares[5][None],
        feed_shares[0][None],
        feed_shares[1][None],
        feed_shares[2][None],
        feed_shares[3][None],
        feed_shares[4][None],
        feed_shares[5][None],
    )


def solution(mesh):
    in_specs = (
        P("pair", "dp", None),
        P("pair", None, None),
        P("pair", None),
        P("pair", None, None),
        P("pair", None),
        P("pair", None),
        P("pair", None),
        P("pair", None, None),
        P("pair", None),
        P("pair", None, None),
        P("pair", None),
        P("pair", None),
        P("pair", None),
        P("pair", "dp", None),
        P(),
        P(),
    )
    out_specs = (
        P("pair", "dp", None),
        P(),
        P("pair", "dp", None),
        P("pair", "dp", None),
        P("pair", "dp"),
        P("pair", "dp", None),
        P("pair", "dp"),
        P("pair", "dp"),
        P("pair", "dp"),
        P("pair", "dp", None),
        P("pair", "dp"),
        P("pair", "dp", None),
        P("pair", "dp"),
        P("pair", "dp"),
        P("pair", "dp"),
    )
    n = mesh.shape["dp"]
    fits = mesh.shape["pair"] == 2 and n == 4 * LINE
    body = partial(fused_shards, n) if fits else shards
    return jax.shard_map(body, mesh=mesh, in_specs=in_specs, out_specs=out_specs, check_vma=False)
```

```python
from functools import partial
import math
from types import SimpleNamespace

import jax
import jax.numpy as jnp
from jax import lax
from jax.experimental import pallas as pl
from jax.experimental.pallas import tpu as pltpu
from jax.sharding import PartitionSpec as P

D = 768
HEADS = 12
HEAD = 64
QLEN = 64
PLEN = 256
BLOCK = 512
KPOS = 4
SEQ = 256
PAIRS = HEADS // 2
WIDE = 2 * HEAD

eps = 1e-06
loss_weight = 32.0
negative = -1e30
VMEM_BYTES = 64 * 1024 * 1024
TOGETHER = 6
BACK_TOGETHER = 2
LINE = 4
PIECES = (1, 1, 1, 1, 1, 1, 1, 2, 2, 2, 2)
MODES = "cdacacacadaacac"
SCHEDULE = {
    "r0": ((0, 0),),
    "r1": ((0, 1),),
    "r2_0": ((1, 0),),
    "r2": ((0, 2), (1, 1),),
    "i0_1": ((1, 2),),
    "e0": ((0, 3),),
    "i1_1": ((2, 0), (1, 3),),
    "e1": ((0, 4),),
    "i2_1": ((1, 4),),
    "e2": ((0, 5),),
    "i3_0": ((2, 2),),
    "i3_1": ((1, 5), (2, 1),),
    "e3": ((0, 6),),
    "f1": ((2, 3),),
    "f3": ((1, 6),),
    "m": ((0, 7), (0, 8), (3, 2), (4, 0),),
    "t0": ((2, 4),),
    "t2": ((1, 7),),
    "t4": ((4, 3),),
    "t5": ((2, 5), (1, 8),),
    "t6": ((3, 4), (4, 1),),
    "t7": ((4, 2),),
    "t11": ((2, 6),),
    "v": ((0, 15), (4, 5),),
    "a0": ((0, 9), (0, 10), (2, 7), (1, 15),),
    "a1": ((0, 11), (0, 12), (1, 9), (1, 10), (4, 4), (2, 8),),
    "a2": ((0, 13), (0, 14), (2, 15), (3, 6), (1, 11), (1, 12),),
    "x0": ((1, 13), (4, 7), (1, 14),),
    "x1": ((2, 10),),
    "x3": ((2, 11),),
    "end": ((2, 9), (3, 8), (2, 12), (3, 15), (4, 6), (3, 10), (2, 13), (4, 8), (3, 11), (2, 14), (4, 9), (4, 12), (4, 10), (4, 11), (3, 13), (4, 14), (4, 13),),
}
MESH = pl.DeviceIdType.MESH
f32 = jnp.float32
bf16 = jnp.bfloat16


def dot_nn(a, b):
    return lax.dot_general(a, b, (((1,), (0,)), ((), ())), preferred_element_type=f32)


def dot_nt(a, b):
    return lax.dot_general(a, b, (((1,), (1,)), ((), ())), preferred_element_type=f32)


def dot_tn(a, b):
    return lax.dot_general(a, b, (((0,), (0,)), ((), ())), preferred_element_type=f32)


def gelu_both(v):
    below = 0.5 + 0.5 * lax.erf(v * (1.0 / math.sqrt(2.0)))
    density = jnp.exp(v * v * -0.5) * (1.0 / math.sqrt(2.0 * math.pi))
    return v * below, below + v * density


def norm_stats(values):
    centred = values - jnp.mean(values, axis=-1, keepdims=True)
    inverse = lax.rsqrt(jnp.mean(centred * centred, axis=-1, keepdims=True) + eps)
    return centred * inverse, inverse


def norm_back(upstream, normed, inverse, gain):
    scaled = upstream * gain
    return inverse * (
        scaled
        - jnp.mean(scaled, axis=-1, keepdims=True)
        - normed * jnp.mean(scaled * normed, axis=-1, keepdims=True)
    )


def scoped(f):
    def inner(*args):
        with jax.named_scope(f.__name__):
            return f(*args)

    return inner


def colsum(values):
    return jnp.sum(values, axis=0, keepdims=True)


def colsum_low(values):
    return dot_nn(jnp.ones((8, values.shape[0]), values.dtype), values)[0:1]


def layer_kernel(n, rows, ff, names, small_count, *refs):
    r = SimpleNamespace(**dict(zip(names, refs, strict=True)))
    wm, we, wr, tok, pk, att_t = r.wm, r.we, r.wr, r.tok, r.pk, r.att_t
    low1, n1, fb, hid, gp, cot = r.low1, r.n1, r.fb, r.hid, r.gp, r.cot
    lse, s1, s2, mask, red = r.lse, r.s1, r.s2, r.mask, r.red
    stage32, cls, vec, vec_out = r.stage32, r.cls, r.vec, r.vec_out
    ab, mb, g1, h1, eb, rb, g2, h2 = r.ab, r.mb, r.g1, r.h1, r.eb, r.rb, r.g2, r.h2
    small = list(zip(refs[6 : 6 + small_count], (ab, mb, g1, h1, eb, rb, g2, h2, r.post, r.cnt), strict=True))
    nz = n // 4
    part = D // n
    half = D // 2
    blocks = rows // SEQ
    ffc = ff // D
    thirds = D // SEQ
    shard = ff // n
    extra = rows // QLEN
    y = lax.axis_index("pair")
    me = lax.axis_index("dp")
    z = me // 4
    x = (me // 2) % 2
    c = me % 2

    sibling = {"dp": z * 4 + x * 2 + (1 - c)}
    across = {"dp": z * 4 + (1 - x) * 2 + c}
    other_pair = {"pair": 1 - y}
    slanted = {"pair": 1 - y, "dp": z * 4 + (1 - x) * 2 + c}
    along = [{"dp": ((z + k) % nz) * 4 + x * 2 + c} for k in range(1, nz)]
    partners = [sibling, across, other_pair, slanted] + along
    barrier = pltpu.get_barrier_semaphore()
    for partner in partners:
        pl.semaphore_signal(barrier, inc=1, device_id=partner, device_id_type=MESH)

    def remote(source, target, send, recv, device):
        return pltpu.make_async_remote_copy(
            src_ref=source,
            dst_ref=target,
            send_sem=send,
            recv_sem=recv,
            device_id=device,
            device_id_type=MESH,
        )

    loads = {}

    def load(key, source, target):
        loads[key] = pltpu.make_async_copy(source, target, r.load_sem.at[len(loads)])
        loads[key].start()

    load("tok", r.tok_hbm, tok)
    for j in range(3):
        for k in range(thirds):
            load(
                ("wa", j, k),
                r.wa_hbm.at[:, pl.ds(j * D + k * SEQ, SEQ)],
                red.at[j, pl.ds(k * D, D), :],
            )
    for k, (source, target) in enumerate(small):
        load(k, source, target)
    load("wm", r.wm_hbm, wm)
    load("we", r.we_hbm, we)
    load("wr", r.wr_hbm, wr)
    load("cot", r.cot_hbm, cot)

    row_id = lax.broadcasted_iota(jnp.int32, (SEQ, SEQ), 0)
    col_id = lax.broadcasted_iota(jnp.int32, (SEQ, SEQ), 1)
    together = ((row_id // QLEN) == (col_id // QLEN)) | (row_id * 0 + y == 1)
    mask[...] = jnp.where(together, 0.0, negative)
    vec[...] = jnp.zeros_like(vec)
    first_head = lax.broadcasted_iota(jnp.int32, (SEQ, WIDE), 1) < HEAD

    def split_heads(pair):
        zero = jnp.zeros_like(pair)
        return jnp.where(first_head, pair, zero), jnp.where(first_head, zero, pair)

    def block_rows(b, shift=0):
        return pl.ds(pl.multiple_of(b * SEQ + shift, 16), SEQ)

    def block_lanes(b):
        return pl.ds(pl.multiple_of(b * SEQ, SEQ), SEQ)

    def wide(h):
        return pl.ds(pl.multiple_of(h * WIDE, WIDE), WIDE)

    def loop(first, last, body):
        def step(i, carry):
            with jax.named_scope(body.__name__):
                body(i)
            return carry

        lax.fori_loop(first, last, step, 0)

    loads["tok"].wait()
    for k in range(small_count):
        loads[k].wait()
    for j in range(3):
        for k in range(thirds):
            loads[("wa", j, k)].wait()

    def project(b):
        at = block_rows(b)
        here = tok[at, :]
        for j in range(3):
            for k in range(thirds):
                lanes = slice(k * SEQ, (k + 1) * SEQ)
                out = dot_nn(here, red[j, k * D : (k + 1) * D, :])
                if j == 0:
                    out = (out + ab[:, lanes]) * (1.0 / math.sqrt(HEAD))
                elif j == 2:
                    out = out + ab[:, D + k * SEQ : D + (k + 1) * SEQ]
                pk[j, at, lanes] = out.astype(bf16)

    loop(0, blocks, project)

    def attend(i):
        per = PAIRS // TOGETHER
        b = i // per
        at = block_rows(b)
        pairs = [(i % per) * TOGETHER + k for k in range(TOGETHER)]
        scores = []
        for h in pairs:
            key_pair = pk[1, at, wide(h)]
            scores += [dot_nt(key_pair, query) for query in split_heads(pk[0, at, wide(h)])]
        weights = []
        scales = []
        for k, score in enumerate(scores):
            score = score + mask[...]
            peak = jnp.max(score, axis=0, keepdims=True)
            weight = jnp.exp(score - peak)
            total = jnp.sum(weight, axis=0, keepdims=True)
            lse[2 * (b * PAIRS + pairs[k // 2]) + k % 2] = peak + jnp.log(total)
            weights.append(weight.astype(bf16))
            scales.append(1.0 / total)
        for k, h in enumerate(pairs):
            value_t = pk[2, at, wide(h)].T
            mixed = [
                dot_nn(value_t[s * HEAD : (s + 1) * HEAD], weights[2 * k + s]) * scales[2 * k + s] for s in range(2)
            ]
            att_t[wide(h), block_lanes(b)] = jnp.concatenate(mixed, axis=0).astype(bf16)

    loop(0, blocks * (PAIRS // TOGETHER), attend)

    def feed_chunk(here, j):
        inner = dot_nn(here, we[:, j * D : (j + 1) * D]) + eb[:, j * D : (j + 1) * D]
        hidden, slope = gelu_both(inner)
        hidden = hidden.astype(bf16)
        return hidden, slope, dot_nn(hidden, wr[j * D : (j + 1) * D, :])

    for key in ("wm", "we", "wr"):
        loads[key].wait()
    picks = lax.broadcasted_iota(jnp.int32, (extra, rows), 1) == QLEN * lax.broadcasted_iota(
        jnp.int32, (extra, rows), 0
    )
    first_attended = dot_nt(jnp.where(picks, 1.0, 0.0).astype(bf16), att_t[...]).astype(bf16)
    for k in range(extra):
        stage32[k : k + 1, :] = tok[k * QLEN : k * QLEN + 16, :].astype(f32)[0:1, :]
    first_rows = norm_stats(stage32[0:extra, :] + (dot_nn(first_attended, wm[...]) + mb[...]))[0] * g1[...] + h1[...]
    first_low = first_rows.astype(bf16)
    leading = rb[...]
    for j in range(ffc):
        leading = leading + feed_chunk(first_low, j)[2]
    leading = norm_stats(first_rows + leading)[0] * g2[...] + h2[...]
    slot = ((c * 2 + y) * 2 + x) * nz + z
    cls[pl.ds(pl.multiple_of(slot * extra, extra), extra), :] = leading.astype(bf16)

    def gather(stage, first, count, device):
        part_of = cls.at[pl.ds(pl.multiple_of(first * extra, extra), count * extra), :]
        return remote(part_of, part_of, r.ag_send.at[stage], r.ag_recv.at[stage], device)

    pl.semaphore_wait(barrier, len(partners))
    gather_z = [gather(k, slot, 1, along[k]) for k in range(nz - 1)]
    line = ((c * 2 + y) * 2 + x) * nz
    gather_plane = [gather(nz - 1 + k, line, nz, to) for k, to in enumerate((across, other_pair, slanted))]
    gather_core = gather(nz + 2, c * 4 * nz, 4 * nz, sibling)
    for copy in gather_z:
        copy.start()

    def merge(b):
        at = block_rows(b)
        branch = dot_tn(att_t[:, block_lanes(b)], wm[...]) + mb[...]
        normed, inverse = norm_stats(tok[at, :].astype(f32) + branch)
        first = normed * g1[...] + h1[...]
        n1[at, :] = normed.astype(bf16)
        s1[at, :] = inverse
        fb[at, :] = first
        low1[at, :] = first.astype(bf16)

    loop(0, blocks, merge)


    def act_stage(b, k):
        return red.at[k, block_rows(b), :]

    def act_copies(b):
        return [
            pltpu.make_async_copy(
                act_stage(b, k),
                r.act_hbm.at[block_rows(b), pl.ds(k * SEQ, SEQ)],
                r.act_sem.at[b, k],
            )
            for k in range(thirds)
        ]

    def feed(b):
        at = block_rows(b)
        here = low1[at, :]
        total = rb[...]
        for j in range(ffc):
            hidden, slope, out = feed_chunk(here, j)
            hid[j, :, block_lanes(b)] = hidden.T
            gp[j, at, :] = slope.astype(bf16)
            total = total + out
        normed, inverse = norm_stats(fb[at, :] + total)
        final = (normed * g2[...] + h2[...]).astype(bf16)
        fb[at, :] = normed
        s2[at, :] = inverse
        for k in range(thirds):
            act_stage(b, k)[...] = final[:, k * SEQ : (k + 1) * SEQ]
        for copy in act_copies(b):
            copy.start()

    def feed_next(b):
        feed(b)

        @pl.when(b == 0)
        def _():
            for copy in gather_z:
                copy.wait()
            for copy in gather_plane:
                copy.start()

        @pl.when(b == 2)
        def _():
            for copy in gather_plane:
                copy.wait()
            gather_core.start()

    loop(0, blocks, feed_next)
    gather_core.wait()

    nq = n * extra
    spare = blocks * SEQ
    for d in range(n):
        there = ((d % 2) * 4 + (d // 2) % 2) * nz + d // 4
        for e in range(2):
            block = there + e * 2 * nz
            for k in range(thirds):
                red[k, spare + e * nq + d * extra : spare + e * nq + (d + 1) * extra, :] = cls[
                    block * extra : (block + 1) * extra, k * SEQ : (k + 1) * SEQ
                ]

    def gathered(e):
        return jnp.concatenate([red[k, spare + e * nq : spare + (e + 1) * nq, :] for k in range(thirds)], axis=1)

    question = gathered(0)
    passage = gathered(1)
    root_width = math.sqrt(D)
    match = dot_nt(passage, question) * (1.0 / root_width)
    place = lax.broadcasted_iota(jnp.int32, (nq, nq), 0)
    number = place // (PLEN // QLEN)
    real = place % (PLEN // QLEN) == 0
    listed = jnp.zeros((nq, nq), jnp.int32)
    for k in range(KPOS):
        wanted = jnp.where(r.cnt[...] > k, r.post[k : k + 1, :], -1)
        listed = jnp.where(number == wanted, 1, listed)
    listed = (listed == 1) & real
    all_scores = jnp.where(real, match, negative)
    all_peak = jnp.max(all_scores, axis=0, keepdims=True)
    all_total = jnp.sum(jnp.exp(all_scores - all_peak), axis=0, keepdims=True)
    lse_all = all_peak + jnp.log(all_total)
    live_scores = jnp.where(listed, match, negative)
    live_peak = jnp.max(live_scores, axis=0, keepdims=True)
    live_total = jnp.sum(jnp.where(listed, jnp.exp(live_scores - live_peak), 0.0), axis=0, keepdims=True)
    lse_live = live_peak + jnp.log(live_total)
    r.loss[...] = jnp.sum(lse_all - lse_live, axis=1, keepdims=True) * (1.0 / nq)
    grad_match = jnp.exp(all_scores - lse_all) - jnp.where(listed, jnp.exp(live_scores - lse_live), 0.0)
    grad_match = (loss_weight * grad_match).astype(bf16)

    @pl.when(y == 0)
    def _():
        stage32[0:nq, :] = dot_tn(grad_match, gathered(1)) * (1.0 / root_width)

    @pl.when(y == 1)
    def _():
        stage32[0:nq, :] = dot_nn(grad_match, gathered(0)) * (1.0 / root_width)

    loads["cot"].wait()

    per_block = SEQ // QLEN
    own_rows = pl.ds(pl.multiple_of(me * extra, extra), extra)
    stage32[nq : nq + extra, :] = stage32[own_rows, :]
    top_row = lax.broadcasted_iota(jnp.int32, (8, D), 0) == 0

    def second_back(b):
        at = block_rows(b)
        given = cot[at, :].astype(f32)
        pieces = []
        for k in range(per_block):
            own = stage32[pl.ds(nq + b * per_block + k, 1), :]
            pieces.append(given[k * QLEN : k * QLEN + 8] + jnp.where(top_row, own, 0.0))
            pieces.append(given[k * QLEN + 8 : (k + 1) * QLEN])
        upstream = jnp.concatenate(pieces, axis=0)
        normed = fb[at, :]
        grad = norm_back(upstream, normed, s2[at, :], g2[...])
        low = grad.astype(bf16)
        fb[at, :] = grad
        cot[at, :] = low
        vec[5 + ffc : 6 + ffc, :] += colsum_low(low)
        vec[6 + ffc : 7 + ffc, :] += colsum(upstream * normed)
        vec[7 + ffc : 8 + ffc, :] += colsum(upstream)

    loop(0, blocks, second_back)

    units = []
    unit_out = []

    def leave(ref, j, kind, at, width, out, first, pieces):
        for k in range(pieces):
            piece = width // pieces
            units.append((ref, j, part if kind else shard, kind, at, k * piece, piece))
            unit_out.append(out.at[:, pl.ds(first + k * piece, piece)])

    for k in range(thirds):
        leave(red, k, 0, k, SEQ, r.dwr_hbm, k * SEQ, PIECES[k])
    for j in range(ffc):
        leave(hid, j, 1, j, D, r.dwe_hbm, j * D, PIECES[thirds + j])
    leave(gp, 0, 1, ffc, D, r.dwm_hbm, 0, PIECES[thirds + ffc])
    for j in range(3):
        leave(gp, 1 + j, 1, ffc + 1 + j, D, r.dwa_hbm, j * D, PIECES[thirds + ffc + 1 + j])
    landing = ((r.recv_cr, r.recv_xr, r.recv_zr), (r.recv_cw, r.recv_xw, r.recv_zw))

    def unit_rows(u, first, count):
        ref, j, each, _, _, column, width = units[u]
        return ref.at[j, pl.ds(pl.multiple_of(first * each, each), count * each), pl.ds(column, width)]

    def arrived(u, stage):
        _, _, _, kind, at, column, width = units[u]
        return landing[kind][stage].at[at, :, pl.ds(column, width)]

    def add_rows(u, first, source, source_first, count):
        each = units[u][2]

        def step(i):
            here = unit_rows(u, first + i, 1)
            more = source[pl.ds(pl.multiple_of((source_first + i) * each, each), each), :]
            here[...] = (here[...].astype(f32) + more.astype(f32)).astype(bf16)

        loop(0, count, step)

    def core_copy(u):
        return remote(
            unit_rows(u, (1 - c) * (n // 2), n // 2),
            arrived(u, 0),
            r.c_send.at[u],
            r.c_recv.at[u],
            sibling,
        )

    here = c * (n // 2) + x * nz
    there = c * (n // 2) + (1 - x) * nz
    mate = z + 1 - 2 * (z % 2)
    far = 2 - 2 * (z // 2)
    outer = (z == 0) | (z == 3)
    skip = 1 - z // 2
    mate_at = {"dp": mate * 4 + x * 2 + c}
    far_at = [{"dp": (far + k) * 4 + x * 2 + c} for k in range(2)]

    def across_copy(u, k, first, count):
        return remote(
            unit_rows(u, there + first, count),
            arrived(u, 1).at[shards_of(u, first, count), :],
            r.x_send.at[u, k],
            r.x_recv.at[u, k],
            across,
        )

    def across_copies(u):
        if MODES[u] == "d":
            return [line_x_copy(u)]
        if MODES[u] != "b":
            return [across_copy(u, 0, 0, nz)]
        return [across_copy(u, 0, far, 2), across_copy(u, 1, z, 1)]

    def line_x_copy(u):
        return remote(
            unit_rows(u, there + z, 1),
            arrived(u, 2).at[shards_of(u, 3, 1), :],
            r.x_send.at[u, 3],
            r.x_recv.at[u, 3],
            across,
        )

    def line_copies(u):
        copies = []
        for k in range(1, nz):
            to = (z + k) % nz
            copies.append(along_copy(u, k))
            copies.append(
                remote(
                    unit_rows(u, there + to, 1),
                    arrived(u, 1).at[shards_of(u, k - 1, 1), :],
                    r.x_send.at[u, k - 1],
                    r.x_recv.at[u, k - 1],
                    along[k - 1],
                )
            )
        return copies

    def shards_of(u, first, count):
        each = units[u][2]
        return pl.ds(pl.multiple_of(first * each, each), count * each)

    def line_copy(u, k, source, count, slot, device, arrival=None):
        return remote(
            unit_rows(u, source, count),
            arrived(u, 2).at[shards_of(u, slot, count), :],
            r.z_send.at[u, k],
            r.z_recv.at[u, k if arrival is None else arrival],
            device,
        )

    def end_copy(u):
        return line_copy(u, 0, here + skip, 3, 0, mate_at)

    def inner_copy(u):
        return line_copy(u, 0, here + mate, 1, 0, mate_at)

    def middle_copies(u):
        return [line_copy(u, 1 + k, here + far + k, 1, 3, far_at[k], 1) for k in range(2)]


    def early_copy(u):
        return line_copy(u, 3, there + mate, 1, 3, mate_at)

    def along_copy(u, k):
        return line_copy(u, k - 1, here + (z + k) % nz, 1, k - 1, along[k - 1])

    def out_stage(u):
        _, _, each, kind, at, column, width = units[u]
        return (stage32 if kind else r.stage_r).at[pl.ds(at * each, each), pl.ds(column, width)]

    def out_copy(u):
        return pltpu.make_async_copy(out_stage(u), unit_out[u], r.out_sem.at[u])

    @scoped
    def core_start(u):
        core_copy(u).start()

    @scoped
    def leave_core(u):
        core_copy(u).wait_recv()
        if MODES[u] == "d":
            add_rows(u, c * (n // 2), arrived(u, 0), 0, n // 2)
            for copy in line_copies(u):
                copy.start()
            return
        if MODES[u] != "b":
            add_rows(u, there, arrived(u, 0), (1 - x) * nz, nz)
            across_copies(u)[0].start()
        else:
            add_rows(u, there + mate, arrived(u, 0), (1 - x) * nz + mate, 1)
            early_copy(u).start()
            add_rows(u, there + far, arrived(u, 0), (1 - x) * nz + far, 2)
            across_copies(u)[0].start()
            add_rows(u, there + z, arrived(u, 0), (1 - x) * nz + z, 1)
        add_rows(u, here, arrived(u, 0), x * nz, nz)

    @scoped
    def second_step(u):
        if MODES[u] == "a":
            across_copies(u)[0].wait_recv()
            add_rows(u, here, arrived(u, 1), 0, nz)

            @pl.when(outer)
            def _():
                end_copy(u).start()

            @pl.when(jnp.logical_not(outer))
            def _():
                inner_copy(u).start()
        elif MODES[u] == "d":
            for copy in line_copies(u):
                copy.wait_recv()
            for k in range(nz - 1):
                add_rows(u, there + z, arrived(u, 1), k, 1)
                add_rows(u, here + z, arrived(u, 2), k, 1)
            line_x_copy(u).start()
        elif MODES[u] == "c":
            across_copies(u)[0].wait_recv()
            add_rows(u, here, arrived(u, 1), 0, nz)
            for k in range(1, nz):
                along_copy(u, k).start()
        else:
            early_copy(u).wait_recv()
            add_rows(u, there + z, arrived(u, 2), 3, 1)
            across_copies(u)[1].start()

    @scoped
    def third_step(u):
        if MODES[u] == "a":

            @pl.when(jnp.logical_not(outer))
            def _():
                end_copy(u).wait_recv()
                add_rows(u, here + skip, arrived(u, 2), 0, 3)
                for copy in middle_copies(u):
                    copy.start()
        else:
            for copy in across_copies(u):
                copy.wait_recv()
            add_rows(u, here + far, arrived(u, 1), far, 2)
            add_rows(u, here + z, arrived(u, 1), z, 1)
            for k in range(1, nz):
                along_copy(u, k).start()

    @scoped
    def finish(u):
        def landed(slot):
            return arrived(u, 2)[shards_of(u, slot, 1), :].astype(f32)

        own = unit_rows(u, here + z, 1)
        if MODES[u] == "d":
            line_x_copy(u).wait_recv()
            out_stage(u)[...] = own[...].astype(f32) + landed(3)
        elif MODES[u] == "a":
            middle_copies(u)[0].wait_recv()
            out_stage(u)[...] = own[...].astype(f32) + landed(3)

            @pl.when(outer)
            def _():
                inner_copy(u).wait_recv()
                out_stage(u)[...] += landed(0)
        else:
            total = own[...].astype(f32)
            for k in range(1, nz):
                along_copy(u, k).wait_recv()
                total = total + landed(k - 1)
            out_stage(u)[...] = total
        out_copy(u).start()

    def vec_part(first, count):
        return vec_out.at[pl.ds(first, count)]

    mine = c * (n // 2) + x * nz
    vec_c = remote(
        vec_part((1 - c) * (n // 2), n // 2), r.vec_c, r.v_send.at[0], r.v_recv.at[0], sibling
    )
    vec_x = remote(
        vec_part(c * (n // 2) + (1 - x) * nz, nz), r.vec_x, r.v_send.at[1], r.v_recv.at[1], across
    )
    vec_z = [
        remote(
            vec_part(mine + (z + k) % nz, 1),
            r.vec_z.at[pl.ds(k - 1, 1)],
            r.v_send.at[1 + k],
            r.v_recv.at[1 + k],
            along[k - 1],
        )
        for k in range(1, nz)
    ]
    def vec_start():
        vec_c.start()

    def vec_leave_core():
        vec_c.wait()
        vec_out[pl.ds(c * (n // 2), n // 2)] += r.vec_c[...]
        vec_x.start()

    def vec_leave_plane():
        vec_x.wait()
        vec_out[pl.ds(mine, nz)] += r.vec_x[...]
        for copy in vec_z:
            copy.start()

    def vec_finish():
        for copy in vec_z:
            copy.wait()
        total = vec_out[mine + z]
        for k in range(1, nz):
            total = total + r.vec_z[k - 1]
        for e in range(2):
            r.dab[:, e * part : (e + 1) * part] = total[e : e + 1, 0:part]
        for e in range(ffc):
            r.deb[:, e * part : (e + 1) * part] = total[5 + e : 6 + e, 0:part]
        for out, row in ((r.dmb, 2), (r.dg1, 3), (r.dh1, 4), (r.drb, 5 + ffc), (r.dg2, 6 + ffc), (r.dh2, 7 + ffc)):
            out[...] = total[row : row + 1, 0:part]

    steps = (core_start, leave_core, second_step, third_step, finish)
    vec_steps = (vec_start, vec_leave_core, vec_leave_plane, vec_finish)

    def tick(name):
        for step, u in SCHEDULE.get(name, ()):
            if u == len(units):
                vec_steps[step]()
            else:
                steps[step](u)

    def ticks_at(name, count, i):
        for k in range(count):
            if name + str(k) in SCHEDULE:
                pl.when(i == k)(partial(tick, name + str(k)))

    def spot(d):
        return ((d % 2) * 2 + (d // 2) % 2) * nz + d // 4

    def spread(ref, j, result, first):
        for d in range(first, first + result.shape[0] // part):
            piece = result[(d - first) * part : (d - first + 1) * part]
            ref[j, spot(d) * part : (spot(d) + 1) * part, 0:D] = piece.astype(bf16)

    for b in range(blocks):
        for copy in act_copies(b):
            copy.wait()
    for u in range(thirds):

        def reduce_grad(i, u=u):
            left = hid[pl.ds(i * 1, 1)].reshape(1 * D, rows)
            result = dot_nn(left, cot[:, u * SEQ : (u + 1) * SEQ]).astype(bf16)
            for k in range(1 * D // shard):
                d = i * (1 * D // shard) + k
                to = pl.ds(pl.multiple_of((((k % 2) * 2 + (k // 2) % 2) * nz + d // 4) * shard, 16), shard)
                red[u, to, :] = result[k * shard : (k + 1) * shard]
            if u > 0:
                ticks_at("r%d_" % u, ffc // 1, i)

        loop(0, ffc // 1, reduce_grad)
        tick("r%d" % u)
    for j in range(ffc):

        def inner_back(b, j=j):
            at = pl.ds(pl.multiple_of(b * 2 * SEQ, 2 * SEQ), 2 * SEQ)
            grad_hidden = dot_nt(cot[at, :], wr[j * D : (j + 1) * D, :])
            low = (grad_hidden * gp[j, at, :].astype(f32)).astype(bf16)
            gp[j, at, :] = low
            vec[5 + j : 6 + j, :] += colsum(low.astype(f32))
            fb[at, :] += dot_nt(low, we[:, j * D : (j + 1) * D])

            ticks_at("i%d_" % j, blocks // 2, b)

        loop(0, blocks // 2, inner_back)
        for t in range(2):
            left = low1[:, t * half : (t + 1) * half]
            spread(hid, j, dot_tn(left, gp[j]), (n // 2) * t)
        tick("e%d" % j)
    load("wa_again", r.wa_hbm, we.at[:, pl.ds(0, 3 * D)])

    def first_back(b):
        at = block_rows(b)
        upstream = fb[at, :]
        normed = n1[at, :].astype(f32)
        grad = norm_back(upstream, normed, s1[at, :], g1[...])
        low = grad.astype(bf16)
        fb[at, :] = grad
        cot[at, :] = low
        vec[2:3, :] += colsum_low(low)
        vec[3:4, :] += colsum(upstream * normed)
        vec[4:5, :] += colsum(upstream)
        n1[at, :] = dot_nt(low, wm[...]).astype(bf16)
        ticks_at("f", blocks, b)

    loop(0, blocks, first_back)
    for t in range(2):
        spread(gp, 0, dot_nn(att_t[t * half : (t + 1) * half, :], cot[...]), (n // 2) * t)
    tick("m")

    def attend_back(i):
        per = PAIRS // BACK_TOGETHER
        b = i // per
        at = block_rows(b)
        pairs = [(i % per) * BACK_TOGETHER + k for k in range(BACK_TOGETHER)]
        queries = []
        grads = []
        scores = []
        grad_probs = []
        for h in pairs:
            queries.append(split_heads(pk[0, at, wide(h)]))
            grads.append(split_heads(n1[at, wide(h)]))
            scores += [dot_nt(pk[1, at, wide(h)], query) for query in queries[-1]]
            grad_probs += [dot_nt(pk[2, at, wide(h)], grad) for grad in grads[-1]]
        probs = []
        slopes = []
        for k in range(2 * BACK_TOGETHER):
            prob = jnp.exp(scores[k] + mask[...] - lse[2 * (b * PAIRS + pairs[k // 2]) + k % 2])
            mean = jnp.sum(prob * grad_probs[k], axis=0, keepdims=True)
            slopes.append((prob * (grad_probs[k] - mean)).astype(bf16))
            probs.append(prob.astype(bf16))
        for k, h in enumerate(pairs):
            lanes = wide(h)
            both = slice(2 * k, 2 * k + 2)
            key_t = pk[1, at, lanes].T
            grad_value = dot_nn(jnp.concatenate(probs[both], axis=1), jnp.concatenate(grads[k], axis=0)).astype(bf16)
            grad_key = dot_nn(jnp.concatenate(slopes[both], axis=1), jnp.concatenate(queries[k], axis=0)).astype(bf16)
            grad_query = [dot_nn(key_t[s * HEAD : (s + 1) * HEAD], slopes[2 * k + s]) for s in range(2)]
            grad_query = (jnp.concatenate(grad_query, axis=0) * (1.0 / math.sqrt(HEAD))).T.astype(bf16)
            pk[0, at, lanes] = grad_query
            pk[1, at, lanes] = grad_key
            pk[2, at, lanes] = grad_value
            vec[0:1, lanes] += colsum(grad_query.astype(f32))
            vec[1:2, lanes] += colsum(grad_value.astype(f32))

        ticks_at("t", blocks * per, i)

    loop(0, blocks * (PAIRS // BACK_TOGETHER), attend_back)

    for d in range(n):
        def chunk(row, first, d=d):
            at = first * part
            return vec[row + at // D : row + at // D + 1, at % D : at % D + part]

        at = spot(d)
        for e in range(2):
            vec_out[at, e : e + 1, 0:part] = chunk(0, 2 * d + e)
        for e in range(3):
            vec_out[at, 2 + e : 3 + e, 0:part] = chunk(2 + e, d)
            vec_out[at, 5 + ffc + e : 6 + ffc + e, 0:part] = chunk(5 + ffc + e, d)
        for e in range(ffc):
            vec_out[at, 5 + e : 6 + e, 0:part] = chunk(5, ffc * d + e)

    tick("v")

    for j in range(3):
        for t in range(2):
            spread(gp, 1 + j, dot_tn(tok[:, t * half : (t + 1) * half], pk[j]), (n // 2) * t)
        tick("a%d" % j)

    loads["wa_again"].wait()

    def dx_copy(b):
        return pltpu.make_async_copy(tok.at[block_rows(b), :], r.dx_hbm.at[block_rows(b), :], r.dx_sem.at[b])

    def token_grad(b):
        at = block_rows(b)
        total = fb[at, :]
        for j in range(3):
            total = total + dot_nt(pk[j, at, :], we[:, j * D : (j + 1) * D])
        tok[at, :] = total.astype(bf16)
        dx_copy(b).start()

        ticks_at("x", blocks, b)

    loop(0, blocks, token_grad)
    def settle(u):
        core_copy(u).wait_send()
        for copy in across_copies(u):
            copy.wait_send()
        if MODES[u] == "d":
            for copy in line_copies(u):
                copy.wait_send()
        elif MODES[u] == "a":

            @pl.when(outer)
            def _(u=u):
                end_copy(u).wait_send()

            @pl.when(jnp.logical_not(outer))
            def _(u=u):
                inner_copy(u).wait_send()
                for copy in middle_copies(u):
                    copy.wait_send()
        else:
            if MODES[u] == "b":
                early_copy(u).wait_send()
            for k in range(1, nz):
                along_copy(u, k).wait_send()
        out_copy(u).wait()

    last = SCHEDULE["end"]
    left = set(range(len(units)))
    for k, (step, u) in enumerate(last):
        if k == len(last) - 2:
            for done in sorted(left - {v for _, v in last[k - 4 :]}):
                settle(done)
                left.remove(done)
            for b in range(blocks):
                dx_copy(b).wait()
        if u == len(units):
            vec_steps[step]()
        else:
            steps[step](u)
    for u in sorted(left):
        settle(u)


def hand_over_kernel(count, *refs):
    given, wanted, held = (refs[k * count : (k + 1) * count] for k in range(3))
    sems = refs[-1]
    arriving = [pltpu.make_async_copy(given[k], held[k], sems.at[0, k]) for k in range(count)]
    leaving = [pltpu.make_async_copy(held[k], wanted[k], sems.at[1, k]) for k in range(count)]
    for copy in arriving:
        copy.start()
    for k in range(count):
        arriving[k].wait()
        leaving[k].start()
    for copy in leaving:
        copy.wait()


def fused_shards(n, *args):
    tokens, cotangent = args[0][0], args[13][0]
    rows = tokens.shape[0]
    ff = args[7].shape[2]
    ffc = ff // D
    nz = n // 4
    part = D // n
    shard = ff // n
    thirds = D // SEQ
    extra = rows // QLEN
    blocks = rows // SEQ
    wide_units = ffc + 4
    units = sum(PIECES)
    wa, wm, we, wr = (args[k][0] for k in (1, 3, 7, 9))
    small = dict(
        ab=args[2],
        mb=args[4],
        g1=args[5],
        h1=args[6],
        eb=args[8],
        rb=args[10],
        g2=args[11],
        h2=args[12],
        post=args[14].T,
        cnt=args[15][None, :],
    )
    given = dict(tok_hbm=tokens, wa_hbm=wa, wm_hbm=wm, we_hbm=we, wr_hbm=wr, cot_hbm=cotangent)
    given.update({k + "_hbm": v for k, v in small.items()})
    dma = pltpu.SemaphoreType.DMA
    scratch = dict(
        {k: pltpu.VMEM(v.shape, v.dtype) for k, v in small.items()},
        wm=pltpu.VMEM((D, D), bf16),
        we=pltpu.VMEM((D, ff), bf16),
        wr=pltpu.VMEM((ff, D), bf16),
        tok=pltpu.VMEM((rows, D), bf16),
        pk=pltpu.VMEM((3, rows, D), bf16),
        att_t=pltpu.VMEM((D, rows), bf16),
        low1=pltpu.VMEM((rows, D), bf16),
        n1=pltpu.VMEM((rows, D), bf16),
        fb=pltpu.VMEM((rows, D), f32),
        hid=pltpu.VMEM((ffc, D, rows), bf16),
        gp=pltpu.VMEM((ffc, rows, D), bf16),
        cot=pltpu.VMEM((rows, D), bf16),
        lse=pltpu.VMEM((blocks * HEADS, 1, SEQ), f32),
        s1=pltpu.VMEM((rows, 1), f32),
        s2=pltpu.VMEM((rows, 1), f32),
        mask=pltpu.VMEM((SEQ, SEQ), f32),
        red=pltpu.VMEM((thirds, ff, SEQ), bf16),
        stage_r=pltpu.VMEM((thirds * shard, SEQ), f32),
        stage32=pltpu.VMEM((wide_units * part, D), f32),
        cls=pltpu.VMEM((8 * nz * extra, D), bf16),
        vec=pltpu.VMEM((16, D), f32),
        vec_out=pltpu.VMEM((n, 16, 128), f32),
        vec_c=pltpu.VMEM((n // 2, 16, 128), f32),
        vec_x=pltpu.VMEM((nz, 16, 128), f32),
        vec_z=pltpu.VMEM((nz - 1, 16, 128), f32),
        recv_cr=pltpu.VMEM((thirds, ff // 2, SEQ), bf16),
        recv_xr=pltpu.VMEM((thirds, ff // 4, SEQ), bf16),
        recv_zr=pltpu.VMEM((thirds, nz * shard, SEQ), bf16),
        recv_cw=pltpu.VMEM((wide_units, D // 2, D), bf16),
        recv_xw=pltpu.VMEM((wide_units, D // 4, D), bf16),
        recv_zw=pltpu.VMEM((wide_units, nz * part, D), bf16),
        load_sem=dma((32,)),
        act_sem=dma((blocks, thirds)),
        dx_sem=dma((blocks,)),
        out_sem=dma((units,)),
        c_send=dma((units,)),
        c_recv=dma((units,)),
        x_send=dma((units, nz)),
        x_recv=dma((units, nz)),
        z_send=dma((units, nz)),
        z_recv=dma((units, nz)),
        ag_send=dma((nz + 3,)),
        ag_recv=dma((nz + 3,)),
        v_send=dma((nz + 1,)),
        v_recv=dma((nz + 1,)),
    )
    hbm = pl.BlockSpec(memory_space=pl.ANY)
    near = pl.BlockSpec(memory_space=pltpu.VMEM)
    shape = jax.ShapeDtypeStruct
    row_out = shape((1, part), f32)
    wanted = dict(
        act_hbm=shape((rows, D), bf16),
        loss=shape((1, 1), f32),
        dx_hbm=shape((rows, D), bf16),
        dwa_hbm=shape((part, 3 * D), f32),
        dwm_hbm=shape((part, D), f32),
        dwe_hbm=shape((part, ff), f32),
        dwr_hbm=shape((ff // n, D), f32),
        dab=shape((1, 2 * part), f32),
        dmb=row_out,
        dg1=row_out,
        dh1=row_out,
        deb=shape((1, ff // n), f32),
        drb=row_out,
        dg2=row_out,
        dh2=row_out,
    )
    shapes = list(wanted.values())
    names = list(given) + list(wanted) + list(scratch)
    outs = pl.pallas_call(
        partial(layer_kernel, n, rows, ff, names, len(small)),
        out_shape=shapes,
        in_specs=[hbm] * len(given),
        out_specs=[hbm, near] + [hbm] * 5 + [near] * 8,
        scratch_shapes=list(scratch.values()),
        compiler_params=pltpu.CompilerParams(
            collective_id=0, has_side_effects=True, vmem_limit_bytes=VMEM_BYTES
        ),
    )(*given.values())
    act, loss, dx, dwa, dwm, dwe, dwr, dab, dmb, dg1, dh1, deb, drb, dg2, dh2 = pl.pallas_call(
        partial(hand_over_kernel, len(shapes)),
        out_shape=shapes,
        in_specs=[hbm] * len(shapes),
        out_specs=[hbm] * len(shapes),
        scratch_shapes=[pltpu.VMEM(out.shape, out.dtype) for out in shapes] + [dma((2, len(shapes)))],
    )(*outs)
    return (
        act[None],
        loss[0, 0],
        dx[None],
        dwa[None],
        dab,
        dwm[None],
        dmb,
        dg1,
        dh1,
        dwe[None],
        deb,
        dwr[None],
        drb,
        dg2,
        dh2,
    )


def layer_norm(values, scale_gain, shift_row):
    centred = values - jnp.mean(values, axis=-1, keepdims=True)
    inverse = lax.rsqrt(jnp.mean(centred * centred, axis=-1, keepdims=True) + eps)
    normed = centred * inverse
    return (normed * scale_gain + shift_row, normed, inverse)


def norm_backward(upstream, normed, inverse, scale_gain):
    scaled = upstream * scale_gain
    centred = (
        scaled
        - jnp.mean(scaled, axis=-1, keepdims=True)
        - normed * jnp.mean(scaled * normed, axis=-1, keepdims=True)
    )
    return (centred * inverse, jnp.sum(upstream * normed, axis=0), jnp.sum(upstream, axis=0))


def masked_scores(query_block, key_block, same_sequence):
    raw_scores = jnp.einsum(
        "qhd,khd->hqk", query_block, key_block, preferred_element_type=jnp.float32
    ) * (1.0 / math.sqrt(HEAD))
    return jnp.where(same_sequence[None], raw_scores, negative)


def shards(
    tokens,
    attend_weight,
    attend_bias,
    merge_weight,
    merge_bias,
    first_gain,
    first_shift,
    expand_weight,
    expand_bias,
    reduce_weight,
    reduce_bias,
    second_gain,
    second_shift,
    cotangent,
    positives,
    counts,
):
    half_index = lax.axis_index("pair")
    group_index = lax.axis_index("dp")
    span_length = jnp.where(half_index == 0, QLEN, PLEN).astype(jnp.int32)
    token_rows = tokens[0]
    row_count, model_width = token_rows.shape
    block_count = row_count // BLOCK
    places = jnp.arange(BLOCK, dtype=jnp.int32) // span_length
    same_sequence = places[:, None] == places[None, :]
    zero_keys = jnp.zeros((model_width,), jnp.float32)
    full_bias = jnp.concatenate(
        [attend_bias[0, :model_width], zero_keys, attend_bias[0, model_width:]]
    )
    packed = (
        jnp.dot(token_rows, attend_weight[0], preferred_element_type=jnp.float32) + full_bias
    ).astype(jnp.bfloat16)
    heads_split = packed.reshape(block_count, BLOCK, 3, HEADS, HEAD)
    queries = heads_split[:, :, 0]
    keys_all = heads_split[:, :, 1]
    values_all = heads_split[:, :, 2]

    def attend_block(members):
        query_block, key_block, value_block = members
        scores = masked_scores(query_block, key_block, same_sequence)
        peak = jnp.max(scores, axis=-1, keepdims=True)
        totals = jnp.sum(jnp.exp(scores - peak), axis=-1, keepdims=True)
        log_total = peak + jnp.log(totals)
        probs16 = jnp.exp(scores - log_total).astype(jnp.bfloat16)
        mixed = jnp.einsum("hqk,khd->qhd", probs16, value_block, preferred_element_type=jnp.float32)
        return (mixed, log_total[..., 0])

    attended, log_totals = lax.map(attend_block, (queries, keys_all, values_all))
    attended16 = attended.reshape(row_count, model_width).astype(jnp.bfloat16)
    branch = (
        jnp.dot(attended16, merge_weight[0], preferred_element_type=jnp.float32) + merge_bias[0]
    )
    rows_float = token_rows.astype(jnp.float32)
    normed_first, first_normed, first_inverse = layer_norm(
        rows_float + branch, first_gain[0], first_shift[0]
    )
    first16 = normed_first.astype(jnp.bfloat16)
    inner_pre = (
        jnp.dot(first16, expand_weight[0], preferred_element_type=jnp.float32) + expand_bias[0]
    )
    hidden16 = jax.nn.gelu(inner_pre, approximate=False).astype(jnp.bfloat16)
    second = (
        jnp.dot(hidden16, reduce_weight[0], preferred_element_type=jnp.float32) + reduce_bias[0]
    )
    final, final_normed, final_inverse = layer_norm(
        normed_first + second, second_gain[0], second_shift[0]
    )
    question_count = row_count // QLEN
    passage_count = row_count // PLEN
    leading = final.reshape(question_count, QLEN, model_width)[:, 0].astype(jnp.bfloat16)
    every_leading = lax.all_gather(leading, ("pair", "dp"), axis=0, tiled=True)
    half_rows = every_leading.shape[0] // 2
    question_cls = every_leading[:half_rows]
    passage_cls = every_leading[half_rows:].reshape(-1, PLEN // QLEN, model_width)[:, 0]
    root_width = math.sqrt(D)
    match_scores = (
        jnp.einsum("qd,pd->qp", question_cls, passage_cls, preferred_element_type=jnp.float32)
        / root_width
    )
    row_peak = jnp.max(match_scores, axis=1, keepdims=True)
    lse_all = row_peak + jnp.log(jnp.sum(jnp.exp(match_scores - row_peak), axis=1, keepdims=True))
    picked = jnp.take_along_axis(match_scores, positives, axis=1)
    live_slots = jnp.arange(KPOS, dtype=jnp.int32)[None, :] < counts[:, None]
    live_peak = jnp.max(jnp.where(live_slots, picked, negative), axis=1, keepdims=True)
    live_total = jnp.sum(
        jnp.where(live_slots, jnp.exp(picked - live_peak), 0.0), axis=1, keepdims=True
    )
    lse_live = live_peak + jnp.log(live_total)
    loss_value = jnp.mean(lse_all[:, 0] - lse_live[:, 0])
    live_weights = jnp.where(live_slots, jnp.exp(picked - lse_live), 0.0)
    columns = jnp.arange(match_scores.shape[1], dtype=jnp.int32)[None, :]
    grad_match = jnp.exp(match_scores - lse_all)
    for slot in range(KPOS):
        grad_match = grad_match - jnp.where(
            columns == positives[:, slot : slot + 1], live_weights[:, slot : slot + 1], 0.0
        )
    grad_match16 = (loss_weight * grad_match).astype(jnp.bfloat16)
    own_questions = lax.dynamic_slice_in_dim(
        grad_match16, group_index * question_count, question_count, 0
    )
    grad_question = (
        jnp.dot(own_questions, passage_cls, preferred_element_type=jnp.float32) / root_width
    )
    own_passages = lax.dynamic_slice_in_dim(
        grad_match16, group_index * passage_count, passage_count, 1
    )
    grad_passage = (
        jnp.einsum("qp,qd->pd", own_passages, question_cls, preferred_element_type=jnp.float32)
        / root_width
    )
    spread_question = (
        jnp.zeros((question_count, QLEN, model_width), jnp.float32)
        .at[:, 0]
        .set(grad_question)
        .reshape(row_count, model_width)
    )
    spread_passage = (
        jnp.zeros((passage_count, PLEN, model_width), jnp.float32)
        .at[:, 0]
        .set(grad_passage)
        .reshape(row_count, model_width)
    )
    grad_final = cotangent[0].astype(jnp.float32) + jnp.where(
        half_index == 0, spread_question, spread_passage
    )
    grad_pair_two, second_gain_grad, second_shift_grad = norm_backward(
        grad_final, final_normed, final_inverse, second_gain[0]
    )
    grad_second16 = grad_pair_two.astype(jnp.bfloat16)
    reduce_weight_grad = jnp.einsum(
        "tf,td->fd", hidden16, grad_second16, preferred_element_type=jnp.float32
    )
    reduce_bias_grad = jnp.sum(grad_second16.astype(jnp.float32), axis=0)
    grad_hidden = jnp.einsum(
        "td,fd->tf", grad_second16, reduce_weight[0], preferred_element_type=jnp.float32
    )
    _, gelu_pullback = jax.vjp(partial(jax.nn.gelu, approximate=False), inner_pre)
    grad_inner16 = gelu_pullback(grad_hidden)[0].astype(jnp.bfloat16)
    expand_weight_grad = jnp.einsum(
        "td,tf->df", first16, grad_inner16, preferred_element_type=jnp.float32
    )
    expand_bias_grad = jnp.sum(grad_inner16.astype(jnp.float32), axis=0)
    grad_first = (
        jnp.einsum("tf,df->td", grad_inner16, expand_weight[0], preferred_element_type=jnp.float32)
        + grad_pair_two
    )
    feed_shares = (
        expand_weight_grad,
        expand_bias_grad,
        reduce_weight_grad,
        reduce_bias_grad,
        second_gain_grad,
        second_shift_grad,
    )
    grad_pair_one, first_gain_grad, first_shift_grad = norm_backward(
        grad_first, first_normed, first_inverse, first_gain[0]
    )
    grad_branch16 = grad_pair_one.astype(jnp.bfloat16)
    merge_weight_grad = jnp.einsum(
        "td,te->de", attended16, grad_branch16, preferred_element_type=jnp.float32
    )
    merge_bias_grad = jnp.sum(grad_branch16.astype(jnp.float32), axis=0)
    grad_attended16 = jnp.einsum(
        "te,de->td", grad_branch16, merge_weight[0], preferred_element_type=jnp.float32
    ).astype(jnp.bfloat16)
    grad_attended_blocks = grad_attended16.reshape(block_count, BLOCK, HEADS, HEAD)

    def attend_backward(members):
        query_block, key_block, value_block, grad_out, log_total = members
        scores = masked_scores(query_block, key_block, same_sequence)
        probs = jnp.exp(scores - log_total[..., None])
        probs16 = probs.astype(jnp.bfloat16)
        grad_value = jnp.einsum(
            "hqk,qhd->khd", probs16, grad_out, preferred_element_type=jnp.float32
        )
        grad_probs = jnp.einsum(
            "qhd,khd->hqk", grad_out, value_block, preferred_element_type=jnp.float32
        )
        grad_scores16 = (
            probs * (grad_probs - jnp.sum(probs * grad_probs, axis=-1, keepdims=True))
        ).astype(jnp.bfloat16)
        grad_query = jnp.einsum(
            "hqk,khd->qhd", grad_scores16, key_block, preferred_element_type=jnp.float32
        ) * (1.0 / math.sqrt(HEAD))
        grad_key = jnp.einsum(
            "hqk,qhd->khd", grad_scores16, query_block, preferred_element_type=jnp.float32
        ) * (1.0 / math.sqrt(HEAD))
        return (grad_query, grad_key, grad_value)

    grad_queries, grad_keys, grad_values = lax.map(
        attend_backward, (queries, keys_all, values_all, grad_attended_blocks, log_totals)
    )
    grad_packed16 = (
        jnp.stack([grad_queries, grad_keys, grad_values], axis=2)
        .reshape(row_count, 3 * model_width)
        .astype(jnp.bfloat16)
    )
    attend_weight_grad = jnp.einsum(
        "td,te->de", token_rows, grad_packed16, preferred_element_type=jnp.float32
    )
    packed_sums = jnp.sum(grad_packed16.astype(jnp.float32), axis=0)
    attend_bias_grad = jnp.concatenate([packed_sums[:model_width], packed_sums[2 * model_width :]])
    grad_rows = (
        jnp.einsum("te,de->td", grad_packed16, attend_weight[0], preferred_element_type=jnp.float32)
        + grad_pair_one
    )
    every_share = (
        lax.psum_scatter(attend_weight_grad, "dp", scatter_dimension=0, tiled=True),
        lax.psum_scatter(attend_bias_grad, "dp", scatter_dimension=0, tiled=True),
        lax.psum_scatter(merge_weight_grad, "dp", scatter_dimension=0, tiled=True),
        lax.psum_scatter(merge_bias_grad, "dp", scatter_dimension=0, tiled=True),
        lax.psum_scatter(first_gain_grad, "dp", scatter_dimension=0, tiled=True),
        lax.psum_scatter(first_shift_grad, "dp", scatter_dimension=0, tiled=True),
        lax.psum_scatter(expand_weight_grad, "dp", scatter_dimension=0, tiled=True),
        lax.psum_scatter(expand_bias_grad, "dp", scatter_dimension=0, tiled=True),
        lax.psum_scatter(reduce_weight_grad, "dp", scatter_dimension=0, tiled=True),
        lax.psum_scatter(reduce_bias_grad, "dp", scatter_dimension=0, tiled=True),
        lax.psum_scatter(second_gain_grad, "dp", scatter_dimension=0, tiled=True),
        lax.psum_scatter(second_shift_grad, "dp", scatter_dimension=0, tiled=True),
    )
    attend_shares = every_share[:6]
    feed_shares = every_share[6:]
    return (
        final.astype(jnp.bfloat16)[None],
        loss_value,
        grad_rows.astype(jnp.bfloat16)[None],
        attend_shares[0][None],
        attend_shares[1][None],
        attend_shares[2][None],
        attend_shares[3][None],
        attend_shares[4][None],
        attend_shares[5][None],
        feed_shares[0][None],
        feed_shares[1][None],
        feed_shares[2][None],
        feed_shares[3][None],
        feed_shares[4][None],
        feed_shares[5][None],
    )


def solution(mesh):
    in_specs = (
        P("pair", "dp", None),
        P("pair", None, None),
        P("pair", None),
        P("pair", None, None),
        P("pair", None),
        P("pair", None),
        P("pair", None),
        P("pair", None, None),
        P("pair", None),
        P("pair", None, None),
        P("pair", None),
        P("pair", None),
        P("pair", None),
        P("pair", "dp", None),
        P(),
        P(),
    )
    out_specs = (
        P("pair", "dp", None),
        P(),
        P("pair", "dp", None),
        P("pair", "dp", None),
        P("pair", "dp"),
        P("pair", "dp", None),
        P("pair", "dp"),
        P("pair", "dp"),
        P("pair", "dp"),
        P("pair", "dp", None),
        P("pair", "dp"),
        P("pair", "dp", None),
        P("pair", "dp"),
        P("pair", "dp"),
        P("pair", "dp"),
    )
    n = mesh.shape["dp"]
    fits = mesh.shape["pair"] == 2 and n == 4 * LINE
    body = partial(fused_shards, n) if fits else shards
    return jax.shard_map(body, mesh=mesh, in_specs=in_specs, out_specs=out_specs, check_vma=False)
```
